32 devices in a mesh: dp: 8 (over z, core), seq: 4 (over y, x).
Axes of the slice: x: 2, y: 2, z: 4, core: 2. Of those that a mesh axis runs over, the one named last changes fastest.
Arguments:
- tokens: bfloat16 [8, 2048, 2048], P('dp', 'seq'), may hold values from -6 to 6
- joined_weight: bfloat16 [2048, 1920], P(('dp', 'seq')), may hold values from -0.125 to 0.125
- output_weight: bfloat16 [1280, 2048], P(None, ('dp', 'seq')), may hold values from -2.5 to 2.5
- expand_weight: bfloat16 [2048, 12288], P(('dp', 'seq')), may hold values from -0.125 to 0.125
- shrink_weight: bfloat16 [6144, 2048], P(None, ('dp', 'seq')), may hold values from -0.078125 to 0.078125
- norm_gains: bfloat16 [4224], P(('dp', 'seq')), may hold values from 0.25 to 1.75
- doc_lengths: int32 [8, 4], P('dp'), may hold values from 1 to 2045, as said below
- cotangent: bfloat16 [8, 2048, 2048], P('dp', 'seq'), may hold values from -6 to 6
Outputs:
- layer_output: bfloat16 [8, 2048, 2048], P('dp', 'seq')
- token_gradient: bfloat16 [8, 2048, 2048], P('dp', 'seq')
- joined_gradient: float32 [2048, 1920], P(('dp', 'seq'))
- output_gradient: float32 [1280, 2048], P(None, ('dp', 'seq'))
- expand_gradient: float32 [2048, 12288], P(('dp', 'seq'))
- shrink_gradient: float32 [6144, 2048], P(None, ('dp', 'seq'))
- gains_gradient: float32 [4224], P(('dp', 'seq'))
The draws below stay inside these ranges and needn't reach their ends.
Inputs may be any that keep to these rules, and one draw needn't show every extreme that they name: `doc_lengths`: each row's lengths sum to 2048. Each row holds one document that starts within the first device's share of the row along seq and ends within the last one's; in some row that document has 2045 tokens.
All inputs are finite; a program needn't handle non-finite values.
Results may differ from the reference program's by a relative error of at most 0.015.
Values may be sent and summed in bfloat16 or wider, within the bound.
A program may use at most 384 MiB of HBM per device.

```python
import jax
import jax.numpy as jnp
from jax import lax

D = 2048
HEADS = 20
KV_HEADS = 5
HEAD_DIM = 64
FF = 6144
ROW_LEN = 2048
DOCS = 4
ROWS_DEV = 1
ROWS = 8
QKV = 1920
GAINS = 4224
N_SEQ = 4


def draw_doc_lengths(key, part):
    key = jax.random.fold_in(key, 11)
    key_slack = jax.random.fold_in(key, 1)
    key_cut = jax.random.fold_in(key, 2)
    key_place = jax.random.fold_in(key, 3)
    share = ROW_LEN // N_SEQ
    slack = jax.random.randint(key_slack, (ROWS,), 0, share - DOCS + 1).astype(jnp.int32)
    slack = jnp.where(jnp.arange(ROWS, dtype=jnp.int32) == 0, 0, slack)
    cuts = jax.random.randint(key_cut, (ROWS, DOCS - 2), 0, slack[:, None] + 1).astype(jnp.int32)
    cuts = jnp.sort(cuts, axis=1)
    bounds = jnp.concatenate([jnp.zeros((ROWS, 1), jnp.int32), cuts, slack[:, None]], axis=1)
    others = bounds[:, 1:] - bounds[:, :-1] + 1
    long_len = ROW_LEN - (DOCS - 1) - slack
    place = jax.random.randint(key_place, (ROWS,), 0, DOCS).astype(jnp.int32)
    slots = jnp.arange(DOCS, dtype=jnp.int32)[None, :]
    source = jnp.clip(slots - (slots > place[:, None]).astype(jnp.int32), 0, DOCS - 2)
    taken = jnp.take_along_axis(others, source, axis=1)
    return jnp.where(slots == place[:, None], long_len[:, None], taken).astype(jnp.int32)


def spiked(array, rng, source, target, shards_of, factor):
    def block_of(position):
        return (jnp.arange(array.shape[position]) // (array.shape[position] // shards_of)).reshape((-1,) + (1,) * (array.ndim - 1 - position))

    one_side = jax.random.permutation(rng, shards_of)[block_of(target)]
    second = (block_of(target) + shards_of // 2) % shards_of
    return jnp.where((block_of(source) == one_side) | (block_of(source) == second), factor * array, array)


def block_scale(stream_key, dims, split, least, top_value):
    factor_of = 1.0
    for position, shards_of in split:
        heights = jax.random.uniform(jax.random.fold_in(jax.random.fold_in(stream_key, 6), position), (shards_of,), jnp.float32, least / len(split), top_value / len(split))
        factor_of = factor_of * jnp.repeat(jnp.exp(heights), dims[position] // shards_of).reshape((-1,) + (1,) * (len(dims) - 1 - position))
    return factor_of


def scatter_about(rng, shape, deviation, bound, pieces=(), kind=jnp.bfloat16):
    loudness = block_scale(rng, shape, pieces, -0.22, 0.18) if pieces else 1.0
    entries = jax.random.normal(rng, shape, jnp.float32) * deviation * loudness
    return jnp.minimum(jnp.maximum(entries, -bound), bound).astype(kind)


def gaussian_with(stream_key, shape, width, most, pieces, heavy, kind=jnp.bfloat16):
    drawn = width * jax.random.normal(stream_key, shape, jnp.float32)
    if pieces:
        drawn = drawn * block_scale(stream_key, shape, pieces, -0.22, 0.18)
    return jnp.clip(spiked(drawn, jax.random.fold_in(stream_key, 3), *heavy), -most, most).astype(kind)


def setup_inputs(seed: int = 0) -> dict:
    streams_of = jax.random.split(jax.random.key(seed), 9)
    tokens = gaussian_with(streams_of[0], (ROWS, ROW_LEN, D), 1.0, 6.0, ((0, 8), (1, 4)), (0, 2, 8, 2.0))
    joined_weight = scatter_about(streams_of[1], (D, QKV), D ** -0.5, 0.125, ((0, 32),))
    output_weight = scatter_about(streams_of[2], (HEADS * HEAD_DIM, D), (max(1, HEADS * HEAD_DIM * 8 // ROW_LEN)) ** -0.5, 2.5, ((1, 32),))
    expand_weight = scatter_about(streams_of[3], (D, 2 * FF), D ** -0.5, 0.125, ((0, 32),))
    shrink_weight = scatter_about(streams_of[4], (FF, D), FF ** -0.5, 0.078125, ((1, 32),))
    norm_gains = jnp.clip(1.0 + 0.15 * jax.random.normal(streams_of[5], (GAINS,), jnp.float32), 0.25, 1.75).astype(jnp.bfloat16)
    doc_lengths = draw_doc_lengths(jax.random.fold_in(streams_of[8], 71), 0)
    cotangent = gaussian_with(streams_of[7], (ROWS, ROW_LEN, D), 1.0, 6.0, ((0, 8), (1, 4)), (0, 2, 8, 2.0))
    return dict(tokens=tokens, joined_weight=joined_weight, output_weight=output_weight, expand_weight=expand_weight, shrink_weight=shrink_weight, norm_gains=norm_gains, doc_lengths=doc_lengths, cotangent=cotangent)


@jax.custom_vjp
def low(v):
    return lax.optimization_barrier(v.astype(jnp.bfloat16)).astype(jnp.float32)

@jax.custom_vjp
def low_back(v):
    return v

def low_keep(v):
    return (low(v), None)

def low_pass(kept, grad):
    return (grad,)

def back_keep(v):
    return (v, None)

def back_low(kept, grad):
    return (low(grad),)
low.defvjp(low_keep, low_pass)
low_back.defvjp(back_keep, back_low)
epsilon = 1e-05
masked_fill = -1e+30

def rms_scale(values):
    return lax.rsqrt(lax.optimization_barrier(jnp.mean(values * values, axis=-1, keepdims=True)) + epsilon)

def rope_tables(positions):
    half_dim = HEAD_DIM // 2
    frequency = 10000.0 ** (-jnp.arange(half_dim, dtype=jnp.float32) / half_dim)
    angles = positions.astype(jnp.float32)[:, None] * frequency[None, :]
    return (jnp.cos(angles), jnp.sin(angles))

def rotate(values, cosine, sine_table):
    half_dim = values.shape[-1] // 2
    first_half = values[..., :half_dim]
    second_half = values[..., half_dim:]
    return jnp.concatenate([first_half * cosine - second_half * sine_table, second_half * cosine + first_half * sine_table], axis=-1)

def document_ids(doc_lengths):
    bounds = jnp.cumsum(doc_lengths, axis=-1).astype(jnp.int32)[:, :-1]
    places = jnp.arange(ROW_LEN, dtype=jnp.int32)
    return lax.optimization_barrier(jnp.sum((places[None, :, None] >= bounds[:, None, :]).astype(jnp.int32), axis=-1))

def product(left, right):
    return jnp.dot(left, right, precision=lax.Precision.HIGHEST, preferred_element_type=jnp.float32)

def attend_row(inputs):
    grouped, key_rot, value_low, doc_row = inputs
    scores = jnp.einsum('qhgd,khd->hgqk', grouped, key_rot, precision=lax.Precision.HIGHEST) * HEAD_DIM ** (-0.5)
    scores = low_back(scores)
    places = jnp.arange(ROW_LEN, dtype=jnp.int32)
    allowed_mask = (doc_row[:, None] == doc_row[None, :]) & (places[None, :] <= places[:, None])
    scores = jnp.where(allowed_mask[None, None], scores, masked_fill)
    probability = low(jax.nn.softmax(scores, axis=-1))
    return jnp.einsum('hgqk,khd->qhgd', probability, value_low, precision=lax.Precision.HIGHEST)

def layer_forward(tokens_in, joined, output_proj, expand, shrink, gain_all, doc_index):
    row_count = tokens_in.shape[0]
    token_count = row_count * ROW_LEN
    query_width = HEADS * HEAD_DIM
    kv_width = KV_HEADS * HEAD_DIM
    gain_one = gain_all[:D]
    gain_query = gain_all[D:D + HEAD_DIM]
    gain_key = gain_all[D + HEAD_DIM:D + 2 * HEAD_DIM]
    gain_two = gain_all[D + 2 * HEAD_DIM:]
    flat = tokens_in.reshape(token_count, D)
    normed = low(flat * rms_scale(flat) * gain_one)
    projected = low_back(product(normed, joined))
    queries = projected[:, :query_width].reshape(row_count, ROW_LEN, HEADS, HEAD_DIM)
    key_rows = projected[:, query_width:query_width + kv_width].reshape(row_count, ROW_LEN, KV_HEADS, HEAD_DIM)
    value_rows = projected[:, query_width + kv_width:].reshape(row_count, ROW_LEN, KV_HEADS, HEAD_DIM)
    cosine, sine_table = rope_tables(jnp.arange(ROW_LEN, dtype=jnp.int32))
    cosine = cosine[None, :, None, :]
    sine_table = sine_table[None, :, None, :]
    query_rot = low(rotate(queries * rms_scale(queries) * gain_query, cosine, sine_table))
    key_rot = low(rotate(key_rows * rms_scale(key_rows) * gain_key, cosine, sine_table))
    value_low = low(value_rows)
    grouped = query_rot.reshape(row_count, ROW_LEN, KV_HEADS, HEADS // KV_HEADS, HEAD_DIM)
    attended = lax.map(jax.checkpoint(attend_row), (grouped, key_rot, value_low, doc_index))
    mixed_out = low_back(low(attended.reshape(token_count, query_width)))
    residual = flat + low_back(product(mixed_out, output_proj))
    normed_two = low(residual * rms_scale(residual) * gain_two)
    both_pre = low_back(product(normed_two, expand))
    hidden = low(jax.nn.silu(both_pre[:, :FF]) * both_pre[:, FF:])
    return (residual + product(hidden, shrink)).reshape(row_count, ROW_LEN, D)

def reference(tokens, joined_weight, output_weight, expand_weight, shrink_weight, norm_gains, doc_lengths, cotangent):
    params = (joined_weight.astype(jnp.float32), output_weight.astype(jnp.float32), expand_weight.astype(jnp.float32), shrink_weight.astype(jnp.float32), norm_gains.astype(jnp.float32))
    group_count = ROWS // ROWS_DEV
    tokens_grouped = tokens.astype(jnp.float32).reshape(group_count, ROWS_DEV, ROW_LEN, D)
    upstream_grouped = cotangent.astype(jnp.float32).reshape(group_count, ROWS_DEV, ROW_LEN, D)
    lengths_grouped = doc_lengths.reshape(group_count, ROWS_DEV, DOCS)

    def one_group(totals, inputs):
        tokens_rows, upstream_rows, length_rows = inputs
        doc_index = document_ids(length_rows)

        def forward(tokens_in, joined, output_proj, expand, shrink, gain_all):
            return layer_forward(tokens_in, joined, output_proj, expand, shrink, gain_all, doc_index)
        result, pullback = jax.vjp(forward, tokens_rows, params[0], params[1], params[2], params[3], params[4])
        gradients = pullback(upstream_rows)
        updated = tuple((total_entry + grad_entry for total_entry, grad_entry in zip(totals, gradients[1:])))
        return (updated, (result.astype(jnp.bfloat16), gradients[0].astype(jnp.bfloat16)))
    initial = tuple((jnp.zeros_like(weight_array) for weight_array in params))
    totals, outputs = lax.scan(one_group, initial, (tokens_grouped, upstream_grouped, lengths_grouped))
    layer_output = outputs[0].reshape(ROWS, ROW_LEN, D)
    token_gradient = outputs[1].reshape(ROWS, ROW_LEN, D)
    return (layer_output, token_gradient, totals[0], totals[1], totals[2], totals[3], totals[4])
```

```python
import jax
import jax.numpy as jnp
from jax import lax
from jax.sharding import PartitionSpec as P

D = 2048
HEADS = 20
KV_HEADS = 5
HEAD_DIM = 64
FF = 6144
ROW_LEN = 2048


epsilon = 1e-05
masked_fill = -1e30


def rms_scale(values):
    return lax.rsqrt(jnp.mean(values * values, axis=-1, keepdims=True) + epsilon)


def norm_back(upstream, values, scaling, gain_vector):
    weighted = upstream * gain_vector
    average = jnp.mean(weighted * values, axis=-1, keepdims=True)
    return scaling * weighted - values * (scaling * scaling * scaling) * average


def rope_tables(positions):
    half_dim = HEAD_DIM // 2
    frequency = 10000.0 ** (-jnp.arange(half_dim, dtype=jnp.float32) / half_dim)
    angles = positions.astype(jnp.float32)[:, None] * frequency[None, :]
    return (jnp.cos(angles), jnp.sin(angles))


def rotate(values, cosine, sine_table):
    half_dim = values.shape[-1] // 2
    first_half = values[..., :half_dim]
    second_half = values[..., half_dim:]
    return jnp.concatenate(
        [
            first_half * cosine - second_half * sine_table,
            second_half * cosine + first_half * sine_table,
        ],
        axis=-1,
    )


def rotate_back(gradient, cosine, sine_table):
    half_dim = gradient.shape[-1] // 2
    first_half = gradient[..., :half_dim]
    second_half = gradient[..., half_dim:]
    return jnp.concatenate(
        [
            first_half * cosine + second_half * sine_table,
            second_half * cosine - first_half * sine_table,
        ],
        axis=-1,
    )


def document_ids(doc_lengths):
    ends = [doc_lengths[:, :1]]
    for index in range(1, doc_lengths.shape[1] - 1):
        ends.append(ends[-1] + doc_lengths[:, index : index + 1])
    bounds = jnp.concatenate(ends, axis=1)
    places = jnp.arange(ROW_LEN, dtype=jnp.int32)
    return jnp.sum((places[None, :, None] >= bounds[:, None, :]).astype(jnp.int32), axis=-1)


def contract(left, right, left_dim, right_dim):
    return lax.dot_general(
        left, right, (((left_dim,), (right_dim,)), ((), ())), preferred_element_type=jnp.float32
    )


def body(
    tokens,
    joined_weight,
    output_weight,
    expand_weight,
    shrink_weight,
    norm_gains,
    doc_lengths,
    cotangent,
):
    row_count, local_len, width = tokens.shape
    token_count = row_count * local_len
    group_size = HEADS // KV_HEADS
    query_width = HEADS * HEAD_DIM
    kv_width = KV_HEADS * HEAD_DIM
    score_scale = HEAD_DIM ** (-0.5)
    offset = lax.axis_index("seq") * local_len
    query_pos = offset + jnp.arange(local_len, dtype=jnp.int32)
    cosine, sine_table = rope_tables(query_pos)
    cosine = cosine[None, :, None, :]
    sine_table = sine_table[None, :, None, :]
    doc_index = document_ids(doc_lengths)
    query_docs = lax.dynamic_slice_in_dim(doc_index, offset, local_len, 1)

    def allowed(piece_len):
        key_pos = jnp.arange(piece_len, dtype=jnp.int32)
        same_doc = query_docs[:, :, None] == doc_index[:, None, :]
        causal = key_pos[None, :] <= query_pos[:, None]
        return (same_doc & causal[None])[:, None, None]

    joined_all, output_all, gains_all = (
        lax.all_gather(joined_weight, ("dp", "seq"), axis=0, tiled=True),
        lax.all_gather(output_weight, ("dp", "seq"), axis=1, tiled=True),
        lax.all_gather(norm_gains, ("dp", "seq"), axis=0, tiled=True),
    )
    gains_float = gains_all.astype(jnp.float32)
    gain_one = gains_float[:D]
    gain_query = gains_float[D : D + HEAD_DIM]
    gain_key = gains_float[D + HEAD_DIM : D + 2 * HEAD_DIM]
    gain_two = gains_float[D + 2 * HEAD_DIM :]
    flat = tokens.reshape(token_count, width).astype(jnp.float32)
    scale_one = rms_scale(flat)
    normed_low = (flat * scale_one * gain_one).astype(jnp.bfloat16)
    projected = jnp.dot(normed_low, joined_all, preferred_element_type=jnp.float32)
    queries = projected[:, :query_width].reshape(row_count, local_len, HEADS, HEAD_DIM)
    key_rows = projected[:, query_width : query_width + kv_width].reshape(
        row_count, local_len, KV_HEADS, HEAD_DIM
    )
    value_rows = projected[:, query_width + kv_width :].reshape(row_count, local_len, kv_width)
    scale_query = rms_scale(queries)
    scale_key = rms_scale(key_rows)
    query_low = rotate(queries * scale_query * gain_query, cosine, sine_table).astype(jnp.bfloat16)
    query_low = query_low.reshape(row_count, local_len, KV_HEADS, group_size, HEAD_DIM)
    key_low = rotate(key_rows * scale_key * gain_key, cosine, sine_table).astype(jnp.bfloat16)
    kv_stack = jnp.concatenate(
        [key_low.reshape(row_count, local_len, kv_width), value_rows.astype(jnp.bfloat16)], axis=-1
    )

    def split_piece(pieces):
        piece_len = pieces.shape[1]
        key_piece = pieces[..., :kv_width].reshape(row_count, piece_len, KV_HEADS, HEAD_DIM)
        value_piece = pieces[..., kv_width:].reshape(row_count, piece_len, KV_HEADS, HEAD_DIM)
        return (key_piece, value_piece, piece_len)

    running_max = jnp.full((row_count, KV_HEADS, group_size, local_len), masked_fill, jnp.float32)
    key_piece, value_piece, piece_len = split_piece(
        lax.all_gather(kv_stack, "seq", axis=1, tiled=True)
    )
    allowed_mask = allowed(piece_len)
    scores = (
        jnp.einsum("rqhgd,rkhd->rhgqk", query_low, key_piece, preferred_element_type=jnp.float32)
        * score_scale
    )
    scores = jnp.where(allowed_mask, scores, masked_fill)
    new_max = jnp.maximum(running_max, jnp.max(scores, axis=-1))
    expo = jnp.where(allowed_mask, jnp.exp(scores - new_max[..., None]), 0.0)
    running_sum = jnp.sum(expo, axis=-1)
    mixed = jnp.einsum(
        "rhgqk,rkhd->rqhgd",
        expo.astype(jnp.bfloat16),
        value_piece,
        preferred_element_type=jnp.float32,
    )
    weighted = mixed
    running_max, running_sum, weighted = (new_max, running_sum, weighted)
    log_total = running_max + jnp.log(running_sum)
    attended = weighted / jnp.transpose(running_sum, (0, 3, 1, 2))[..., None]
    attended_low = attended.astype(jnp.bfloat16).reshape(token_count, query_width)
    residual = flat + jnp.dot(attended_low, output_all, preferred_element_type=jnp.float32)
    scale_two = rms_scale(residual)
    normed_two = (residual * scale_two * gain_two).astype(jnp.bfloat16)
    expand_all, shrink_all = (
        lax.all_gather(expand_weight, ("dp", "seq"), axis=0, tiled=True),
        lax.all_gather(shrink_weight, ("dp", "seq"), axis=1, tiled=True),
    )
    both_pre = jnp.dot(normed_two, expand_all, preferred_element_type=jnp.float32)
    gate_pre = both_pre[:, :FF]
    up_pre = both_pre[:, FF:]
    gate_sigmoid = jax.nn.sigmoid(gate_pre)
    hidden_low = (gate_pre * gate_sigmoid * up_pre).astype(jnp.bfloat16)
    result = residual + jnp.dot(hidden_low, shrink_all, preferred_element_type=jnp.float32)
    layer_output = result.astype(jnp.bfloat16).reshape(row_count, local_len, width)
    expand_back, shrink_back = (
        lax.all_gather(expand_weight, ("dp", "seq"), axis=0, tiled=True),
        lax.all_gather(shrink_weight, ("dp", "seq"), axis=1, tiled=True),
    )
    upstream_low = cotangent.reshape(token_count, width)
    upstream = upstream_low.astype(jnp.float32)
    grad_hidden = contract(upstream_low, shrink_back, 1, 1)
    grad_gate = grad_hidden * up_pre * gate_sigmoid * (1.0 + gate_pre * (1.0 - gate_sigmoid))
    grad_up = grad_hidden * gate_pre * gate_sigmoid
    grad_both = jnp.concatenate([grad_gate, grad_up], axis=1).astype(jnp.bfloat16)
    grad_normed_two = contract(grad_both, expand_back, 1, 1)
    gain_two_grad = jnp.sum(grad_normed_two * residual * scale_two, axis=0)
    grad_residual = upstream + norm_back(grad_normed_two, residual, scale_two, gain_two)
    shrink_term = contract(hidden_low, upstream_low, 0, 0)
    expand_term = contract(normed_two, grad_both, 0, 0)
    expand_gradient, shrink_gradient = (
        lax.psum_scatter(expand_term.astype(jnp.bfloat16), ("dp", "seq"), scatter_dimension=0, tiled=True),
        lax.psum_scatter(shrink_term.astype(jnp.bfloat16), ("dp", "seq"), scatter_dimension=1, tiled=True),
    )
    joined_back, output_back = (
        lax.all_gather(joined_weight, ("dp", "seq"), axis=0, tiled=True),
        lax.all_gather(output_weight, ("dp", "seq"), axis=1, tiled=True),
    )
    grad_attn_low = grad_residual.astype(jnp.bfloat16)
    output_term = contract(attended_low, grad_attn_low, 0, 0)
    grad_out_low = contract(grad_attn_low, output_back, 1, 1).astype(jnp.bfloat16)
    grad_out_low = grad_out_low.reshape(row_count, local_len, KV_HEADS, group_size, HEAD_DIM)
    row_inner = jnp.sum(grad_out_low.astype(jnp.float32) * attended, axis=-1)
    row_inner = jnp.transpose(row_inner, (0, 2, 3, 1))
    key_piece, value_piece, piece_len = split_piece(
        lax.all_gather(kv_stack, "seq", axis=1, tiled=True)
    )
    allowed_mask = allowed(piece_len)
    scores = (
        jnp.einsum("rqhgd,rkhd->rhgqk", query_low, key_piece, preferred_element_type=jnp.float32)
        * score_scale
    )
    scores = jnp.where(allowed_mask, scores, masked_fill)
    probability = jnp.where(allowed_mask, jnp.exp(scores - log_total[..., None]), 0.0)
    grad_prob = jnp.einsum(
        "rqhgd,rkhd->rhgqk", grad_out_low, value_piece, preferred_element_type=jnp.float32
    )
    grad_scores = (probability * (grad_prob - row_inner[..., None])).astype(jnp.bfloat16)
    grad_query = (
        jnp.einsum("rhgqk,rkhd->rqhgd", grad_scores, key_piece, preferred_element_type=jnp.float32)
        * score_scale
    )
    key_term = (
        jnp.einsum("rhgqk,rqhgd->rkhd", grad_scores, query_low, preferred_element_type=jnp.float32)
        * score_scale
    )
    value_term = jnp.einsum(
        "rhgqk,rqhgd->rkhd",
        probability.astype(jnp.bfloat16),
        grad_out_low,
        preferred_element_type=jnp.float32,
    )
    both_terms = jnp.concatenate(
        [
            key_term.reshape(row_count, piece_len, kv_width),
            value_term.reshape(row_count, piece_len, kv_width),
        ],
        axis=-1,
    )
    grad_query, grad_kv_all = (grad_query, both_terms)
    grad_kv = lax.psum_scatter(
        grad_kv_all.astype(jnp.bfloat16), "seq", scatter_dimension=1, tiled=True
    ).astype(jnp.float32)
    grad_key_rot = grad_kv[..., :kv_width].reshape(row_count, local_len, KV_HEADS, HEAD_DIM)
    grad_values = grad_kv[..., kv_width:].reshape(token_count, kv_width)
    grad_query_rot = rotate_back(
        grad_query.reshape(row_count, local_len, HEADS, HEAD_DIM), cosine, sine_table
    )
    grad_key_norm = rotate_back(grad_key_rot, cosine, sine_table)
    gain_query_grad = jnp.sum(grad_query_rot * queries * scale_query, axis=(0, 1, 2))
    gain_key_grad = jnp.sum(grad_key_norm * key_rows * scale_key, axis=(0, 1, 2))
    grad_queries = norm_back(grad_query_rot, queries, scale_query, gain_query)
    grad_keys = norm_back(grad_key_norm, key_rows, scale_key, gain_key)
    grad_projected = jnp.concatenate(
        [
            grad_queries.reshape(token_count, query_width),
            grad_keys.reshape(token_count, kv_width),
            grad_values,
        ],
        axis=1,
    ).astype(jnp.bfloat16)
    joined_term = contract(normed_low, grad_projected, 0, 0)
    grad_normed = contract(grad_projected, joined_back, 1, 1)
    gain_one_grad = jnp.sum(grad_normed * flat * scale_one, axis=0)
    token_gradient = grad_residual + norm_back(grad_normed, flat, scale_one, gain_one)
    gains_term = jnp.concatenate([gain_one_grad, gain_query_grad, gain_key_grad, gain_two_grad])
    joined_gradient, output_gradient, gains_gradient = (
        lax.psum_scatter(joined_term.astype(jnp.bfloat16), ("dp", "seq"), scatter_dimension=0, tiled=True),
        lax.psum_scatter(output_term.astype(jnp.bfloat16), ("dp", "seq"), scatter_dimension=1, tiled=True),
        lax.psum_scatter(gains_term, ("dp", "seq"), scatter_dimension=0, tiled=True),
    )
    return (
        layer_output,
        token_gradient.astype(jnp.bfloat16).reshape(row_count, local_len, width),
        joined_gradient.astype(jnp.float32),
        output_gradient.astype(jnp.float32),
        expand_gradient.astype(jnp.float32),
        shrink_gradient.astype(jnp.float32),
        gains_gradient,
    )


def solution(mesh):
    placed = (
        P("dp", "seq", None),
        P(("dp", "seq"), None),
        P(None, ("dp", "seq")),
        P(("dp", "seq"), None),
        P(None, ("dp", "seq")),
        P(("dp", "seq")),
        P("dp", None),
        P("dp", "seq", None),
    )
    return jax.shard_map(
        body,
        mesh=mesh,
        in_specs=placed,
        out_specs=(
            P("dp", "seq", None),
            P("dp", "seq", None),
            P(("dp", "seq"), None),
            P(None, ("dp", "seq")),
            P(("dp", "seq"), None),
            P(None, ("dp", "seq")),
            P(("dp", "seq")),
        ),
        check_vma=False,
    )
```

```python
import functools

import jax
import jax.numpy as jnp
from jax import lax
from jax.experimental import pallas as pl
from jax.experimental.pallas import tpu as pltpu
from jax.sharding import PartitionSpec as P

D = 2048
HEADS = 20
KV_HEADS = 5
HEAD_DIM = 64
FF = 6144
ROW_LEN = 2048
GAINS = 4224
PAIR = 2 * HEAD_DIM
Q_WIDTH = HEADS * HEAD_DIM
KV_WIDTH = KV_HEADS * HEAD_DIM
QKV = Q_WIDTH + 2 * KV_WIDTH
CORES = 2

epsilon = 1e-05
f32 = jnp.float32
bf16 = jnp.bfloat16
AXES = ("dp", "seq")
NN = (((1,), (0,)), ((), ()))
NT = (((1,), (1,)), ((), ()))
TN = (((0,), (0,)), ((), ()))


def dot(left, right, dims):
    return lax.dot_general(left, right, dims, preferred_element_type=f32)


def rms_scale(values):
    return lax.rsqrt(jnp.mean(values * values, axis=-1, keepdims=True) + epsilon)


def norm_back(upstream, values, scaling, gain_vector):
    weighted = upstream * gain_vector
    average = jnp.mean(weighted * values, axis=-1, keepdims=True)
    return scaling * weighted - values * (scaling * scaling * scaling) * average


def lanes(shape):
    return lax.broadcasted_iota(jnp.int32, shape, len(shape) - 1)


def swap_halves(values):
    half = HEAD_DIM // 2
    first = lanes(values.shape) % HEAD_DIM < half
    return jnp.where(first, pltpu.roll(values, PAIR - half, axis=1), pltpu.roll(values, half, axis=1))


def head_means(values):
    low = lanes(values.shape) < HEAD_DIM
    left = jnp.sum(jnp.where(low, values, 0.0), axis=-1, keepdims=True)
    right = jnp.sum(jnp.where(low, 0.0, values), axis=-1, keepdims=True)
    return jnp.where(low, left, right) * (1.0 / HEAD_DIM)


def rope_kernel(query_pairs, projected, gains, tables, out):
    step = pl.program_id(0)
    is_query = step < query_pairs
    values = projected[...]
    plain = (lanes(values.shape) >= HEAD_DIM) & jnp.logical_not(is_query)
    gain = jnp.where(is_query, gains[0:1], gains[1:2])
    normed = values * lax.rsqrt(head_means(values * values) + epsilon) * gain
    turned = normed * tables[0] + swap_halves(normed) * tables[1]
    turned = turned * jnp.where(is_query, HEAD_DIM**-0.5, 1.0)
    out[...] = jnp.where(plain, values, turned).astype(bf16)


def rope(projected, gains, tables):
    tokens, width = projected.shape
    return pl.pallas_call(
        functools.partial(rope_kernel, Q_WIDTH // PAIR),
        grid=(width // PAIR,),
        in_specs=[
            pl.BlockSpec((tokens, PAIR), lambda i: (0, i)),
            pl.BlockSpec((2, PAIR), lambda i: (0, 0)),
            pl.BlockSpec((2, tokens, PAIR), lambda i: (0, 0, 0)),
        ],
        out_specs=pl.BlockSpec((tokens, PAIR), lambda i: (0, i)),
        out_shape=jax.ShapeDtypeStruct((tokens, width), bf16),
        cost_estimate=pl.CostEstimate(flops=40 * tokens * width, bytes_accessed=6 * tokens * width, transcendentals=0),
        name="rope",
    )(projected, gains, tables)


def rope_back_kernel(query_pairs, dq, dkv, projected, gains, tables, out, gain_sums):
    step = pl.program_id(0)
    is_query = step < query_pairs
    values = projected[...]
    upstream = jnp.where(is_query, dq[...] * HEAD_DIM**-0.5, dkv[...])
    plain = (lanes(values.shape) >= HEAD_DIM) & jnp.logical_not(is_query)
    gain = jnp.where(is_query, gains[0:1], gains[1:2])
    turned = upstream * tables[0] + swap_halves(upstream * tables[1])
    scaling = lax.rsqrt(head_means(values * values) + epsilon)
    weighted = turned * gain
    back = scaling * weighted - values * (scaling * scaling * scaling) * head_means(weighted * values)
    out[...] = jnp.where(plain, upstream, back).astype(bf16)
    sums = jnp.sum(jnp.where(plain, 0.0, turned * values * scaling), axis=0, keepdims=True)

    @pl.when(step == 0)
    def _():
        gain_sums[...] = jnp.zeros_like(gain_sums)

    row = lax.broadcasted_iota(jnp.int32, gain_sums.shape, 0)
    gain_sums[...] += jnp.where(row == jnp.where(is_query, 0, 1), sums, 0.0)


def rope_back(dq, dkv, projected, gains, tables):
    tokens, width = projected.shape
    query_pairs = Q_WIDTH // PAIR
    return pl.pallas_call(
        functools.partial(rope_back_kernel, query_pairs),
        grid=(width // PAIR,),
        in_specs=[
            pl.BlockSpec((tokens, PAIR), lambda i: (0, jnp.minimum(i, query_pairs - 1))),
            pl.BlockSpec((tokens, PAIR), lambda i: (0, jnp.maximum(i - query_pairs, 0))),
            pl.BlockSpec((tokens, PAIR), lambda i: (0, i)),
            pl.BlockSpec((2, PAIR), lambda i: (0, 0)),
            pl.BlockSpec((2, tokens, PAIR), lambda i: (0, 0, 0)),
        ],
        out_specs=[
            pl.BlockSpec((tokens, PAIR), lambda i: (0, i)),
            pl.BlockSpec((8, PAIR), lambda i: (0, 0)),
        ],
        out_shape=[
            jax.ShapeDtypeStruct((tokens, width), bf16),
            jax.ShapeDtypeStruct((8, PAIR), f32),
        ],
        cost_estimate=pl.CostEstimate(flops=60 * tokens * width, bytes_accessed=10 * tokens * width, transcendentals=0),
        name="rope_back",
    )(dq, dkv, projected, gains, tables)


def three_parts(values):
    first = values.astype(bf16).astype(f32)
    second = (values - first).astype(bf16).astype(f32)
    return first, second, values - first - second


def spread_kv(kv, key_marks, keys, vals):
    both = kv[...]
    lane = lanes(both.shape)
    keys[...] = jnp.where(lane < HEAD_DIM, both, key_marks[...])
    vals[...] = jnp.where(lane < HEAD_DIM, jnp.where(lane < 3, 1.0, 0.0).astype(bf16), both)


MARK = 8


def attend_kernel(tq, tk, offset, q, kv, key_marks, query_marks, out, q_marked, keys, vals, rows):
    local_len = q.shape[0]
    group = q.shape[1] // HEAD_DIM
    spread_kv(kv, key_marks, keys, vals)
    lane1 = lanes((tq, PAIR))
    for tile in range(local_len // tq):
        part = slice(tile * tq, (tile + 1) * tq)
        for head in range(group):
            wide = q[part, (head // 2) * PAIR : (head // 2 + 1) * PAIR].astype(f32)
            if head % 2:
                wide = pltpu.roll(wide, HEAD_DIM, axis=1)
            marked = jnp.where(lane1 < HEAD_DIM, wide, query_marks[part].astype(f32))
            rows[head * tq : (head + 1) * tq] = marked.astype(bf16)
        first = offset[0] + tile * tq

        def block(index, total, masked):
            span = pl.ds(pl.multiple_of(index * tk, tk), tk)
            expo = jnp.exp(dot(rows[...], keys[span], NT))
            if masked:
                query_pos = first + lax.broadcasted_iota(jnp.int32, (tq, tk), 0)
                key_pos = index * tk + lax.broadcasted_iota(jnp.int32, (tq, tk), 1)
                expo = jnp.where((key_pos <= query_pos)[None], expo.reshape(group, tq, tk), 0.0)
                expo = expo.reshape(group * tq, tk)
            return total + dot(expo.astype(bf16), vals[span], NN)

        full = first // tk
        end = (first + tq + tk - 1) // tk
        total = jnp.zeros((group * tq, PAIR), f32)
        total = lax.fori_loop(0, full, lambda i, t: block(i, t, False), total)
        total = lax.fori_loop(full, end, lambda i, t: block(i, t, True), total)
        denominator = total[:, 0:1]
        mixed = total / denominator
        one, two, three = three_parts(-jnp.log(denominator))
        lane = lanes(total.shape) - HEAD_DIM - MARK
        kept = rows[...].astype(f32)
        kept = jnp.where(lane == 0, one, jnp.where(lane == 1, two, jnp.where(lane == 2, three, kept)))
        kept = kept.astype(bf16)
        for head in range(group):
            q_marked[head, part] = kept[head * tq : (head + 1) * tq]
        for head in range(0, group, 2):
            even = pltpu.roll(mixed[head * tq : (head + 1) * tq], HEAD_DIM, axis=1)
            odd = mixed[(head + 1) * tq : (head + 2) * tq]
            out[part, (head // 2) * PAIR : (head // 2 + 1) * PAIR] = jnp.where(lane1 < HEAD_DIM, even, odd)


def attention_cost(tokens, products):
    pairs = HEADS * tokens * ROW_LEN
    return pl.CostEstimate(flops=products * 2 * 4 * HEAD_DIM * pairs, bytes_accessed=1 << 24, transcendentals=pairs)


def attend(offset, q, kv, key_marks, query_marks):
    tokens = q.shape[0]
    keys = kv.shape[0]
    group = HEADS // KV_HEADS
    width = group * HEAD_DIM
    tq, tk = tokens, min(512, keys)
    spec = pltpu.PrefetchScalarGridSpec(
        num_scalar_prefetch=1,
        grid=(KV_HEADS,),
        in_specs=[
            pl.BlockSpec((tokens, width), lambda g, _: (0, g)),
            pl.BlockSpec((keys, PAIR), lambda g, _: (0, g)),
            pl.BlockSpec((keys, PAIR), lambda g, _: (0, 0)),
            pl.BlockSpec((tokens, PAIR), lambda g, _: (0, 0)),
        ],
        out_specs=[
            pl.BlockSpec((tokens, width), lambda g, _: (0, g)),
            pl.BlockSpec((group, tokens, PAIR), lambda g, _: (g, 0, 0)),
        ],
        scratch_shapes=[
            pltpu.VMEM((keys, PAIR), bf16),
            pltpu.VMEM((keys, PAIR), bf16),
            pltpu.VMEM((group * tq, PAIR), bf16),
        ],
    )
    return pl.pallas_call(
        functools.partial(attend_kernel, tq, tk),
        grid_spec=spec,
        out_shape=[
            jax.ShapeDtypeStruct((tokens, Q_WIDTH), f32),
            jax.ShapeDtypeStruct((HEADS, tokens, PAIR), bf16),
        ],
        compiler_params=pltpu.CompilerParams(vmem_limit_bytes=56 << 20),
        cost_estimate=attention_cost(tokens, 2),
        name="attend",
    )(offset, q, kv, key_marks, query_marks)


def attend_back_kernel(
    tq, tk, offset, q_marked, d_out, out, kv, key_marks, dq, dkv, keys, vals, d_rows, rows, dk_sum, dv_sum
):
    local_len = d_out.shape[0]
    group = d_out.shape[1] // HEAD_DIM
    spread_kv(kv, key_marks, keys, vals)
    dk_sum[...] = jnp.zeros_like(dk_sum)
    dv_sum[...] = jnp.zeros_like(dv_sum)
    lane1 = lanes((tq, PAIR))
    for tile in range(local_len // tq):
        part = slice(tile * tq, (tile + 1) * tq)
        for head in range(group):
            pair = slice((head // 2) * PAIR, (head // 2 + 1) * PAIR)
            wide = d_out[part, pair].astype(f32)
            mine = (lane1 < HEAD_DIM) if head % 2 == 0 else (lane1 >= HEAD_DIM)
            delta = jnp.sum(jnp.where(mine, wide * out[part, pair], 0.0), axis=1, keepdims=True)
            one, two, three = three_parts(-delta)
            if head % 2 == 0:
                wide = pltpu.roll(wide, HEAD_DIM, axis=1)
            marks = jnp.where(lane1 == 0, one, jnp.where(lane1 == 1, two, jnp.where(lane1 == 2, three, 0.0)))
            d_rows[head * tq : (head + 1) * tq] = jnp.where(lane1 < HEAD_DIM, marks, wide).astype(bf16)
            rows[head * tq : (head + 1) * tq] = q_marked[head, part]
        first = offset[0] + tile * tq

        def block(index, total, masked):
            span = pl.ds(pl.multiple_of(index * tk, tk), tk)
            prob = jnp.exp(dot(keys[span], rows[...], NT))
            if masked:
                key_pos = index * tk + lax.broadcasted_iota(jnp.int32, (tk, tq), 0)
                query_pos = first + lax.broadcasted_iota(jnp.int32, (tk, tq), 1)
                prob = jnp.where(jnp.concatenate([key_pos <= query_pos] * group, axis=1), prob, 0.0)
            d_scores = (prob * dot(vals[span], d_rows[...], NT)).astype(bf16)
            dv_sum[span] += dot(prob.astype(bf16), d_rows[...], NN)
            dk_sum[span] += dot(d_scores, rows[...], NN)
            return total + dot(d_scores, keys[span], TN)

        full = first // tk
        end = (first + tq + tk - 1) // tk
        total = jnp.zeros((group * tq, PAIR), f32)
        total = lax.fori_loop(0, full, lambda i, t: block(i, t, False), total)
        total = lax.fori_loop(full, end, lambda i, t: block(i, t, True), total)
        for head in range(0, group, 2):
            even = total[head * tq : (head + 1) * tq]
            odd = pltpu.roll(total[(head + 1) * tq : (head + 2) * tq], HEAD_DIM, axis=1)
            dq[part, (head // 2) * PAIR : (head // 2 + 1) * PAIR] = jnp.where(lane1 < HEAD_DIM, even, odd)
    dkv[...] = jnp.where(lanes(dk_sum.shape) < HEAD_DIM, dk_sum[...], dv_sum[...]).astype(bf16)


def attend_back(offset, q_marked, d_out, out, kv, key_marks):
    tokens = d_out.shape[0]
    keys = kv.shape[0]
    group = HEADS // KV_HEADS
    width = group * HEAD_DIM
    tq, tk = tokens, min(512, keys)
    spec = pltpu.PrefetchScalarGridSpec(
        num_scalar_prefetch=1,
        grid=(KV_HEADS,),
        in_specs=[
            pl.BlockSpec((group, tokens, PAIR), lambda g, _: (g, 0, 0)),
            pl.BlockSpec((tokens, width), lambda g, _: (0, g)),
            pl.BlockSpec((tokens, width), lambda g, _: (0, g)),
            pl.BlockSpec((keys, PAIR), lambda g, _: (0, g)),
            pl.BlockSpec((keys, PAIR), lambda g, _: (0, 0)),
        ],
        out_specs=[
            pl.BlockSpec((tokens, width), lambda g, _: (0, g)),
            pl.BlockSpec((keys, PAIR), lambda g, _: (0, g)),
        ],
        scratch_shapes=[
            pltpu.VMEM((keys, PAIR), bf16),
            pltpu.VMEM((keys, PAIR), bf16),
            pltpu.VMEM((group * tq, PAIR), bf16),
            pltpu.VMEM((group * tq, PAIR), bf16),
            pltpu.VMEM((keys, PAIR), f32),
            pltpu.VMEM((keys, PAIR), f32),
        ],
    )
    return pl.pallas_call(
        functools.partial(attend_back_kernel, tq, tk),
        grid_spec=spec,
        out_shape=[
            jax.ShapeDtypeStruct((tokens, Q_WIDTH), f32),
            jax.ShapeDtypeStruct(kv.shape, bf16),
        ],
        compiler_params=pltpu.CompilerParams(vmem_limit_bytes=56 << 20),
        cost_estimate=attention_cost(tokens, 4),
        name="attend_back",
    )(offset, q_marked, d_out, out, kv, key_marks)


def feed_kernel(normed, upstream, weights, hidden, both, result, back):
    units = hidden.shape[1]
    values = normed[...]
    gate = dot(values, weights[:, :units], NN)
    up = dot(values, weights[:, units : 2 * units], NN)
    d_hidden = dot(upstream[...], weights[:, 2 * units :], NN)
    sigmoid = 1.0 / (1.0 + jnp.exp(-gate))
    silu = gate * sigmoid
    low = (silu * up).astype(bf16)
    hidden[...] = low
    result[...] = dot(low, weights[:, 2 * units :], NT).astype(bf16)
    d_gate = (d_hidden * up * sigmoid * (1.0 + gate * (1.0 - sigmoid))).astype(bf16)
    d_up = (d_hidden * silu).astype(bf16)
    both[:, :units] = d_gate
    both[:, units:] = d_up
    d_normed = dot(d_gate, weights[:, :units], NT) + dot(d_up, weights[:, units : 2 * units], NT)
    back[...] = d_normed.astype(bf16)


def feed(normed, upstream, weights):
    tokens = normed.shape[0]
    units = weights.shape[1] // 3
    tile = 256
    row = lambda n: pl.BlockSpec((tile, n), lambda i: (i, 0))
    out = lambda n: jax.ShapeDtypeStruct((tokens, n), bf16)
    return pl.pallas_call(
        feed_kernel,
        grid=(tokens // tile,),
        in_specs=[
            row(D),
            row(D),
            pl.BlockSpec(weights.shape, lambda i: (0, 0), pipeline_mode=pl.Buffered(1)),
        ],
        out_specs=[row(units), row(2 * units), row(D), row(D)],
        out_shape=[out(units), out(2 * units), out(D), out(D)],
        compiler_params=pltpu.CompilerParams(vmem_limit_bytes=56 << 20),
        cost_estimate=pl.CostEstimate(
            flops=20 * tokens * D * units,
            bytes_accessed=2 * (3 * D * units + tokens * (4 * D + 3 * units)),
            transcendentals=tokens * units,
        ),
        name="feed",
    )(normed, upstream, weights)


def weight_gradient_kernel(count, *refs):
    normed, upstream, both, hidden = (refs[i * count : (i + 1) * count] for i in range(4))
    out = refs[-1]
    units = hidden[0].shape[1]
    expand = shrink = None
    for j in range(count):
        one = dot(normed[j][...], both[j][...], TN)
        two = dot(upstream[j][...], hidden[j][...], TN)
        expand = one if expand is None else expand + one
        shrink = two if shrink is None else shrink + two
    out[:, : 2 * units] = expand.astype(bf16)
    out[:, 2 * units :] = shrink.astype(bf16)


def weight_gradient(normed, upstream, both, hidden):
    count = len(normed)
    units = hidden[0].shape[1]
    tile = 256
    columns = [pl.BlockSpec((a.shape[0], tile), lambda i: (0, i)) for a in normed]
    whole = lambda xs: [pl.BlockSpec(a.shape, lambda i: (0, 0), pipeline_mode=pl.Buffered(1)) for a in xs]
    tokens = sum(a.shape[0] for a in normed)
    return pl.pallas_call(
        functools.partial(weight_gradient_kernel, count),
        grid=(D // tile,),
        in_specs=columns + columns + whole(both) + whole(hidden),
        out_specs=pl.BlockSpec((tile, 3 * units), lambda i: (i, 0)),
        out_shape=jax.ShapeDtypeStruct((D, 3 * units), bf16),
        compiler_params=pltpu.CompilerParams(vmem_limit_bytes=60 << 20),
        cost_estimate=pl.CostEstimate(
            flops=8 * tokens * D * units, bytes_accessed=2 * tokens * (2 * D + 3 * units), transcendentals=0
        ),
        name="weight_gradient",
    )(*normed, *upstream, *both, *hidden)


class Links:
    def __init__(self, n_dp, n_seq):
        self.n_z = n_dp // CORES
        self.n_seq = n_seq
        self.plane = CORES * n_seq

    def place(self):
        dp = lax.axis_index("dp")
        return dp // CORES, dp % CORES, lax.axis_index("seq")

    def send(self, values, pairs_of):
        pairs = []
        for z in range(self.n_z):
            for c in range(CORES):
                for s in range(self.n_seq):
                    to = pairs_of(z, c, s)
                    if to is not None:
                        tz, tc, ts = to
                        pairs.append((((z * CORES + c) * self.n_seq + s), (tz * CORES + tc) * self.n_seq + ts))
        return lax.ppermute(values, AXES, pairs)

    def core(self, values):
        return self.send(values, lambda z, c, s: (z, 1 - c, s))

    def peer(self, values, k):
        return self.send(values, lambda z, c, s: (z, c, s ^ k))

    def up(self, values, first, last):
        return self.send(values, lambda z, c, s: (z + 1, c, s) if first <= z <= last else None)

    def down(self, values, first, last):
        return self.send(values, lambda z, c, s: (z - 1, c, s) if first <= z <= last else None)

    def seq_gather(self, values):
        if self.n_seq != 4:
            return [[values]] + [[self.peer(values, k)] for k in range(1, self.n_seq)]
        half = values.shape[0] // 2
        one, two = self.peer(values, 1), self.peer(values, 2)
        top = self.peer(one[:half], 2)
        bottom = self.peer(two[half:], 1)
        return [[values], [one], [two], [top, bottom]]

    def seq_scatter(self, parts, add):
        if self.n_seq != 4:
            return add([parts[0]] + [self.peer(parts[k], k) for k in range(1, self.n_seq)])
        half = parts[0].shape[0] // 2
        top = self.peer(parts[3][:half], 1)
        bottom = self.peer(parts[3][half:], 2)
        two = [self.peer(add([parts[2][:half], top]), 2), self.peer(parts[2][half:], 2)]
        one = [self.peer(parts[1][:half], 1), self.peer(add([parts[1][half:], bottom]), 1)]
        return [add([parts[0][:half], two[0], one[0]]), add([parts[0][half:], two[1], one[1]])]

    def line_gather(self, values):
        n = self.n_z
        z, _, _ = self.place()
        rows = values.shape[0]
        ups, downs = [values], [values]
        for k in range(1, n):
            ups.append(self.up(ups[-1], k - 1, n - 2))
            downs.append(self.down(downs[-1], 1, n - k))
        full = lax.dynamic_update_slice_in_dim(jnp.zeros((n * rows, values.shape[1]), values.dtype), values, z * rows, 0)
        for r in range(1, n):
            piece = jnp.where(z + r < n, downs[r], ups[n - r])
            full = lax.dynamic_update_slice_in_dim(full, piece, ((z + r) % n) * rows, 0)
        return full

    def line_scatter(self, full, add):
        n = self.n_z
        z, _, _ = self.place()
        rows = full.shape[0] // n
        take = lambda d: lax.dynamic_slice_in_dim(full, jnp.clip(d, 0, n - 1) * rows, rows, 0)
        above = below = None
        for k in range(1, n):
            one, two = take(z + n - k), take(z - n + k)
            one = one if above is None else add([one, above])
            two = two if below is None else add([two, below])
            above = self.up(one, 0, k - 1)
            below = self.down(two, n - k, n - 1)
        return [take(z)] + ([above, below] if n > 1 else [])


def add_low(parts):
    return functools.reduce(lambda a, b: a + b, [p.astype(f32) for p in parts]).astype(bf16)


def add_wide(parts):
    return functools.reduce(lambda a, b: a + b, [p.astype(f32) for p in parts])


def body(
    n_dp,
    n_seq,
    tokens,
    joined_weight,
    output_weight,
    expand_weight,
    shrink_weight,
    norm_gains,
    doc_lengths,
    cotangent,
):
    links = Links(n_dp, n_seq)
    n_z, plane = links.n_z, links.plane
    z, core, seq = links.place()
    me = core * n_seq + seq
    devices = n_dp * n_seq
    local_len = tokens.shape[1]
    rows = D // devices
    units = FF // plane
    own_gains = GAINS // devices
    offset = seq * local_len

    kv_columns = joined_weight[:, Q_WIDTH:].reshape(rows, 2, KV_HEADS, HEAD_DIM).transpose(0, 2, 1, 3)
    gain_block = jnp.pad(norm_gains, (0, rows * PAIR - own_gains)).reshape(rows, PAIR)
    joined_block = jnp.concatenate(
        [joined_weight[:, :Q_WIDTH], kv_columns.reshape(rows, 2 * KV_WIDTH), gain_block], axis=1
    )
    joined_all = lax.all_gather(joined_block, AXES, axis=0, tiled=True)
    output_all = lax.all_gather(output_weight.T, AXES, axis=0, tiled=True)
    gains = joined_all[:, QKV:].reshape(devices, rows * PAIR)[:, :own_gains].reshape(GAINS).astype(f32)
    joined_all = joined_all[:, :QKV]
    gain_one = gains[:D]
    gain_query = gains[D : D + HEAD_DIM]
    gain_key = gains[D + HEAD_DIM : D + PAIR]
    gain_two = gains[D + PAIR :]
    head_gains = jnp.stack([jnp.tile(gain_query, 2), jnp.tile(gain_key, 2)])

    shrink_rows = shrink_weight.T
    shares = []
    for k in range(plane):
        p = (core ^ (k // n_seq)) * n_seq + (seq ^ (k % n_seq))
        take = lambda a, start: lax.dynamic_slice_in_dim(a, start + p * units, units, 1)
        share = jnp.concatenate([take(expand_weight, 0), take(expand_weight, FF), take(shrink_rows, 0)], axis=1)
        if k:
            share = links.send(share, lambda a, c, s: (a, c ^ (k // n_seq), s ^ (k % n_seq)))
        shares.append((p, share))
    block = jnp.zeros((plane * rows, 3 * units), bf16)
    for p, share in shares:
        block = lax.dynamic_update_slice_in_dim(block, share, p * rows, 0)
    weights = links.line_gather(block)

    half = HEAD_DIM // 2
    frequency = 10000.0 ** (-jnp.arange(half, dtype=f32) / half)
    angles = (offset + jnp.arange(local_len, dtype=jnp.int32)).astype(f32)[:, None] * frequency[None, :]
    cosine, sine = jnp.cos(angles), jnp.sin(angles)
    tables = jnp.stack(
        [jnp.concatenate([cosine] * 4, axis=1), jnp.concatenate([-sine, sine, -sine, sine], axis=1)]
    )
    places = jnp.arange(ROW_LEN, dtype=jnp.int32)
    docs = jnp.zeros((ROW_LEN,), jnp.int32)
    bound = 0
    for index in range(doc_lengths.shape[1] - 1):
        bound = bound + doc_lengths[0, index]
        docs = docs + (places >= bound).astype(jnp.int32)
    mark = jnp.arange(PAIR, dtype=jnp.int32)[None] - HEAD_DIM
    same = (mark >= 0) & (mark < MARK) & (mark == docs[:, None])
    other = (mark >= 0) & (mark < MARK) & (mark != docs[:, None])
    carries = (mark >= MARK) & (mark < MARK + 3)
    key_marks = jnp.where(other, -1024.0, jnp.where(carries, 1.0, 0.0)).astype(bf16)
    query_marks = lax.dynamic_slice_in_dim(same.astype(bf16), offset, local_len, 0)
    offset_array = jnp.reshape(offset, (1,)).astype(jnp.int32)

    flat = tokens.reshape(local_len, D).astype(f32)
    scale_one = rms_scale(flat)
    normed_low = (flat * scale_one * gain_one).astype(bf16)
    projected = dot(normed_low, joined_all, NN)
    turned = rope(projected, head_gains, tables)
    own_kv = turned[:, Q_WIDTH:]
    kv = jnp.zeros((ROW_LEN, 2 * KV_WIDTH), bf16)
    for k, parts in enumerate(links.seq_gather(own_kv)):
        start = (seq ^ k) * local_len
        for part in parts:
            kv = lax.dynamic_update_slice_in_dim(kv, part, start, 0)
            start = start + part.shape[0]
    attended, q_marked = attend(offset_array, turned, kv, key_marks, query_marks)
    attended_low = attended.astype(bf16)
    residual = flat + dot(attended_low, output_all, NT)
    scale_two = rms_scale(residual)
    normed_two = (residual * scale_two * gain_two).astype(bf16)

    def plane_gather(values):
        groups = []
        for parts in links.seq_gather(values):
            parts = parts + [links.core(p) for p in parts]
            groups.append(jnp.concatenate(parts, axis=0))
        return groups

    upstream_low = cotangent.reshape(local_len, D)
    upstream_all = plane_gather(upstream_low)
    normed_all = plane_gather(normed_two)
    hidden_all, both_all, result_parts, back_parts = [], [], [], []
    for values, above in zip(normed_all, upstream_all):
        hidden, both, result, back = feed(values, above, weights)
        hidden_all.append(hidden)
        both_all.append(both)
        result_parts.append(result)
        back_parts.append(back)

    def plane_scatter(parts):
        parts = [add_low([p[:local_len], links.core(p[local_len:])]) for p in parts]
        out = links.seq_scatter(parts, add_low)
        return jnp.concatenate(out, axis=0) if isinstance(out, list) else out

    grad_normed_two = plane_scatter(back_parts).astype(f32)
    share_gradient = weight_gradient(normed_all, upstream_all, both_all, hidden_all)
    feed_result = plane_scatter(result_parts).astype(f32)
    layer_output = (residual + feed_result).astype(bf16)

    mine = add_low(links.line_scatter(share_gradient, add_low))
    expand_gradient = jnp.zeros((rows, 2 * FF), f32)
    shrink_gradient = jnp.zeros((rows, FF), f32)
    for k in range(plane):
        p = (core ^ (k // n_seq)) * n_seq + (seq ^ (k % n_seq))
        piece = lax.dynamic_slice_in_dim(mine, p * rows, rows, 0)
        if k:
            piece = links.send(piece, lambda a, c, s: (a, c ^ (k // n_seq), s ^ (k % n_seq)))
        piece = piece.astype(f32)
        put = lambda a, part, start: lax.dynamic_update_slice_in_dim(a, part, start + p * units, 1)
        expand_gradient = put(expand_gradient, piece[:, :units], 0)
        expand_gradient = put(expand_gradient, piece[:, units : 2 * units], FF)
        shrink_gradient = put(shrink_gradient, piece[:, 2 * units :], 0)
    shrink_gradient = shrink_gradient.T

    upstream = upstream_low.astype(f32)
    gain_two_grad = jnp.sum(grad_normed_two * residual * scale_two, axis=0)
    grad_residual = upstream + norm_back(grad_normed_two, residual, scale_two, gain_two)
    grad_attn_low = grad_residual.astype(bf16)
    output_term = dot(grad_attn_low, attended_low, TN).astype(bf16)
    grad_out_low = dot(grad_attn_low, output_all, NN).astype(bf16)
    grad_query, grad_kv_all = attend_back(offset_array, q_marked, grad_out_low, attended, kv, key_marks)
    kv_parts = [lax.dynamic_slice_in_dim(grad_kv_all, (seq ^ k) * local_len, local_len, 0) for k in range(n_seq)]
    grad_kv = links.seq_scatter(kv_parts, add_wide if n_seq != 4 else add_low)
    grad_kv = jnp.concatenate(grad_kv, axis=0) if isinstance(grad_kv, list) else grad_kv
    grad_projected, head_gain_sums = rope_back(grad_query, grad_kv.astype(f32), projected, head_gains, tables)
    joined_term = dot(normed_low, grad_projected, TN).astype(bf16)
    grad_normed = dot(grad_projected, joined_all, NT)
    gain_one_grad = jnp.sum(grad_normed * flat * scale_one, axis=0)
    token_gradient = grad_residual + norm_back(grad_normed, flat, scale_one, gain_one)
    gain_query_grad = head_gain_sums[0, :HEAD_DIM] + head_gain_sums[0, HEAD_DIM:]
    gain_key_grad = head_gain_sums[1, :HEAD_DIM]
    gain_grads = jnp.concatenate([gain_one_grad, gain_query_grad, gain_key_grad, gain_two_grad])
    gain_block = jnp.pad(gain_grads.reshape(devices, own_gains), ((0, 0), (0, rows * PAIR - own_gains)))
    gain_block = gain_block.reshape(devices * rows, PAIR).astype(bf16)

    def scatter_all(full):
        width = full.shape[1]
        full = full.reshape(n_z, CORES, n_seq, rows, width)
        other = links.core(lax.dynamic_index_in_dim(full, 1 - core, 1, keepdims=False))
        full = add_low([lax.dynamic_index_in_dim(full, core, 1, keepdims=False), other])
        full = full.transpose(1, 0, 2, 3).reshape(n_seq, n_z * rows, width)
        parts = [lax.dynamic_index_in_dim(full, seq ^ k, 0, keepdims=False) for k in range(n_seq)]
        out = links.seq_scatter(parts, add_low)
        out = jnp.concatenate(out, axis=0) if isinstance(out, list) else out
        return add_wide(links.line_scatter(out, add_low))

    output_gradient = scatter_all(output_term).T
    joined_sum = scatter_all(jnp.concatenate([joined_term, gain_block], axis=1))
    kv_sum = joined_sum[:, Q_WIDTH:QKV].reshape(rows, KV_HEADS, 2, HEAD_DIM).transpose(0, 2, 1, 3)
    joined_gradient = jnp.concatenate([joined_sum[:, :Q_WIDTH], kv_sum.reshape(rows, 2 * KV_WIDTH)], axis=1)
    gains_gradient = joined_sum[:, QKV:].reshape(rows * PAIR)[:own_gains]
    return (
        layer_output.reshape(1, local_len, D),
        token_gradient.astype(bf16).reshape(1, local_len, D),
        joined_gradient,
        output_gradient,
        expand_gradient,
        shrink_gradient,
        gains_gradient,
    )


def solution(mesh):
    placed = (
        P("dp", "seq", None),
        P(AXES, None),
        P(None, AXES),
        P(AXES, None),
        P(None, AXES),
        P(AXES),
        P("dp", None),
        P("dp", "seq", None),
    )
    return jax.shard_map(
        functools.partial(body, mesh.shape["dp"], mesh.shape["seq"]),
        mesh=mesh,
        in_specs=placed,
        out_specs=(
            P("dp", "seq", None),
            P("dp", "seq", None),
            P(AXES, None),
            P(None, AXES),
            P(AXES, None),
            P(None, AXES),
            P(AXES),
        ),
        check_vma=False,
    )
```

```python
import functools

import jax
import jax.numpy as jnp
from jax import lax
from jax.experimental import pallas as pl
from jax.experimental.pallas import tpu as pltpu
from jax.sharding import PartitionSpec as P

D = 2048
HEADS = 20
KV_HEADS = 5
HEAD_DIM = 64
FF = 6144
ROW_LEN = 2048
GAINS = 4224
PAIR = 2 * HEAD_DIM
Q_WIDTH = HEADS * HEAD_DIM
KV_WIDTH = KV_HEADS * HEAD_DIM
QKV = Q_WIDTH + 2 * KV_WIDTH
CORES = 2

epsilon = 1e-05
f32 = jnp.float32
bf16 = jnp.bfloat16
AXES = ("dp", "seq")
MESH = pl.DeviceIdType.MESH
ANY = pl.BlockSpec(memory_space=pl.ANY)
VMEM = pl.BlockSpec(memory_space=pltpu.VMEM)
NN = (((1,), (0,)), ((), ()))
NT = (((1,), (1,)), ((), ()))
TN = (((0,), (0,)), ((), ()))


def dot(left, right, dims):
    return lax.dot_general(left, right, dims, preferred_element_type=f32)


def rms_scale(values):
    return lax.rsqrt(jnp.mean(values * values, axis=-1, keepdims=True) + epsilon)


def norm_back(upstream, values, scaling, gain_vector):
    weighted = upstream * gain_vector
    average = jnp.mean(weighted * values, axis=-1, keepdims=True)
    return scaling * weighted - values * (scaling * scaling * scaling) * average


def lanes(shape):
    return lax.broadcasted_iota(jnp.int32, shape, len(shape) - 1)


def swap_halves(values):
    half = HEAD_DIM // 2
    first = lanes(values.shape) % HEAD_DIM < half
    return jnp.where(first, pltpu.roll(values, PAIR - half, axis=1), pltpu.roll(values, half, axis=1))


def head_means(values):
    low = lanes(values.shape) < HEAD_DIM
    left = jnp.sum(jnp.where(low, values, 0.0), axis=-1, keepdims=True)
    right = jnp.sum(jnp.where(low, 0.0, values), axis=-1, keepdims=True)
    return jnp.where(low, left, right) * (1.0 / HEAD_DIM)


def rope_kernel(query_pairs, projected, gains, tables, out):
    step = pl.program_id(0)
    is_query = step < query_pairs
    values = projected[...]
    plain = (lanes(values.shape) >= HEAD_DIM) & jnp.logical_not(is_query)
    gain = jnp.where(is_query, gains[0:1], gains[1:2])
    normed = values * lax.rsqrt(head_means(values * values) + epsilon) * gain
    turned = normed * tables[0] + swap_halves(normed) * tables[1]
    turned = turned * jnp.where(is_query, HEAD_DIM**-0.5, 1.0)
    out[...] = jnp.where(plain, values, turned).astype(bf16)


def rope(projected, gains, tables):
    tokens, width = projected.shape
    return pl.pallas_call(
        functools.partial(rope_kernel, Q_WIDTH // PAIR),
        grid=(width // PAIR,),
        in_specs=[
            pl.BlockSpec((tokens, PAIR), lambda i: (0, i)),
            pl.BlockSpec((2, PAIR), lambda i: (0, 0)),
            pl.BlockSpec((2, tokens, PAIR), lambda i: (0, 0, 0)),
        ],
        out_specs=pl.BlockSpec((tokens, PAIR), lambda i: (0, i)),
        out_shape=jax.ShapeDtypeStruct((tokens, width), bf16),
        cost_estimate=pl.CostEstimate(flops=40 * tokens * width, bytes_accessed=6 * tokens * width, transcendentals=0),
        name="rope",
    )(projected, gains, tables)


def rope_back_kernel(query_pairs, dq, dkv, projected, gains, tables, out, gain_sums):
    step = pl.program_id(0)
    is_query = step < query_pairs
    values = projected[...]
    upstream = jnp.where(is_query, dq[...] * HEAD_DIM**-0.5, dkv[...])
    plain = (lanes(values.shape) >= HEAD_DIM) & jnp.logical_not(is_query)
    gain = jnp.where(is_query, gains[0:1], gains[1:2])
    turned = upstream * tables[0] + swap_halves(upstream * tables[1])
    scaling = lax.rsqrt(head_means(values * values) + epsilon)
    weighted = turned * gain
    back = scaling * weighted - values * (scaling * scaling * scaling) * head_means(weighted * values)
    out[...] = jnp.where(plain, upstream, back).astype(bf16)
    sums = jnp.sum(jnp.where(plain, 0.0, turned * values * scaling), axis=0, keepdims=True)

    @pl.when(step == 0)
    def _():
        gain_sums[...] = jnp.zeros_like(gain_sums)

    row = lax.broadcasted_iota(jnp.int32, gain_sums.shape, 0)
    gain_sums[...] += jnp.where(row == jnp.where(is_query, 0, 1), sums, 0.0)


def rope_back(dq, dkv, projected, gains, tables):
    tokens, width = projected.shape
    query_pairs = Q_WIDTH // PAIR
    return pl.pallas_call(
        functools.partial(rope_back_kernel, query_pairs),
        grid=(width // PAIR,),
        in_specs=[
            pl.BlockSpec((tokens, PAIR), lambda i: (0, jnp.minimum(i, query_pairs - 1))),
            pl.BlockSpec((tokens, PAIR), lambda i: (0, jnp.maximum(i - query_pairs, 0))),
            pl.BlockSpec((tokens, PAIR), lambda i: (0, i)),
            pl.BlockSpec((2, PAIR), lambda i: (0, 0)),
            pl.BlockSpec((2, tokens, PAIR), lambda i: (0, 0, 0)),
        ],
        out_specs=[
            pl.BlockSpec((tokens, PAIR), lambda i: (0, i)),
            pl.BlockSpec((8, PAIR), lambda i: (0, 0)),
        ],
        out_shape=[
            jax.ShapeDtypeStruct((tokens, width), bf16),
            jax.ShapeDtypeStruct((8, PAIR), f32),
        ],
        cost_estimate=pl.CostEstimate(flops=60 * tokens * width, bytes_accessed=10 * tokens * width, transcendentals=0),
        name="rope_back",
    )(dq, dkv, projected, gains, tables)


def three_parts(values):
    first = values.astype(bf16).astype(f32)
    second = (values - first).astype(bf16).astype(f32)
    return first, second, values - first - second


def spread_kv(kv, key_marks, keys, vals):
    both = kv[...]
    lane = lanes(both.shape)
    keys[...] = jnp.where(lane < HEAD_DIM, both, key_marks[...])
    vals[...] = jnp.where(lane < HEAD_DIM, jnp.where(lane < 3, 1.0, 0.0).astype(bf16), both)


MARK = 8


def attend_kernel(tq, tk, offset, q, kv, key_marks, query_marks, out, q_marked, keys, vals, rows):
    local_len = q.shape[0]
    group = q.shape[1] // HEAD_DIM
    spread_kv(kv, key_marks, keys, vals)
    lane1 = lanes((tq, PAIR))
    for tile in range(local_len // tq):
        part = slice(tile * tq, (tile + 1) * tq)
        for head in range(group):
            wide = q[part, (head // 2) * PAIR : (head // 2 + 1) * PAIR].astype(f32)
            if head % 2:
                wide = pltpu.roll(wide, HEAD_DIM, axis=1)
            marked = jnp.where(lane1 < HEAD_DIM, wide, query_marks[part].astype(f32))
            rows[head * tq : (head + 1) * tq] = marked.astype(bf16)
        first = offset[0] + tile * tq

        def block(index, total, masked):
            span = pl.ds(pl.multiple_of(index * tk, tk), tk)
            expo = jnp.exp(dot(rows[...], keys[span], NT))
            if masked:
                query_pos = first + lax.broadcasted_iota(jnp.int32, (tq, tk), 0)
                key_pos = index * tk + lax.broadcasted_iota(jnp.int32, (tq, tk), 1)
                expo = jnp.where((key_pos <= query_pos)[None], expo.reshape(group, tq, tk), 0.0)
                expo = expo.reshape(group * tq, tk)
            return total + dot(expo.astype(bf16), vals[span], NN)

        full = first // tk
        end = (first + tq + tk - 1) // tk
        total = jnp.zeros((group * tq, PAIR), f32)
        total = lax.fori_loop(0, full, lambda i, t: block(i, t, False), total)
        total = lax.fori_loop(full, end, lambda i, t: block(i, t, True), total)
        denominator = total[:, 0:1]
        mixed = total / denominator
        one, two, three = three_parts(-jnp.log(denominator))
        lane = lanes(total.shape) - HEAD_DIM - MARK
        kept = rows[...].astype(f32)
        kept = jnp.where(lane == 0, one, jnp.where(lane == 1, two, jnp.where(lane == 2, three, kept)))
        kept = kept.astype(bf16)
        for head in range(group):
            q_marked[head, part] = kept[head * tq : (head + 1) * tq]
        for head in range(0, group, 2):
            even = pltpu.roll(mixed[head * tq : (head + 1) * tq], HEAD_DIM, axis=1)
            odd = mixed[(head + 1) * tq : (head + 2) * tq]
            out[part, (head // 2) * PAIR : (head // 2 + 1) * PAIR] = jnp.where(lane1 < HEAD_DIM, even, odd)


def attention_cost(tokens, products):
    pairs = HEADS * tokens * ROW_LEN
    return pl.CostEstimate(flops=products * 2 * 4 * HEAD_DIM * pairs, bytes_accessed=1 << 24, transcendentals=pairs)


def attend(offset, q, kv, key_marks, query_marks):
    tokens = q.shape[0]
    keys = kv.shape[0]
    group = HEADS // KV_HEADS
    width = group * HEAD_DIM
    tq, tk = tokens, min(512, keys)
    spec = pltpu.PrefetchScalarGridSpec(
        num_scalar_prefetch=1,
        grid=(KV_HEADS,),
        in_specs=[
            pl.BlockSpec((tokens, width), lambda g, _: (0, g)),
            pl.BlockSpec((keys, PAIR), lambda g, _: (0, g)),
            pl.BlockSpec((keys, PAIR), lambda g, _: (0, 0)),
            pl.BlockSpec((tokens, PAIR), lambda g, _: (0, 0)),
        ],
        out_specs=[
            pl.BlockSpec((tokens, width), lambda g, _: (0, g)),
            pl.BlockSpec((group, tokens, PAIR), lambda g, _: (g, 0, 0)),
        ],
        scratch_shapes=[
            pltpu.VMEM((keys, PAIR), bf16),
            pltpu.VMEM((keys, PAIR), bf16),
            pltpu.VMEM((group * tq, PAIR), bf16),
        ],
    )
    return pl.pallas_call(
        functools.partial(attend_kernel, tq, tk),
        grid_spec=spec,
        out_shape=[
            jax.ShapeDtypeStruct((tokens, Q_WIDTH), f32),
            jax.ShapeDtypeStruct((HEADS, tokens, PAIR), bf16),
        ],
        compiler_params=pltpu.CompilerParams(vmem_limit_bytes=56 << 20),
        cost_estimate=attention_cost(tokens, 2),
        name="attend",
    )(offset, q, kv, key_marks, query_marks)


def attend_back_kernel(
    tq, tk, offset, q_marked, d_out, out, kv, key_marks, dq, dkv, keys, vals, d_rows, rows, dk_sum, dv_sum
):
    local_len = d_out.shape[0]
    group = d_out.shape[1] // HEAD_DIM
    spread_kv(kv, key_marks, keys, vals)
    dk_sum[...] = jnp.zeros_like(dk_sum)
    dv_sum[...] = jnp.zeros_like(dv_sum)
    lane1 = lanes((tq, PAIR))
    for tile in range(local_len // tq):
        part = slice(tile * tq, (tile + 1) * tq)
        for head in range(group):
            pair = slice((head // 2) * PAIR, (head // 2 + 1) * PAIR)
            wide = d_out[part, pair].astype(f32)
            mine = (lane1 < HEAD_DIM) if head % 2 == 0 else (lane1 >= HEAD_DIM)
            delta = jnp.sum(jnp.where(mine, wide * out[part, pair], 0.0), axis=1, keepdims=True)
            one, two, three = three_parts(-delta)
            if head % 2 == 0:
                wide = pltpu.roll(wide, HEAD_DIM, axis=1)
            marks = jnp.where(lane1 == 0, one, jnp.where(lane1 == 1, two, jnp.where(lane1 == 2, three, 0.0)))
            d_rows[head * tq : (head + 1) * tq] = jnp.where(lane1 < HEAD_DIM, marks, wide).astype(bf16)
            rows[head * tq : (head + 1) * tq] = q_marked[head, part]
        first = offset[0] + tile * tq

        def block(index, total, masked):
            span = pl.ds(pl.multiple_of(index * tk, tk), tk)
            prob = jnp.exp(dot(keys[span], rows[...], NT))
            if masked:
                key_pos = index * tk + lax.broadcasted_iota(jnp.int32, (tk, tq), 0)
                query_pos = first + lax.broadcasted_iota(jnp.int32, (tk, tq), 1)
                prob = jnp.where(jnp.concatenate([key_pos <= query_pos] * group, axis=1), prob, 0.0)
            d_scores = (prob * dot(vals[span], d_rows[...], NT)).astype(bf16)
            dv_sum[span] += dot(prob.astype(bf16), d_rows[...], NN)
            dk_sum[span] += dot(d_scores, rows[...], NN)
            return total + dot(d_scores, keys[span], TN)

        full = first // tk
        end = (first + tq + tk - 1) // tk
        total = jnp.zeros((group * tq, PAIR), f32)
        total = lax.fori_loop(0, full, lambda i, t: block(i, t, False), total)
        total = lax.fori_loop(full, end, lambda i, t: block(i, t, True), total)
        for head in range(0, group, 2):
            even = total[head * tq : (head + 1) * tq]
            odd = pltpu.roll(total[(head + 1) * tq : (head + 2) * tq], HEAD_DIM, axis=1)
            dq[part, (head // 2) * PAIR : (head // 2 + 1) * PAIR] = jnp.where(lane1 < HEAD_DIM, even, odd)
    dkv[...] = jnp.where(lanes(dk_sum.shape) < HEAD_DIM, dk_sum[...], dv_sum[...]).astype(bf16)


def attend_back(offset, q_marked, d_out, out, kv, key_marks):
    tokens = d_out.shape[0]
    keys = kv.shape[0]
    group = HEADS // KV_HEADS
    width = group * HEAD_DIM
    tq, tk = tokens, min(512, keys)
    spec = pltpu.PrefetchScalarGridSpec(
        num_scalar_prefetch=1,
        grid=(KV_HEADS,),
        in_specs=[
            pl.BlockSpec((group, tokens, PAIR), lambda g, _: (g, 0, 0)),
            pl.BlockSpec((tokens, width), lambda g, _: (0, g)),
            pl.BlockSpec((tokens, width), lambda g, _: (0, g)),
            pl.BlockSpec((keys, PAIR), lambda g, _: (0, g)),
            pl.BlockSpec((keys, PAIR), lambda g, _: (0, 0)),
        ],
        out_specs=[
            pl.BlockSpec((tokens, width), lambda g, _: (0, g)),
            pl.BlockSpec((keys, PAIR), lambda g, _: (0, g)),
        ],
        scratch_shapes=[
            pltpu.VMEM((keys, PAIR), bf16),
            pltpu.VMEM((keys, PAIR), bf16),
            pltpu.VMEM((group * tq, PAIR), bf16),
            pltpu.VMEM((group * tq, PAIR), bf16),
            pltpu.VMEM((keys, PAIR), f32),
            pltpu.VMEM((keys, PAIR), f32),
        ],
    )
    return pl.pallas_call(
        functools.partial(attend_back_kernel, tq, tk),
        grid_spec=spec,
        out_shape=[
            jax.ShapeDtypeStruct((tokens, Q_WIDTH), f32),
            jax.ShapeDtypeStruct(kv.shape, bf16),
        ],
        compiler_params=pltpu.CompilerParams(vmem_limit_bytes=56 << 20),
        cost_estimate=attention_cost(tokens, 4),
        name="attend_back",
    )(offset, q_marked, d_out, out, kv, key_marks)


def feed_kernel(normed, upstream, weights, hidden, both, result, back):
    units = hidden.shape[1]
    values = normed[...]
    gate = dot(values, weights[:, :units], NN)
    up = dot(values, weights[:, units : 2 * units], NN)
    d_hidden = dot(upstream[...], weights[:, 2 * units :], NN)
    sigmoid = 1.0 / (1.0 + jnp.exp(-gate))
    silu = gate * sigmoid
    low = (silu * up).astype(bf16)
    hidden[...] = low
    result[...] = dot(low, weights[:, 2 * units :], NT).astype(bf16)
    d_gate = (d_hidden * up * sigmoid * (1.0 + gate * (1.0 - sigmoid))).astype(bf16)
    d_up = (d_hidden * silu).astype(bf16)
    both[:, :units] = d_gate
    both[:, units:] = d_up
    d_normed = dot(d_gate, weights[:, :units], NT) + dot(d_up, weights[:, units : 2 * units], NT)
    back[...] = d_normed.astype(bf16)


def feed(normed, upstream, weights):
    tokens = normed.shape[0]
    units = weights.shape[1] // 3
    tile = 256
    row = lambda n: pl.BlockSpec((tile, n), lambda i: (i, 0))
    out = lambda n: jax.ShapeDtypeStruct((tokens, n), bf16)
    return pl.pallas_call(
        feed_kernel,
        grid=(tokens // tile,),
        in_specs=[
            row(D),
            row(D),
            pl.BlockSpec(weights.shape, lambda i: (0, 0), pipeline_mode=pl.Buffered(1)),
        ],
        out_specs=[row(units), row(2 * units), row(D), row(D)],
        out_shape=[out(units), out(2 * units), out(D), out(D)],
        compiler_params=pltpu.CompilerParams(vmem_limit_bytes=56 << 20),
        cost_estimate=pl.CostEstimate(
            flops=20 * tokens * D * units,
            bytes_accessed=2 * (3 * D * units + tokens * (4 * D + 3 * units)),
            transcendentals=tokens * units,
        ),
        name="feed",
    )(normed, upstream, weights)


def weight_gradient_kernel(count, *refs):
    normed, upstream, both, hidden = (refs[i * count : (i + 1) * count] for i in range(4))
    out = refs[-1]
    units = hidden[0].shape[1]
    expand = shrink = None
    for j in range(count):
        one = dot(normed[j][...], both[j][...], TN)
        two = dot(upstream[j][...], hidden[j][...], TN)
        expand = one if expand is None else expand + one
        shrink = two if shrink is None else shrink + two
    out[:, : 2 * units] = expand.astype(bf16)
    out[:, 2 * units :] = shrink.astype(bf16)


def weight_gradient(normed, upstream, both, hidden):
    count = len(normed)
    units = hidden[0].shape[1]
    tile = 256
    columns = [pl.BlockSpec((a.shape[0], tile), lambda i: (0, i)) for a in normed]
    whole = lambda xs: [pl.BlockSpec(a.shape, lambda i: (0, 0), pipeline_mode=pl.Buffered(1)) for a in xs]
    tokens = sum(a.shape[0] for a in normed)
    return pl.pallas_call(
        functools.partial(weight_gradient_kernel, count),
        grid=(D // tile,),
        in_specs=columns + columns + whole(both) + whole(hidden),
        out_specs=pl.BlockSpec((tile, 3 * units), lambda i: (i, 0)),
        out_shape=jax.ShapeDtypeStruct((D, 3 * units), bf16),
        compiler_params=pltpu.CompilerParams(vmem_limit_bytes=60 << 20),
        cost_estimate=pl.CostEstimate(
            flops=8 * tokens * D * units, bytes_accessed=2 * tokens * (2 * D + 3 * units), transcendentals=0
        ),
        name="weight_gradient",
    )(*normed, *upstream, *both, *hidden)


def coordinates():
    dp = lax.axis_index("dp")
    return dp // CORES, dp % CORES, lax.axis_index("seq")


def device_at(place):
    z, c, s = place
    return z * CORES + c, s


def greet(peers, neighbours):
    barrier = pltpu.get_barrier_semaphore()
    count = len(peers)
    for device in peers:
        pl.semaphore_signal(barrier, inc=1, device_id=device_at(device), device_id_type=MESH)
    for condition, device in neighbours:

        @pl.when(condition)
        def _():
            pl.semaphore_signal(barrier, inc=1, device_id=device_at(device), device_id_type=MESH)

        count = count + condition.astype(jnp.int32)
    pl.semaphore_wait(barrier, count)


def remote(source, target, sems, slot, device):
    send, receive = sems
    return pltpu.make_async_remote_copy(
        src_ref=source,
        dst_ref=target,
        send_sem=send.at[slot],
        recv_sem=receive.at[slot],
        device_id=device_at(device),
        device_id_type=MESH,
    )


def first_gather_kernel(n_z, n_seq, shares, joined, out_rows, block, joined_z, out_z, local, send, receive):
    z, c, s = coordinates()
    plane = CORES * n_seq
    rows = joined.shape[0]
    me = c * n_seq + s
    others = [(z, c ^ (k // n_seq), s ^ (k % n_seq)) for k in range(1, plane)]
    above, below = (z + 1, c, s), (z - 1, c, s)
    greet(others, [(z > 0, below), (z < n_z - 1, above)])
    sems = (send, receive)
    mine = [
        pltpu.make_async_copy(joined, joined_z.at[z], local.at[0]),
        pltpu.make_async_copy(out_rows, out_z.at[z], local.at[1]),
        pltpu.make_async_copy(shares.at[me], block.at[me], local.at[2]),
    ]
    for copy in mine:
        copy.start()
    slot = 0
    chains = []
    for source, target in ((joined, joined_z), (out_rows, out_z)):
        ups, downs = [], []
        for k in range(1, n_z):
            held = source if k == 1 else target.at[z - (k - 1)]
            ups.append(remote(held, target.at[z - (k - 1)], sems, slot, above))
            held = source if k == 1 else target.at[z + (k - 1)]
            downs.append(remote(held, target.at[z + (k - 1)], sems, slot + 1, below))
            slot += 2
        chains.append((ups, downs))
    for ups, downs in chains:
        pl.when(z < n_z - 1)(ups[0].start)
        pl.when(z > 0)(downs[0].start)
    sent = []
    for k, (tz, tc, ts) in enumerate(others):
        copy = remote(shares.at[tc * n_seq + ts], block.at[me], sems, slot + k, (tz, tc, ts))
        copy.start()
        sent.append(copy)
    for k in range(1, n_z):
        for ups, downs in chains:
            pl.when(z >= k)(ups[k - 1].wait_recv)
            pl.when(z + k < n_z)(downs[k - 1].wait_recv)
            if k < n_z - 1:
                pl.when((z >= k) & (z < n_z - 1))(ups[k].start)
                pl.when((z + k < n_z) & (z > 0))(downs[k].start)
    for k in range(1, n_z):
        for ups, downs in chains:
            pl.when((z >= k - 1) & (z < n_z - 1))(ups[k - 1].wait_send)
            pl.when((z + k - 1 < n_z) & (z > 0))(downs[k - 1].wait_send)
    for copy in sent:
        copy.wait()
    for copy in mine:
        copy.wait()


def first_gather(n_z, n_seq, shares, joined, out_rows):
    plane = CORES * n_seq
    rows = joined.shape[0]
    copies = 4 * (n_z - 1) + plane - 1
    shape = lambda *dims: jax.ShapeDtypeStruct(dims, bf16)
    return pl.pallas_call(
        functools.partial(first_gather_kernel, n_z, n_seq),
        in_specs=[VMEM] * 3,
        out_specs=[ANY] * 3,
        out_shape=[
            shape(*shares.shape),
            shape(n_z, rows, joined.shape[1]),
            shape(n_z, rows, out_rows.shape[1]),
        ],
        scratch_shapes=[
            pltpu.SemaphoreType.DMA((3,)),
            pltpu.SemaphoreType.DMA((copies,)),
            pltpu.SemaphoreType.DMA((copies,)),
        ],
        compiler_params=pltpu.CompilerParams(collective_id=0, has_side_effects=True),
        name="first_gather",
    )(shares, joined, out_rows)


def plane_routes(n_seq):
    if n_seq == 4:
        return [(1, 0, 0, 1), (2, 0, 0, 2)], [(3, 1, 1, 2), (4, 2, 2, 1)]
    return [(k, 0, 0, k) for k in range(1, n_seq)], []


def spread_plane_kernel(n_z, n_seq, joined_z, out_z, joined, out_rows, local, send, receive):
    z, c, s = coordinates()
    direct, handed = plane_routes(n_seq)
    count = len(direct) + len(handed) + 1
    core_peer = (z, 1 - c, s)
    greet([(z, c, s ^ k) for k in sorted({r[3] for r in direct + handed})] + [core_peer], [])
    half = n_z // 2
    parts = {0: slice(0, n_z), 1: slice(0, half), 2: slice(half, n_z)}
    plans = []
    own = []
    for index, (source, target) in enumerate(((joined_z, joined), (out_z, out_rows))):
        sems = (send.at[index], receive.at[index])
        at = lambda k, part, target=target: target.at[parts[part], c * n_seq + (s ^ k)]
        own.append(pltpu.make_async_copy(source, at(0, 0), local.at[index]))
        own[-1].start()
        first = [remote(source, at(0, 0), sems, slot, (z, c, s ^ peer)) for slot, _, _, peer in direct]
        second = [remote(at(k, p), at(k, p), sems, slot, (z, c, s ^ peer)) for slot, k, p, peer in handed]
        to_core = [remote(source, at(0, 0), sems, count, core_peer)]
        held = [(k, 0) for k in range(1, n_seq)] if not handed else [(1, 0), (2, 0), (3, 1), (3, 2)]
        to_core += [remote(at(k, p), at(k, p), sems, count + 1 + i, core_peer) for i, (k, p) in enumerate(held)]
        plans.append((first, second, to_core))
    for first, second, to_core in plans:
        for copy in first + to_core[:1]:
            copy.start()
    for first, second, to_core in plans:
        for i, copy in enumerate(first):
            copy.wait_recv()
            if second:
                second[i].start()
            to_core[1 + i].start()
    for first, second, to_core in plans:
        for i, copy in enumerate(second):
            copy.wait_recv()
            to_core[1 + len(first) + i].start()
    for first, second, to_core in plans:
        for copy in first + second:
            copy.wait_send()
        for copy in to_core:
            copy.wait()
    for copy in own:
        copy.wait()


def spread_plane(n_z, n_seq, joined_z, out_z):
    rows = joined_z.shape[1]
    direct, handed = plane_routes(n_seq)
    slots = 2 * (len(direct) + len(handed)) + 3
    shape = lambda a: jax.ShapeDtypeStruct((n_z, CORES * n_seq, rows, a.shape[2]), bf16)
    return pl.pallas_call(
        functools.partial(spread_plane_kernel, n_z, n_seq),
        in_specs=[VMEM] * 2,
        out_specs=[ANY] * 2,
        out_shape=[shape(joined_z), shape(out_z)],
        scratch_shapes=[
            pltpu.SemaphoreType.DMA((2,)),
            pltpu.SemaphoreType.DMA((2, slots)),
            pltpu.SemaphoreType.DMA((2, slots)),
        ],
        compiler_params=pltpu.CompilerParams(collective_id=1, has_side_effects=True),
        name="spread_plane",
    )(joined_z, out_z)


class Links:
    def __init__(self, n_dp, n_seq):
        self.n_z = n_dp // CORES
        self.n_seq = n_seq
        self.plane = CORES * n_seq

    def place(self):
        return coordinates()

    def send(self, values, pairs_of):
        pairs = []
        for z in range(self.n_z):
            for c in range(CORES):
                for s in range(self.n_seq):
                    to = pairs_of(z, c, s)
                    if to is not None:
                        tz, tc, ts = to
                        pairs.append((((z * CORES + c) * self.n_seq + s), (tz * CORES + tc) * self.n_seq + ts))
        return lax.ppermute(values, AXES, pairs)

    def core(self, values):
        return self.send(values, lambda z, c, s: (z, 1 - c, s))

    def peer(self, values, k):
        return self.send(values, lambda z, c, s: (z, c, s ^ k))

    def up(self, values, first, last):
        return self.send(values, lambda z, c, s: (z + 1, c, s) if first <= z <= last else None)

    def down(self, values, first, last):
        return self.send(values, lambda z, c, s: (z - 1, c, s) if first <= z <= last else None)

    def seq_gather(self, values):
        if self.n_seq != 4:
            return [[values]] + [[self.peer(values, k)] for k in range(1, self.n_seq)]
        half = values.shape[0] // 2
        one, two = self.peer(values, 1), self.peer(values, 2)
        top = self.peer(one[:half], 2)
        bottom = self.peer(two[half:], 1)
        return [[values], [one], [two], [top, bottom]]

    def seq_scatter(self, parts, add):
        if self.n_seq != 4:
            return add([parts[0]] + [self.peer(parts[k], k) for k in range(1, self.n_seq)])
        half = parts[0].shape[0] // 2
        top = self.peer(parts[3][:half], 1)
        bottom = self.peer(parts[3][half:], 2)
        two = [self.peer(add([parts[2][:half], top]), 2), self.peer(parts[2][half:], 2)]
        one = [self.peer(parts[1][:half], 1), self.peer(add([parts[1][half:], bottom]), 1)]
        return [add([parts[0][:half], two[0], one[0]]), add([parts[0][half:], two[1], one[1]])]

    def line_gather(self, values):
        n = self.n_z
        z, _, _ = self.place()
        rows = values.shape[0]
        ups, downs = [values], [values]
        for k in range(1, n):
            ups.append(self.up(ups[-1], k - 1, n - 2))
            downs.append(self.down(downs[-1], 1, n - k))
        full = lax.dynamic_update_slice_in_dim(jnp.zeros((n * rows, values.shape[1]), values.dtype), values, z * rows, 0)
        for r in range(1, n):
            piece = jnp.where(z + r < n, downs[r], ups[n - r])
            full = lax.dynamic_update_slice_in_dim(full, piece, ((z + r) % n) * rows, 0)
        return full

    def line_scatter(self, full, add):
        n = self.n_z
        z, _, _ = self.place()
        rows = full.shape[0] // n
        take = lambda d: lax.dynamic_slice_in_dim(full, jnp.clip(d, 0, n - 1) * rows, rows, 0)
        above = below = None
        for k in range(1, n):
            one, two = take(z + n - k), take(z - n + k)
            one = one if above is None else add([one, above])
            two = two if below is None else add([two, below])
            above = self.up(one, 0, k - 1)
            below = self.down(two, n - k, n - 1)
        return [take(z)] + ([above, below] if n > 1 else [])


def add_low(parts):
    return functools.reduce(lambda a, b: a + b, [p.astype(f32) for p in parts]).astype(bf16)


def add_wide(parts):
    return functools.reduce(lambda a, b: a + b, [p.astype(f32) for p in parts])


def body(
    n_dp,
    n_seq,
    tokens,
    joined_weight,
    output_weight,
    expand_weight,
    shrink_weight,
    norm_gains,
    doc_lengths,
    cotangent,
):
    links = Links(n_dp, n_seq)
    n_z, plane = links.n_z, links.plane
    z, core, seq = links.place()
    me = core * n_seq + seq
    devices = n_dp * n_seq
    local_len = tokens.shape[1]
    rows = D // devices
    units = FF // plane
    own_gains = GAINS // devices
    offset = seq * local_len

    kv_columns = joined_weight[:, Q_WIDTH:].reshape(rows, 2, KV_HEADS, HEAD_DIM).transpose(0, 2, 1, 3)
    gain_block = jnp.pad(norm_gains, (0, rows * PAIR - own_gains)).reshape(rows, PAIR)
    joined_block = jnp.concatenate(
        [joined_weight[:, :Q_WIDTH], kv_columns.reshape(rows, 2 * KV_WIDTH), gain_block], axis=1
    )
    shrink_rows = shrink_weight.T
    shares = jnp.concatenate(
        [expand_weight.reshape(rows, 2, plane, units), shrink_rows.reshape(rows, 1, plane, units)], axis=1
    )
    shares = shares.transpose(2, 0, 1, 3).reshape(plane, rows, 3 * units)
    block, joined_z, output_z = first_gather(n_z, n_seq, shares, joined_block, output_weight.T)
    lines = [[a * CORES + c for a in range(n_z)] for c in range(CORES)]
    weights = lax.all_gather(
        block.reshape(plane * rows, 3 * units), "dp", axis=0, tiled=True, axis_index_groups=lines
    )
    joined_all, output_all = spread_plane(n_z, n_seq, joined_z, output_z)
    joined_all = joined_all.reshape(D, QKV + PAIR)
    output_all = output_all.reshape(D, Q_WIDTH)
    gains = joined_all[:, QKV:].reshape(devices, rows * PAIR)[:, :own_gains].reshape(GAINS).astype(f32)
    joined_all = joined_all[:, :QKV]
    gain_one = gains[:D]
    gain_query = gains[D : D + HEAD_DIM]
    gain_key = gains[D + HEAD_DIM : D + PAIR]
    gain_two = gains[D + PAIR :]
    head_gains = jnp.stack([jnp.tile(gain_query, 2), jnp.tile(gain_key, 2)])

    half = HEAD_DIM // 2
    frequency = 10000.0 ** (-jnp.arange(half, dtype=f32) / half)
    angles = (offset + jnp.arange(local_len, dtype=jnp.int32)).astype(f32)[:, None] * frequency[None, :]
    cosine, sine = jnp.cos(angles), jnp.sin(angles)
    tables = jnp.stack(
        [jnp.concatenate([cosine] * 4, axis=1), jnp.concatenate([-sine, sine, -sine, sine], axis=1)]
    )
    places = jnp.arange(ROW_LEN, dtype=jnp.int32)
    docs = jnp.zeros((ROW_LEN,), jnp.int32)
    bound = 0
    for index in range(doc_lengths.shape[1] - 1):
        bound = bound + doc_lengths[0, index]
        docs = docs + (places >= bound).astype(jnp.int32)
    mark = jnp.arange(PAIR, dtype=jnp.int32)[None] - HEAD_DIM
    same = (mark >= 0) & (mark < MARK) & (mark == docs[:, None])
    other = (mark >= 0) & (mark < MARK) & (mark != docs[:, None])
    carries = (mark >= MARK) & (mark < MARK + 3)
    key_marks = jnp.where(other, -1024.0, jnp.where(carries, 1.0, 0.0)).astype(bf16)
    query_marks = lax.dynamic_slice_in_dim(same.astype(bf16), offset, local_len, 0)
    offset_array = jnp.reshape(offset, (1,)).astype(jnp.int32)

    flat = tokens.reshape(local_len, D).astype(f32)
    scale_one = rms_scale(flat)
    normed_low = (flat * scale_one * gain_one).astype(bf16)
    projected = dot(normed_low, joined_all, NN)
    turned = rope(projected, head_gains, tables)
    own_kv = turned[:, Q_WIDTH:]
    kv = jnp.zeros((ROW_LEN, 2 * KV_WIDTH), bf16)
    for k, parts in enumerate(links.seq_gather(own_kv)):
        start = (seq ^ k) * local_len
        for part in parts:
            kv = lax.dynamic_update_slice_in_dim(kv, part, start, 0)
            start = start + part.shape[0]
    attended, q_marked = attend(offset_array, turned, kv, key_marks, query_marks)
    attended_low = attended.astype(bf16)
    residual = flat + dot(attended_low, output_all, NT)
    scale_two = rms_scale(residual)
    normed_two = (residual * scale_two * gain_two).astype(bf16)

    def plane_gather(values):
        groups = []
        for parts in links.seq_gather(values):
            parts = parts + [links.core(p) for p in parts]
            groups.append(jnp.concatenate(parts, axis=0))
        return groups

    upstream_low = cotangent.reshape(local_len, D)
    upstream_all = plane_gather(upstream_low)
    normed_all = plane_gather(normed_two)
    hidden_all, both_all, result_parts, back_parts = [], [], [], []
    for values, above in zip(normed_all, upstream_all):
        hidden, both, result, back = feed(values, above, weights)
        hidden_all.append(hidden)
        both_all.append(both)
        result_parts.append(result)
        back_parts.append(back)

    def plane_scatter(parts):
        parts = [add_low([p[:local_len], links.core(p[local_len:])]) for p in parts]
        out = links.seq_scatter(parts, add_low)
        return jnp.concatenate(out, axis=0) if isinstance(out, list) else out

    grad_normed_two = plane_scatter(back_parts).astype(f32)
    share_gradient = weight_gradient(normed_all, upstream_all, both_all, hidden_all)
    feed_result = plane_scatter(result_parts).astype(f32)
    layer_output = (residual + feed_result).astype(bf16)

    mine = lax.psum_scatter(
        share_gradient, "dp", scatter_dimension=0, tiled=True, axis_index_groups=lines
    )
    expand_gradient = jnp.zeros((rows, 2 * FF), f32)
    shrink_gradient = jnp.zeros((rows, FF), f32)
    for k in range(plane):
        p = (core ^ (k // n_seq)) * n_seq + (seq ^ (k % n_seq))
        piece = lax.dynamic_slice_in_dim(mine, p * rows, rows, 0)
        if k:
            piece = links.send(piece, lambda a, c, s: (a, c ^ (k // n_seq), s ^ (k % n_seq)))
        piece = piece.astype(f32)
        put = lambda a, part, start: lax.dynamic_update_slice_in_dim(a, part, start + p * units, 1)
        expand_gradient = put(expand_gradient, piece[:, :units], 0)
        expand_gradient = put(expand_gradient, piece[:, units : 2 * units], FF)
        shrink_gradient = put(shrink_gradient, piece[:, 2 * units :], 0)
    shrink_gradient = shrink_gradient.T

    upstream = upstream_low.astype(f32)
    gain_two_grad = jnp.sum(grad_normed_two * residual * scale_two, axis=0)
    grad_residual = upstream + norm_back(grad_normed_two, residual, scale_two, gain_two)
    grad_attn_low = grad_residual.astype(bf16)
    output_term = dot(grad_attn_low, attended_low, TN).astype(bf16)
    grad_out_low = dot(grad_attn_low, output_all, NN).astype(bf16)
    grad_query, grad_kv_all = attend_back(offset_array, q_marked, grad_out_low, attended, kv, key_marks)
    kv_parts = [lax.dynamic_slice_in_dim(grad_kv_all, (seq ^ k) * local_len, local_len, 0) for k in range(n_seq)]
    grad_kv = links.seq_scatter(kv_parts, add_wide if n_seq != 4 else add_low)
    grad_kv = jnp.concatenate(grad_kv, axis=0) if isinstance(grad_kv, list) else grad_kv
    grad_projected, head_gain_sums = rope_back(grad_query, grad_kv.astype(f32), projected, head_gains, tables)
    joined_term = dot(normed_low, grad_projected, TN).astype(bf16)
    grad_normed = dot(grad_projected, joined_all, NT)
    gain_one_grad = jnp.sum(grad_normed * flat * scale_one, axis=0)
    token_gradient = grad_residual + norm_back(grad_normed, flat, scale_one, gain_one)
    gain_query_grad = head_gain_sums[0, :HEAD_DIM] + head_gain_sums[0, HEAD_DIM:]
    gain_key_grad = head_gain_sums[1, :HEAD_DIM]
    gain_grads = jnp.concatenate([gain_one_grad, gain_query_grad, gain_key_grad, gain_two_grad])
    gain_block = jnp.pad(gain_grads.reshape(devices, own_gains), ((0, 0), (0, rows * PAIR - own_gains)))
    gain_block = gain_block.reshape(devices * rows, PAIR).astype(bf16)

    def scatter_all(full):
        width = full.shape[1]
        full = full.reshape(n_z, CORES, n_seq, rows, width)
        other = links.core(lax.dynamic_index_in_dim(full, 1 - core, 1, keepdims=False))
        full = add_low([lax.dynamic_index_in_dim(full, core, 1, keepdims=False), other])
        full = full.transpose(1, 0, 2, 3).reshape(n_seq, n_z * rows, width)
        parts = [lax.dynamic_index_in_dim(full, seq ^ k, 0, keepdims=False) for k in range(n_seq)]
        out = links.seq_scatter(parts, add_low)
        out = jnp.concatenate(out, axis=0) if isinstance(out, list) else out
        return add_wide(links.line_scatter(out, add_low))

    output_gradient = scatter_all(output_term).T
    joined_sum = scatter_all(jnp.concatenate([joined_term, gain_block], axis=1))
    kv_sum = joined_sum[:, Q_WIDTH:QKV].reshape(rows, KV_HEADS, 2, HEAD_DIM).transpose(0, 2, 1, 3)
    joined_gradient = jnp.concatenate([joined_sum[:, :Q_WIDTH], kv_sum.reshape(rows, 2 * KV_WIDTH)], axis=1)
    gains_gradient = joined_sum[:, QKV:].reshape(rows * PAIR)[:own_gains]
    return (
        layer_output.reshape(1, local_len, D),
        token_gradient.astype(bf16).reshape(1, local_len, D),
        joined_gradient,
        output_gradient,
        expand_gradient,
        shrink_gradient,
        gains_gradient,
    )


def solution(mesh):
    token_spec, row_spec, column_spec = P("dp", "seq", None), P(AXES, None), P(None, AXES)
    return jax.shard_map(
        functools.partial(body, mesh.shape["dp"], mesh.shape["seq"]),
        mesh=mesh,
        in_specs=(
            token_spec,
            row_spec,
            column_spec,
            row_spec,
            column_spec,
            P(AXES),
            P("dp", None),
            token_spec,
        ),
        out_specs=(token_spec, token_spec, row_spec, column_spec, row_spec, column_spec, P(AXES)),
        check_vma=False,
    )
```

```python
import functools

import jax
import jax.numpy as jnp
from jax import lax
from jax.experimental import pallas as pl
from jax.experimental.pallas import tpu as pltpu
from jax.sharding import PartitionSpec as P

D = 2048
HEADS = 20
KV_HEADS = 5
HEAD_DIM = 64
FF = 6144
ROW_LEN = 2048
GAINS = 4224
PAIR = 2 * HEAD_DIM
Q_WIDTH = HEADS * HEAD_DIM
KV_WIDTH = KV_HEADS * HEAD_DIM
QKV = Q_WIDTH + 2 * KV_WIDTH
CORES = 2

epsilon = 1e-05
f32 = jnp.float32
bf16 = jnp.bfloat16
AXES = ("dp", "seq")
MESH = pl.DeviceIdType.MESH
ANY = pl.BlockSpec(memory_space=pl.ANY)
VMEM = pl.BlockSpec(memory_space=pltpu.VMEM)
NN = (((1,), (0,)), ((), ()))
NT = (((1,), (1,)), ((), ()))
TN = (((0,), (0,)), ((), ()))


def dot(left, right, dims):
    return lax.dot_general(left, right, dims, preferred_element_type=f32)


def rms_scale(values):
    return lax.rsqrt(jnp.mean(values * values, axis=-1, keepdims=True) + epsilon)


def norm_back(upstream, values, scaling, gain_vector):
    weighted = upstream * gain_vector
    average = jnp.mean(weighted * values, axis=-1, keepdims=True)
    return scaling * weighted - values * (scaling * scaling * scaling) * average


def lanes(shape):
    return lax.broadcasted_iota(jnp.int32, shape, len(shape) - 1)


def swap_halves(values):
    half = HEAD_DIM // 2
    first = lanes(values.shape) % HEAD_DIM < half
    return jnp.where(first, pltpu.roll(values, PAIR - half, axis=1), pltpu.roll(values, half, axis=1))


def head_means(values):
    low = lanes(values.shape) < HEAD_DIM
    left = jnp.sum(jnp.where(low, values, 0.0), axis=-1, keepdims=True)
    right = jnp.sum(jnp.where(low, 0.0, values), axis=-1, keepdims=True)
    return jnp.where(low, left, right) * (1.0 / HEAD_DIM)


BAND = 2 * KV_WIDTH
QUERY_BANDS = Q_WIDTH // BAND


def rope_kernel(projected, gains, tables, out):
    is_query = pl.program_id(0) < QUERY_BANDS
    gain = jnp.where(is_query, gains[0:1] * HEAD_DIM**-0.5, gains[1:2])
    direct, crossed = tables[0] * gain, tables[1]
    for start in range(0, BAND, PAIR):
        columns = slice(start, start + PAIR)
        values = projected[:, columns]
        scaling = lax.rsqrt(head_means(values * values) + epsilon)
        turned = values * direct + swap_halves(values * gain) * crossed
        plain = (lanes(values.shape) >= HEAD_DIM) & jnp.logical_not(is_query)
        out[:, columns] = jnp.where(plain, values, turned * scaling).astype(bf16)


def rope(projected, gains, tables):
    tokens, width = projected.shape
    return pl.pallas_call(
        rope_kernel,
        grid=(width // BAND,),
        in_specs=[
            pl.BlockSpec((tokens, BAND), lambda i: (0, i)),
            pl.BlockSpec((2, PAIR), lambda i: (0, 0)),
            pl.BlockSpec((2, tokens, PAIR), lambda i: (0, 0, 0)),
        ],
        out_specs=pl.BlockSpec((tokens, BAND), lambda i: (0, i)),
        out_shape=jax.ShapeDtypeStruct((tokens, width), bf16),
        compiler_params=pltpu.CompilerParams(vmem_limit_bytes=40 << 20),
        cost_estimate=pl.CostEstimate(flops=40 * tokens * width, bytes_accessed=6 * tokens * width, transcendentals=0),
        name="rope",
    )(projected, gains, tables)


def rope_back_kernel(dq, dkv, projected, gains, tables, out, gain_sums):
    step = pl.program_id(0)
    is_query = step < QUERY_BANDS
    gain = jnp.where(is_query, gains[0:1], gains[1:2])
    sums = jnp.zeros((1, PAIR), f32)
    for start in range(0, BAND, PAIR):
        columns = slice(start, start + PAIR)
        values = projected[:, columns]
        upstream = jnp.where(is_query, dq[:, columns] * HEAD_DIM**-0.5, dkv[:, columns].astype(f32))
        plain = (lanes(values.shape) >= HEAD_DIM) & jnp.logical_not(is_query)
        turned = upstream * tables[0] + swap_halves(upstream * tables[1])
        scaling = lax.rsqrt(head_means(values * values) + epsilon)
        unit = values * scaling
        weighted = turned * gain
        back = scaling * (weighted - unit * head_means(weighted * unit))
        out[:, columns] = jnp.where(plain, upstream, back).astype(bf16)
        sums = sums + jnp.sum(jnp.where(plain, 0.0, turned * unit), axis=0, keepdims=True)

    @pl.when(step == 0)
    def _():
        gain_sums[...] = jnp.zeros_like(gain_sums)

    row = lax.broadcasted_iota(jnp.int32, gain_sums.shape, 0)
    gain_sums[...] += jnp.where(row == jnp.where(is_query, 0, 1), sums, 0.0)


def rope_back(dq, dkv, projected, gains, tables):
    tokens, width = projected.shape
    return pl.pallas_call(
        rope_back_kernel,
        grid=(width // BAND,),
        in_specs=[
            pl.BlockSpec((tokens, BAND), lambda i: (0, jnp.minimum(i, QUERY_BANDS - 1))),
            pl.BlockSpec((tokens, BAND), lambda i: (0, 0)),
            pl.BlockSpec((tokens, BAND), lambda i: (0, i)),
            pl.BlockSpec((2, PAIR), lambda i: (0, 0)),
            pl.BlockSpec((2, tokens, PAIR), lambda i: (0, 0, 0)),
        ],
        out_specs=[
            pl.BlockSpec((tokens, BAND), lambda i: (0, i)),
            pl.BlockSpec((8, PAIR), lambda i: (0, 0)),
        ],
        out_shape=[
            jax.ShapeDtypeStruct((tokens, width), bf16),
            jax.ShapeDtypeStruct((8, PAIR), f32),
        ],
        compiler_params=pltpu.CompilerParams(vmem_limit_bytes=40 << 20),
        cost_estimate=pl.CostEstimate(flops=60 * tokens * width, bytes_accessed=10 * tokens * width, transcendentals=0),
        name="rope_back",
    )(dq, dkv, projected, gains, tables)


def three_parts(values):
    first = values.astype(bf16).astype(f32)
    second = (values - first).astype(bf16).astype(f32)
    return first, second, values - first - second


def spread_kv(kv, key_marks, keys, vals):
    both = kv[...]
    lane = lanes(both.shape)
    keys[...] = jnp.where(lane < HEAD_DIM, both, key_marks[...])
    vals[...] = jnp.where(lane < HEAD_DIM, jnp.where(lane < 3, 1.0, 0.0).astype(bf16), both)


MARK = 8


def attend_kernel(tq, tk, offset, q, kv, key_marks, query_marks, out, q_marked, keys, vals, rows):
    local_len = q.shape[0]
    group = q.shape[1] // HEAD_DIM
    spread_kv(kv, key_marks, keys, vals)
    lane1 = lanes((tq, PAIR))
    for tile in range(local_len // tq):
        part = slice(tile * tq, (tile + 1) * tq)
        for head in range(group):
            wide = q[part, (head // 2) * PAIR : (head // 2 + 1) * PAIR].astype(f32)
            if head % 2:
                wide = pltpu.roll(wide, HEAD_DIM, axis=1)
            marked = jnp.where(lane1 < HEAD_DIM, wide, query_marks[part].astype(f32))
            rows[head * tq : (head + 1) * tq] = marked.astype(bf16)
        first = offset[0] + tile * tq

        def block(index, total, masked):
            span = pl.ds(pl.multiple_of(index * tk, tk), tk)
            expo = jnp.exp(dot(rows[...], keys[span], NT))
            if masked:
                query_pos = first + lax.broadcasted_iota(jnp.int32, (tq, tk), 0)
                key_pos = index * tk + lax.broadcasted_iota(jnp.int32, (tq, tk), 1)
                expo = jnp.where((key_pos <= query_pos)[None], expo.reshape(group, tq, tk), 0.0)
                expo = expo.reshape(group * tq, tk)
            return total + dot(expo.astype(bf16), vals[span], NN)

        full = first // tk
        end = (first + tq + tk - 1) // tk
        total = jnp.zeros((group * tq, PAIR), f32)
        total = lax.fori_loop(0, full, lambda i, t: block(i, t, False), total)
        total = lax.fori_loop(full, end, lambda i, t: block(i, t, True), total)
        denominator = total[:, 0:1]
        mixed = total / denominator
        one, two, three = three_parts(-jnp.log(denominator))
        lane = lanes(total.shape) - HEAD_DIM - MARK
        kept = rows[...].astype(f32)
        kept = jnp.where(lane == 0, one, jnp.where(lane == 1, two, jnp.where(lane == 2, three, kept)))
        kept = kept.astype(bf16)
        for head in range(group):
            q_marked[head, part] = kept[head * tq : (head + 1) * tq]
        for head in range(0, group, 2):
            even = pltpu.roll(mixed[head * tq : (head + 1) * tq], HEAD_DIM, axis=1)
            odd = mixed[(head + 1) * tq : (head + 2) * tq]
            out[part, (head // 2) * PAIR : (head // 2 + 1) * PAIR] = jnp.where(lane1 < HEAD_DIM, even, odd)


def attention_cost(tokens, products):
    pairs = HEADS * tokens * ROW_LEN
    return pl.CostEstimate(flops=products * 2 * 4 * HEAD_DIM * pairs, bytes_accessed=1 << 24, transcendentals=pairs)


def attend(offset, q, kv, key_marks, query_marks):
    tokens = q.shape[0]
    keys = kv.shape[0]
    group = HEADS // KV_HEADS
    width = group * HEAD_DIM
    tq, tk = tokens, min(512, keys)
    spec = pltpu.PrefetchScalarGridSpec(
        num_scalar_prefetch=1,
        grid=(KV_HEADS,),
        in_specs=[
            pl.BlockSpec((tokens, width), lambda g, _: (0, g)),
            pl.BlockSpec((keys, PAIR), lambda g, _: (0, g)),
            pl.BlockSpec((keys, PAIR), lambda g, _: (0, 0)),
            pl.BlockSpec((tokens, PAIR), lambda g, _: (0, 0)),
        ],
        out_specs=[
            pl.BlockSpec((tokens, width), lambda g, _: (0, g)),
            pl.BlockSpec((group, tokens, PAIR), lambda g, _: (g, 0, 0)),
        ],
        scratch_shapes=[
            pltpu.VMEM((keys, PAIR), bf16),
            pltpu.VMEM((keys, PAIR), bf16),
            pltpu.VMEM((group * tq, PAIR), bf16),
        ],
    )
    return pl.pallas_call(
        functools.partial(attend_kernel, tq, tk),
        grid_spec=spec,
        out_shape=[
            jax.ShapeDtypeStruct((tokens, Q_WIDTH), f32),
            jax.ShapeDtypeStruct((HEADS, tokens, PAIR), bf16),
        ],
        compiler_params=pltpu.CompilerParams(vmem_limit_bytes=56 << 20),
        cost_estimate=attention_cost(tokens, 2),
        name="attend",
    )(offset, q, kv, key_marks, query_marks)


def attend_back_kernel(
    tq, tk, offset, q_marked, d_out, out, kv, key_marks, dq, dkv, keys, vals, d_rows, rows, dk_sum, dv_sum
):
    local_len = d_out.shape[0]
    group = d_out.shape[1] // HEAD_DIM
    spread_kv(kv, key_marks, keys, vals)
    dk_sum[...] = jnp.zeros_like(dk_sum)
    dv_sum[...] = jnp.zeros_like(dv_sum)
    lane1 = lanes((tq, PAIR))
    for tile in range(local_len // tq):
        part = slice(tile * tq, (tile + 1) * tq)
        for head in range(group):
            pair = slice((head // 2) * PAIR, (head // 2 + 1) * PAIR)
            wide = d_out[part, pair].astype(f32)
            mine = (lane1 < HEAD_DIM) if head % 2 == 0 else (lane1 >= HEAD_DIM)
            delta = jnp.sum(jnp.where(mine, wide * out[part, pair], 0.0), axis=1, keepdims=True)
            one, two, three = three_parts(-delta)
            if head % 2 == 0:
                wide = pltpu.roll(wide, HEAD_DIM, axis=1)
            marks = jnp.where(lane1 == 0, one, jnp.where(lane1 == 1, two, jnp.where(lane1 == 2, three, 0.0)))
            d_rows[head * tq : (head + 1) * tq] = jnp.where(lane1 < HEAD_DIM, marks, wide).astype(bf16)
            rows[head * tq : (head + 1) * tq] = q_marked[head, part]
        first = offset[0] + tile * tq

        def block(index, total, masked):
            span = pl.ds(pl.multiple_of(index * tk, tk), tk)
            prob = jnp.exp(dot(keys[span], rows[...], NT))
            if masked:
                key_pos = index * tk + lax.broadcasted_iota(jnp.int32, (tk, tq), 0)
                query_pos = first + lax.broadcasted_iota(jnp.int32, (tk, tq), 1)
                prob = jnp.where(jnp.concatenate([key_pos <= query_pos] * group, axis=1), prob, 0.0)
            d_scores = (prob * dot(vals[span], d_rows[...], NT)).astype(bf16)
            dv_sum[span] += dot(prob.astype(bf16), d_rows[...], NN)
            dk_sum[span] += dot(d_scores, rows[...], NN)
            return total + dot(d_scores, keys[span], TN)

        full = first // tk
        end = (first + tq + tk - 1) // tk
        total = jnp.zeros((group * tq, PAIR), f32)
        total = lax.fori_loop(0, full, lambda i, t: block(i, t, False), total)
        total = lax.fori_loop(full, end, lambda i, t: block(i, t, True), total)
        for head in range(0, group, 2):
            even = total[head * tq : (head + 1) * tq]
            odd = pltpu.roll(total[(head + 1) * tq : (head + 2) * tq], HEAD_DIM, axis=1)
            dq[part, (head // 2) * PAIR : (head // 2 + 1) * PAIR] = jnp.where(lane1 < HEAD_DIM, even, odd)
    dkv[...] = jnp.where(lanes(dk_sum.shape) < HEAD_DIM, dk_sum[...], dv_sum[...]).astype(bf16)


def attend_back(offset, q_marked, d_out, out, kv, key_marks):
    tokens = d_out.shape[0]
    keys = kv.shape[0]
    group = HEADS // KV_HEADS
    width = group * HEAD_DIM
    tq, tk = tokens, min(512, keys)
    spec = pltpu.PrefetchScalarGridSpec(
        num_scalar_prefetch=1,
        grid=(KV_HEADS,),
        in_specs=[
            pl.BlockSpec((group, tokens, PAIR), lambda g, _: (g, 0, 0)),
            pl.BlockSpec((tokens, width), lambda g, _: (0, g)),
            pl.BlockSpec((tokens, width), lambda g, _: (0, g)),
            pl.BlockSpec((keys, PAIR), lambda g, _: (0, g)),
            pl.BlockSpec((keys, PAIR), lambda g, _: (0, 0)),
        ],
        out_specs=[
            pl.BlockSpec((tokens, width), lambda g, _: (0, g)),
            pl.BlockSpec((keys, PAIR), lambda g, _: (0, g)),
        ],
        scratch_shapes=[
            pltpu.VMEM((keys, PAIR), bf16),
            pltpu.VMEM((keys, PAIR), bf16),
            pltpu.VMEM((group * tq, PAIR), bf16),
            pltpu.VMEM((group * tq, PAIR), bf16),
            pltpu.VMEM((keys, PAIR), f32),
            pltpu.VMEM((keys, PAIR), f32),
        ],
    )
    return pl.pallas_call(
        functools.partial(attend_back_kernel, tq, tk),
        grid_spec=spec,
        out_shape=[
            jax.ShapeDtypeStruct((tokens, Q_WIDTH), f32),
            jax.ShapeDtypeStruct(kv.shape, bf16),
        ],
        compiler_params=pltpu.CompilerParams(vmem_limit_bytes=56 << 20),
        cost_estimate=attention_cost(tokens, 4),
        name="attend_back",
    )(offset, q_marked, d_out, out, kv, key_marks)


def coordinates():
    dp = lax.axis_index("dp")
    return dp // CORES, dp % CORES, lax.axis_index("seq")


def device_at(place):
    z, c, s = place
    return z * CORES + c, s


def greet(peers, neighbours):
    barrier = pltpu.get_barrier_semaphore()
    count = len(peers)
    for device in peers:
        pl.semaphore_signal(barrier, inc=1, device_id=device_at(device), device_id_type=MESH)
    for condition, device in neighbours:

        @pl.when(condition)
        def _():
            pl.semaphore_signal(barrier, inc=1, device_id=device_at(device), device_id_type=MESH)

        count = count + condition.astype(jnp.int32)
    pl.semaphore_wait(barrier, count)


def remote(source, target, sems, slot, device):
    send, receive = sems
    return pltpu.make_async_remote_copy(
        src_ref=source,
        dst_ref=target,
        send_sem=send.at[slot],
        recv_sem=receive.at[slot],
        device_id=device_at(device),
        device_id_type=MESH,
    )


def first_gather_kernel(n_z, n_seq, shares, joined, out_rows, block, joined_z, out_z, local, send, receive):
    z, c, s = coordinates()
    plane = CORES * n_seq
    rows = joined.shape[0]
    me = c * n_seq + s
    others = [(z, c ^ (k // n_seq), s ^ (k % n_seq)) for k in range(1, plane)]
    above, below = (z + 1, c, s), (z - 1, c, s)
    greet(others, [(z > 0, below), (z < n_z - 1, above)])
    sems = (send, receive)
    mine = [
        pltpu.make_async_copy(joined, joined_z.at[z], local.at[0]),
        pltpu.make_async_copy(out_rows, out_z.at[z], local.at[1]),
        pltpu.make_async_copy(shares.at[me], block.at[me], local.at[2]),
    ]
    for copy in mine:
        copy.start()
    slot = 0
    chains = []
    for source, target in ((joined, joined_z), (out_rows, out_z)):
        ups, downs = [], []
        for k in range(1, n_z):
            held = source if k == 1 else target.at[z - (k - 1)]
            ups.append(remote(held, target.at[z - (k - 1)], sems, slot, above))
            held = source if k == 1 else target.at[z + (k - 1)]
            downs.append(remote(held, target.at[z + (k - 1)], sems, slot + 1, below))
            slot += 2
        chains.append((ups, downs))
    for ups, downs in chains:
        pl.when(z < n_z - 1)(ups[0].start)
        pl.when(z > 0)(downs[0].start)
    sent = []
    for k, (tz, tc, ts) in enumerate(others):
        copy = remote(shares.at[tc * n_seq + ts], block.at[me], sems, slot + k, (tz, tc, ts))
        copy.start()
        sent.append(copy)
    for k in range(1, n_z):
        for ups, downs in chains:
            pl.when(z >= k)(ups[k - 1].wait_recv)
            pl.when(z + k < n_z)(downs[k - 1].wait_recv)
            if k < n_z - 1:
                pl.when((z >= k) & (z < n_z - 1))(ups[k].start)
                pl.when((z + k < n_z) & (z > 0))(downs[k].start)
    for k in range(1, n_z):
        for ups, downs in chains:
            pl.when((z >= k - 1) & (z < n_z - 1))(ups[k - 1].wait_send)
            pl.when((z + k - 1 < n_z) & (z > 0))(downs[k - 1].wait_send)
    for copy in sent:
        copy.wait()
    for copy in mine:
        copy.wait()


def first_gather(n_z, n_seq, shares, joined, out_rows):
    plane = CORES * n_seq
    rows = joined.shape[0]
    copies = 4 * (n_z - 1) + plane - 1
    shape = lambda *dims: jax.ShapeDtypeStruct(dims, bf16)
    return pl.pallas_call(
        functools.partial(first_gather_kernel, n_z, n_seq),
        in_specs=[VMEM] * 3,
        out_specs=[ANY] * 3,
        out_shape=[
            shape(*shares.shape),
            shape(n_z, rows, joined.shape[1]),
            shape(n_z, rows, out_rows.shape[1]),
        ],
        scratch_shapes=[
            pltpu.SemaphoreType.DMA((3,)),
            pltpu.SemaphoreType.DMA((copies,)),
            pltpu.SemaphoreType.DMA((copies,)),
        ],
        compiler_params=pltpu.CompilerParams(collective_id=0, has_side_effects=True),
        name="first_gather",
    )(shares, joined, out_rows)


def plane_routes(n_seq):
    if n_seq == 4:
        return [(1, 0, 0, 1), (2, 0, 0, 2)], [(3, 1, 1, 2), (4, 2, 2, 1)]
    return [(k, 0, 0, k) for k in range(1, n_seq)], []


def spread_plane_kernel(n_z, n_seq, joined_z, out_z, joined, out_rows, local, send, receive):
    z, c, s = coordinates()
    direct, handed = plane_routes(n_seq)
    count = len(direct) + len(handed) + 1
    core_peer = (z, 1 - c, s)
    greet([(z, c, s ^ k) for k in sorted({r[3] for r in direct + handed})] + [core_peer], [])
    half = n_z // 2
    parts = {0: slice(0, n_z), 1: slice(0, half), 2: slice(half, n_z)}
    plans = []
    own = []
    for index, (source, target) in enumerate(((joined_z, joined), (out_z, out_rows))):
        sems = (send.at[index], receive.at[index])
        at = lambda k, part, target=target: target.at[parts[part], c * n_seq + (s ^ k)]
        own.append(pltpu.make_async_copy(source, at(0, 0), local.at[index]))
        own[-1].start()
        first = [remote(source, at(0, 0), sems, slot, (z, c, s ^ peer)) for slot, _, _, peer in direct]
        second = [remote(at(k, p), at(k, p), sems, slot, (z, c, s ^ peer)) for slot, k, p, peer in handed]
        to_core = [remote(source, at(0, 0), sems, count, core_peer)]
        held = [(k, 0) for k in range(1, n_seq)] if not handed else [(1, 0), (2, 0), (3, 1), (3, 2)]
        to_core += [remote(at(k, p), at(k, p), sems, count + 1 + i, core_peer) for i, (k, p) in enumerate(held)]
        plans.append((first, second, to_core))
    for first, second, to_core in plans:
        for copy in first + to_core[:1]:
            copy.start()
    for first, second, to_core in plans:
        for i, copy in enumerate(first):
            copy.wait_recv()
            if second:
                second[i].start()
            to_core[1 + i].start()
    for first, second, to_core in plans:
        for i, copy in enumerate(second):
            copy.wait_recv()
            to_core[1 + len(first) + i].start()
    for first, second, to_core in plans:
        for copy in first + second:
            copy.wait_send()
        for copy in to_core:
            copy.wait()
    for copy in own:
        copy.wait()


def spread_plane(n_z, n_seq, joined_z, out_z):
    rows = joined_z.shape[1]
    direct, handed = plane_routes(n_seq)
    slots = 2 * (len(direct) + len(handed)) + 3
    shape = lambda a: jax.ShapeDtypeStruct((n_z, CORES * n_seq, rows, a.shape[2]), bf16)
    return pl.pallas_call(
        functools.partial(spread_plane_kernel, n_z, n_seq),
        in_specs=[VMEM] * 2,
        out_specs=[ANY] * 2,
        out_shape=[shape(joined_z), shape(out_z)],
        scratch_shapes=[
            pltpu.SemaphoreType.DMA((2,)),
            pltpu.SemaphoreType.DMA((2, slots)),
            pltpu.SemaphoreType.DMA((2, slots)),
        ],
        compiler_params=pltpu.CompilerParams(collective_id=1, has_side_effects=True),
        name="spread_plane",
    )(joined_z, out_z)


TILE = 256


def chunk_of(q):
    k = q // 2
    return k, jnp.where(k == 0, q % 2, 1 - q % 2)


def feed_plane_kernel(n_seq, near_count, *refs):
    near = refs[:near_count]
    normed, weights, n_all, d_all, y_own, y_core, back, gradient, arrived = refs[near_count : near_count + 9]
    scratch = refs[near_count + 9 :]
    (w, hidden, both, core_sum, own_back, t_in, n_tile, d_tile, core_out, y_out, g_out) = scratch[:11]
    (local, tile_sem, y_sem, g_sem, n_send, n_recv, d_send, d_recv, c_send, c_recv, yc_send, yc_recv, r_send, r_recv) = scratch[11:]
    z, c, s = coordinates()
    length = normed.shape[0]
    units = hidden.shape[1]
    steps = length // TILE
    chunks = CORES * n_seq
    folded = (n_seq, steps) == (4, 2)
    core_peer = (z, 1 - c, s)
    peer = lambda k: (z, c, s ^ k)
    neighbours = [1, 2] if folded else list(range(1, n_seq))
    greet([peer(k) for k in neighbours] + [core_peer], [])
    mine = lambda k: 0 if k == 0 else 2 * k + 1
    cross = lambda k: 1 if k == 0 else 2 * k

    w_copy = pltpu.make_async_copy(weights, w.at[:, : 3 * units], local.at[0])
    w_copy.start()
    n_here = [(0, normed)]
    d_here = [(mine(k), near[i]) for i, k in enumerate([0] + neighbours)]

    def lies(here, gathered, index):
        for place, ref in here:
            if place == index:
                return ref
        return gathered.at[index]

    n_sems, d_sems = (n_send, n_recv), (d_send, d_recv)
    n_core = [remote(normed, n_all.at[1], n_sems, 0, core_peer)]
    d_core = [remote(near[i], d_all.at[cross(k)], d_sems, i, core_peer) for i, k in enumerate([0] + neighbours)]
    n_direct = [remote(normed, n_all.at[mine(k)], n_sems, 1 + i, peer(k)) for i, k in enumerate(neighbours)]
    for copy in n_core + n_direct + d_core:
        copy.start()
    base = 1 + len(neighbours)
    n_core += [remote(n_all.at[mine(k)], n_all.at[cross(k)], n_sems, base + i, core_peer) for i, k in enumerate(neighbours)]
    base_n, base_d = 2 * len(neighbours) + 1, 1 + len(neighbours)
    if folded:
        top, bottom = pl.ds(0, TILE), pl.ds(TILE, TILE)
        diag = lambda ref, half: ref.at[mine(3), half]
        n_fold = [
            remote(n_all.at[mine(1), top], diag(n_all, top), n_sems, base_n, peer(2)),
            remote(n_all.at[mine(2), bottom], diag(n_all, bottom), n_sems, base_n + 1, peer(1)),
        ]
        d_fold = [
            remote(near[1].at[top], diag(d_all, top), d_sems, base_d, peer(2)),
            remote(near[2].at[bottom], diag(d_all, bottom), d_sems, base_d + 1, peer(1)),
        ]
        n_core.append(remote(n_all.at[mine(3)], n_all.at[cross(3)], n_sems, base_n + 2, core_peer))
        d_core.append(remote(d_all.at[mine(3)], d_all.at[cross(3)], d_sems, base_d + 2, core_peer))

    def chunk_ready(q):
        @pl.when(q == 1)
        def _():
            n_core[0].wait_recv()
            d_core[0].wait_recv()

        @pl.when(q == 2)
        def _():
            for i, copy in enumerate(n_direct):
                copy.wait_recv()
                n_core[1 + i].start()
                if folded:
                    n_fold[i].start()
            if folded:
                for copy in d_fold:
                    copy.start()

        for i, k in enumerate(neighbours):

            pl.when(q == cross(k))(n_core[1 + i].wait_recv)
            pl.when(q == cross(k))(d_core[1 + i].wait_recv)

        if folded:

            @pl.when(q == cross(3))
            def _():
                for copy in n_fold + d_fold:
                    copy.wait_recv()
                n_core[3].start()
                d_core[3].start()
                n_core[3].wait_recv()
                d_core[3].wait_recv()

    def tile_copies(t, step_of):
        q, h = t // steps, t % steps
        rows = pl.ds(pl.multiple_of(h * TILE, TILE), TILE)
        for a, (here, gathered, tile) in enumerate(((n_here, n_all, n_tile), (d_here, d_all, d_tile))):
            copy = lambda source: pltpu.make_async_copy(source, tile.at[t % 2], tile_sem.at[a, t % 2])
            elsewhere = True
            for index, ref in here:
                pl.when(q == index)(lambda: step_of(copy(ref.at[rows])))
                elsewhere = elsewhere & (q != index)
            pl.when(elsewhere)(lambda: step_of(copy(gathered.at[q, rows])))

    def begin(copy):
        copy.start()

    def finish(copy):
        copy.wait()

    def core_copy(k, h):
        return remote(core_out.at[h], core_sum.at[k, h], (c_send.at[k], c_recv.at[k]), h, core_peer)

    def y_local(k, h):
        rows = pl.ds(pl.multiple_of(h * TILE, TILE), TILE)
        return pltpu.make_async_copy(y_out.at[h], y_own.at[k, rows], y_sem.at[h])

    def y_remote(k, h):
        rows = pl.ds(pl.multiple_of(h * TILE, TILE), TILE)
        return remote(y_out.at[h], y_core.at[k, rows], (yc_send.at[k], yc_recv.at[k]), h, core_peer)

    ends = (r_send, r_recv)

    def to_peer(k, h):
        if (folded, k) == (True, 3):
            return remote(core_sum.at[3, h], t_in.at[h], ends, h, peer(1 + h))
        slot = (2 if folded else 0) + (k - 1) * steps + h
        return remote(core_sum.at[k, h], arrived.at[k - 1, h], ends, slot, peer(k))

    late = [(2, 0), (1, 1)] if folded else []
    prompt = [(k, h) for k in range(1, n_seq) for h in range(steps)]
    for pair in late:
        prompt.remove(pair)

    tile_copies(jnp.int32(0), begin)
    w_copy.wait()

    def tile_step(t, _):
        q, h = t // steps, t % steps
        k, other = chunk_of(q)
        slot = t % 2
        tile_copies(t, finish)
        values = n_tile[slot]
        gate = dot(values, w[:, :units], NN)
        up = dot(values, w[:, units : 2 * units], NN)
        d_hidden = dot(d_tile[slot], w[:, 2 * units : 3 * units], NN)
        sigmoid = 1.0 / (1.0 + jnp.exp(-gate))
        silu = gate * sigmoid
        low = (silu * up).astype(bf16)
        d_gate = (d_hidden * up * sigmoid * (1.0 + gate * (1.0 - sigmoid))).astype(bf16)
        d_up = (d_hidden * silu).astype(bf16)
        rows = pl.ds(pl.multiple_of(t * TILE, TILE), TILE)
        hidden[rows] = low
        both[rows, :units] = d_gate
        both[rows, units:] = d_up

        @pl.when(t + 1 < chunks * steps)
        def _():
            pl.when((t + 1) % steps == 0)(lambda: chunk_ready((t + 1) // steps))
            tile_copies(t + 1, begin)

        result = dot(low, w[:, 2 * units : 3 * units], NT).astype(bf16)
        before = q - 1
        k_before, other_before = chunk_of(jnp.maximum(before, 0))
        pl.when((before >= 0) & (other_before == 0))(lambda: y_local(k_before, h).wait())
        pl.when((before >= 0) & (other_before == 1))(lambda: y_remote(k_before, h).wait_send())
        y_out[h] = result
        pl.when(other == 0)(lambda: y_local(k, h).start())
        pl.when(other == 1)(lambda: y_remote(k, h).start())

        part = dot(d_gate, w[:, :units], NT) + dot(d_up, w[:, units : 2 * units], NT)

        @pl.when(q == 0)
        def _():
            own_back[h] = part.astype(bf16)

        @pl.when(other == 1)
        def _():
            pl.when(k > 0)(lambda: core_copy(k - 1, h).wait_send())
            core_out[h] = part.astype(bf16)
            core_copy(k, h).start()

        @pl.when((other == 0) & (k > 0))
        def _():
            core_copy(k, h).wait_recv()
            core_sum[k, h] = (part + core_sum[k, h].astype(f32)).astype(bf16)
            for key, half in prompt:
                pl.when((k == key) & (h == half))(to_peer(key, half).start)

        return 0

    lax.fori_loop(0, chunks * steps, tile_step, 0)

    blocks = chunks * length // D
    width = blocks * TILE

    def column_copies(j):
        slot = j % 2
        columns = pl.ds(pl.multiple_of(j * TILE, TILE), TILE)
        copies = []
        for a, (here, gathered) in enumerate(((n_here, n_all), (d_here, d_all))):
            for b in range(blocks):
                for q in range(D // length):
                    first = pl.multiple_of((slot * 2 + a) * width + b * TILE, TILE)
                    target = w.at[pl.ds(q * length, length), pl.ds(first, TILE)]
                    index = b * (D // length) + q
                    source = lies(here, gathered, index)
                    copies.append((source.at[:, columns], target, (slot, a * blocks + b, q)))
        return [pltpu.make_async_copy(x, y, g_sem.at[i]) for x, y, i in copies]

    def g_store(j):
        rows = pl.ds(pl.multiple_of(j * TILE, TILE), TILE)
        return pltpu.make_async_copy(g_out.at[j % 2], gradient.at[rows], local.at[j % 2])

    for copy in column_copies(0):
        copy.start()

    def column_step(j, _):
        slot = j % 2

        @pl.when(j + 1 < D // TILE)
        def _():
            for copy in column_copies(j + 1):
                copy.start()

        for copy in column_copies(j):
            copy.wait()
        pl.when(j >= 2)(lambda: g_store(j - 2).wait())
        expand = shrink = None
        for b in range(blocks):
            rows = slice(b * D, (b + 1) * D)
            at = lambda a: pl.ds(pl.multiple_of((slot * 2 + a) * width + b * TILE, TILE), TILE)
            one = dot(w[:, at(0)], both[rows], TN)
            two = dot(w[:, at(1)], hidden[rows], TN)
            expand = one if expand is None else expand + one
            shrink = two if shrink is None else shrink + two
        g_out[slot, :, : 2 * units] = expand.astype(bf16)
        g_out[slot, :, 2 * units :] = shrink.astype(bf16)
        g_store(j).start()
        if folded:

            @pl.when(j == 3)
            def _():
                for i, (key, half) in enumerate(late):
                    to_peer(3, i).wait_recv()
                    total = core_sum[key, half].astype(f32) + t_in[i].astype(f32)
                    core_sum[key, half] = total.astype(bf16)
                    to_peer(key, half).start()

        return 0

    lax.fori_loop(0, D // TILE, column_step, 0)
    for j in (D // TILE - 2, D // TILE - 1):
        g_store(j).wait()

    for h in range(steps):
        core_copy(0, h).wait_recv()
        held = own_back[h].astype(f32) + core_sum[0, h].astype(f32)
        for i, key in enumerate(neighbours):
            to_peer(key, h).wait_recv()
            incoming = pltpu.make_async_copy(arrived.at[i, h], n_tile.at[i % 2], tile_sem.at[0, i % 2])
            incoming.start()
            incoming.wait()
            held = held + n_tile[i % 2].astype(f32)
        d_tile[h % 2] = held.astype(bf16)
        out = pltpu.make_async_copy(d_tile.at[h % 2], back.at[pl.ds(h * TILE, TILE)], tile_sem.at[1, h % 2])
        out.start()
        out.wait()

    for copy in n_direct + n_core + d_core:
        copy.wait_send()
    if folded:
        for copy in n_fold + d_fold:
            copy.wait_send()
    for key, half in prompt + late:
        to_peer(key, half).wait_send()
    for h in range(steps):
        core_copy(n_seq - 1, h).wait_send()
        y_local(n_seq - 1, h).wait()
        for k in range(n_seq):
            y_remote(k, h).wait_recv()


def feed_plane(n_seq, normed, upstream, weights):
    length = normed.shape[0]
    units = weights.shape[1] // 3
    steps = length // TILE
    chunks = CORES * n_seq
    tokens = chunks * length
    near = len(upstream)
    count = near - 1
    copies = 2 * count + 5
    w_columns = 3 * units if 3 * units > 4 * TILE * tokens // D else 4 * TILE * tokens // D
    sums = 2 + near * steps
    shape = lambda *dims: jax.ShapeDtypeStruct(dims, bf16)

    outs = pl.pallas_call(
        functools.partial(feed_plane_kernel, n_seq, near),
        in_specs=[ANY] * (near + 2),
        out_specs=[ANY] * 7,
        out_shape=[
            shape(chunks, length, D),
            shape(chunks, length, D),
            shape(n_seq, length, D),
            shape(n_seq, length, D),
            shape(length, D),
            shape(D, 3 * units),
            shape(count, steps, TILE, D),
        ],
        scratch_shapes=[
            pltpu.VMEM((D, w_columns), bf16),
            pltpu.VMEM((tokens, units), bf16),
            pltpu.VMEM((tokens, 2 * units), bf16),
            pltpu.VMEM((n_seq, steps, TILE, D), bf16),
            pltpu.VMEM((steps, TILE, D), bf16),
            pltpu.VMEM((2, TILE, D), bf16),
            pltpu.VMEM((2, TILE, D), bf16),
            pltpu.VMEM((2, TILE, D), bf16),
            pltpu.VMEM((steps, TILE, D), bf16),
            pltpu.VMEM((steps, TILE, D), bf16),
            pltpu.VMEM((2, TILE, 3 * units), bf16),
            pltpu.SemaphoreType.DMA((near + 3,)),
            pltpu.SemaphoreType.DMA((2, 2)),
            pltpu.SemaphoreType.DMA((steps,)),
            pltpu.SemaphoreType.DMA((2, 2 * tokens // D, D // length)),
            pltpu.SemaphoreType.DMA((copies,)),
            pltpu.SemaphoreType.DMA((copies,)),
            pltpu.SemaphoreType.DMA((copies,)),
            pltpu.SemaphoreType.DMA((copies,)),
            pltpu.SemaphoreType.DMA((n_seq, steps)),
            pltpu.SemaphoreType.DMA((n_seq, steps)),
            pltpu.SemaphoreType.DMA((n_seq, steps)),
            pltpu.SemaphoreType.DMA((n_seq, steps)),
            pltpu.SemaphoreType.DMA((sums,)),
            pltpu.SemaphoreType.DMA((sums,)),
        ],
        compiler_params=pltpu.CompilerParams(
            collective_id=2, has_side_effects=True, vmem_limit_bytes=60 << 20
        ),
        cost_estimate=pl.CostEstimate(
            flops=20 * tokens * D * units, bytes_accessed=12 * tokens * D, transcendentals=tokens * units
        ),
        name="feed_plane",
    )(*upstream, normed, weights)
    return outs[2:6]


class Links:
    def __init__(self, n_dp, n_seq):
        self.n_z = n_dp // CORES
        self.n_seq = n_seq
        self.plane = CORES * n_seq

    def place(self):
        return coordinates()

    def send(self, values, pairs_of):
        pairs = []
        for z in range(self.n_z):
            for c in range(CORES):
                for s in range(self.n_seq):
                    to = pairs_of(z, c, s)
                    if to is not None:
                        tz, tc, ts = to
                        pairs.append((((z * CORES + c) * self.n_seq + s), (tz * CORES + tc) * self.n_seq + ts))
        return lax.ppermute(values, AXES, pairs)

    def core(self, values):
        return self.send(values, lambda z, c, s: (z, 1 - c, s))

    def peer(self, values, k):
        return self.send(values, lambda z, c, s: (z, c, s ^ k))

    def up(self, values, first, last):
        return self.send(values, lambda z, c, s: (z + 1, c, s) if first <= z <= last else None)

    def down(self, values, first, last):
        return self.send(values, lambda z, c, s: (z - 1, c, s) if first <= z <= last else None)

    def seq_gather(self, values):
        if self.n_seq != 4:
            return [[values]] + [[self.peer(values, k)] for k in range(1, self.n_seq)]
        half = values.shape[0] // 2
        one, two = self.peer(values, 1), self.peer(values, 2)
        top = self.peer(one[:half], 2)
        bottom = self.peer(two[half:], 1)
        return [[values], [one], [two], [top, bottom]]

    def seq_scatter(self, parts, add):
        if self.n_seq != 4:
            return add([parts[0]] + [self.peer(parts[k], k) for k in range(1, self.n_seq)])
        half = parts[0].shape[0] // 2
        top = self.peer(parts[3][:half], 1)
        bottom = self.peer(parts[3][half:], 2)
        two = [self.peer(add([parts[2][:half], top]), 2), self.peer(parts[2][half:], 2)]
        one = [self.peer(parts[1][:half], 1), self.peer(add([parts[1][half:], bottom]), 1)]
        return [add([parts[0][:half], two[0], one[0]]), add([parts[0][half:], two[1], one[1]])]

    def line_scatter(self, full, add):
        n = self.n_z
        z, _, _ = self.place()
        rows = full.shape[0] // n
        take = lambda d: lax.dynamic_slice_in_dim(full, jnp.clip(d, 0, n - 1) * rows, rows, 0)
        above = below = None
        for k in range(1, n):
            one, two = take(z + n - k), take(z - n + k)
            one = one if above is None else add([one, above])
            two = two if below is None else add([two, below])
            above = self.up(one, 0, k - 1)
            below = self.down(two, n - k, n - 1)
        return [take(z)] + ([above, below] if n > 1 else [])


def add_low(parts):
    return functools.reduce(lambda a, b: a + b, [p.astype(f32) for p in parts]).astype(bf16)


def add_wide(parts):
    return functools.reduce(lambda a, b: a + b, [p.astype(f32) for p in parts])


def body(
    n_dp,
    n_seq,
    tokens,
    joined_weight,
    output_weight,
    expand_weight,
    shrink_weight,
    norm_gains,
    doc_lengths,
    cotangent,
):
    links = Links(n_dp, n_seq)
    n_z, plane = links.n_z, links.plane
    z, core, seq = links.place()
    me = core * n_seq + seq
    devices = n_dp * n_seq
    local_len = tokens.shape[1]
    rows = D // devices
    units = FF // plane
    own_gains = GAINS // devices
    offset = seq * local_len

    kv_columns = joined_weight[:, Q_WIDTH:].reshape(rows, 2, KV_HEADS, HEAD_DIM).transpose(0, 2, 1, 3)
    gain_block = jnp.pad(norm_gains, (0, rows * PAIR - own_gains)).reshape(rows, PAIR)
    joined_block = jnp.concatenate(
        [joined_weight[:, :Q_WIDTH], kv_columns.reshape(rows, 2 * KV_WIDTH), gain_block], axis=1
    )
    shrink_rows = shrink_weight.T
    shares = jnp.concatenate(
        [expand_weight.reshape(rows, 2, plane, units), shrink_rows.reshape(rows, 1, plane, units)], axis=1
    )
    shares = shares.transpose(2, 0, 1, 3).reshape(plane, rows, 3 * units)
    block, joined_z, output_z = first_gather(n_z, n_seq, shares, joined_block, output_weight.T)
    lines = [[a * CORES + c for a in range(n_z)] for c in range(CORES)]
    weights = lax.all_gather(
        block.reshape(plane * rows, 3 * units), "dp", axis=0, tiled=True, axis_index_groups=lines
    )
    joined_all, output_all = spread_plane(n_z, n_seq, joined_z, output_z)
    joined_all = joined_all.reshape(D, QKV + PAIR)
    output_all = output_all.reshape(D, Q_WIDTH)
    gains = joined_all[:, QKV:].reshape(devices, rows * PAIR)[:, :own_gains].reshape(GAINS).astype(f32)
    joined_all = joined_all[:, :QKV]
    gain_one = gains[:D]
    gain_query = gains[D : D + HEAD_DIM]
    gain_key = gains[D + HEAD_DIM : D + PAIR]
    gain_two = gains[D + PAIR :]
    head_gains = jnp.stack([jnp.tile(gain_query, 2), jnp.tile(gain_key, 2)])

    half = HEAD_DIM // 2
    frequency = 10000.0 ** (-jnp.arange(half, dtype=f32) / half)
    angles = (offset + jnp.arange(local_len, dtype=jnp.int32)).astype(f32)[:, None] * frequency[None, :]
    cosine, sine = jnp.cos(angles), jnp.sin(angles)
    tables = jnp.stack(
        [jnp.concatenate([cosine] * 4, axis=1), jnp.concatenate([-sine, sine, -sine, sine], axis=1)]
    )
    places = jnp.arange(ROW_LEN, dtype=jnp.int32)
    docs = jnp.zeros((ROW_LEN,), jnp.int32)
    bound = 0
    for index in range(doc_lengths.shape[1] - 1):
        bound = bound + doc_lengths[0, index]
        docs = docs + (places >= bound).astype(jnp.int32)
    mark = jnp.arange(PAIR, dtype=jnp.int32)[None] - HEAD_DIM
    same = (mark >= 0) & (mark < MARK) & (mark == docs[:, None])
    other = (mark >= 0) & (mark < MARK) & (mark != docs[:, None])
    carries = (mark >= MARK) & (mark < MARK + 3)
    key_marks = jnp.where(other, -1024.0, jnp.where(carries, 1.0, 0.0)).astype(bf16)
    query_marks = lax.dynamic_slice_in_dim(same.astype(bf16), offset, local_len, 0)
    offset_array = jnp.reshape(offset, (1,)).astype(jnp.int32)

    flat = tokens.reshape(local_len, D).astype(f32)
    scale_one = rms_scale(flat)
    normed_low = (flat * scale_one * gain_one).astype(bf16)
    projected = dot(normed_low, joined_all, NN)
    turned = rope(projected, head_gains, tables)
    own_kv = turned[:, Q_WIDTH:]
    kv = jnp.zeros((ROW_LEN, 2 * KV_WIDTH), bf16)
    for k, parts in enumerate(links.seq_gather(own_kv)):
        start = (seq ^ k) * local_len
        for part in parts:
            kv = lax.dynamic_update_slice_in_dim(kv, part, start, 0)
            start = start + part.shape[0]
    attended, q_marked = attend(offset_array, turned, kv, key_marks, query_marks)
    attended_low = attended.astype(bf16)
    residual = flat + dot(attended_low, output_all, NT)
    scale_two = rms_scale(residual)
    normed_two = (residual * scale_two * gain_two).astype(bf16)

    upstream_low = cotangent.reshape(local_len, D)
    early, _ = lax.optimization_barrier((upstream_low, kv))
    near = [1, 2] if (n_seq, local_len) == (4, 2 * TILE) else list(range(1, n_seq))
    upstream_near = [upstream_low] + [links.peer(early, k) for k in near]
    y_own, y_core, back, share_gradient = feed_plane(n_seq, normed_two, upstream_near, weights)
    grad_normed_two = back.astype(f32)
    mine = lax.psum_scatter(
        share_gradient, "dp", scatter_dimension=0, tiled=True, axis_index_groups=lines
    )
    expand_gradient = jnp.zeros((rows, 2 * FF), f32)
    shrink_gradient = jnp.zeros((rows, FF), f32)
    for k in range(plane):
        p = (core ^ (k // n_seq)) * n_seq + (seq ^ (k % n_seq))
        piece = lax.dynamic_slice_in_dim(mine, p * rows, rows, 0)
        if k:
            piece = links.send(piece, lambda a, c, s: (a, c ^ (k // n_seq), s ^ (k % n_seq)))
        piece = piece.astype(f32)
        put = lambda a, part, start: lax.dynamic_update_slice_in_dim(a, part, start + p * units, 1)
        expand_gradient = put(expand_gradient, piece[:, :units], 0)
        expand_gradient = put(expand_gradient, piece[:, units : 2 * units], FF)
        shrink_gradient = put(shrink_gradient, piece[:, 2 * units :], 0)
    shrink_gradient = shrink_gradient.T

    upstream = upstream_low.astype(f32)
    gain_two_grad = jnp.sum(grad_normed_two * residual * scale_two, axis=0)
    grad_residual = upstream + norm_back(grad_normed_two, residual, scale_two, gain_two)
    grad_attn_low = grad_residual.astype(bf16)
    output_term = dot(grad_attn_low, attended_low, TN).astype(bf16)
    grad_out_low = dot(grad_attn_low, output_all, NN).astype(bf16)
    y_own, y_core, _ = lax.optimization_barrier((y_own, y_core, grad_out_low))
    feed_result = links.seq_scatter([add_low([y_own[k], y_core[k]]) for k in range(n_seq)], add_low)
    feed_result = jnp.concatenate(feed_result, axis=0) if isinstance(feed_result, list) else feed_result
    layer_output = (residual + feed_result.astype(f32)).astype(bf16)
    grad_query, grad_kv_all = attend_back(offset_array, q_marked, grad_out_low, attended, kv, key_marks)
    kv_parts = [lax.dynamic_slice_in_dim(grad_kv_all, (seq ^ k) * local_len, local_len, 0) for k in range(n_seq)]
    grad_kv = links.seq_scatter(kv_parts, add_wide if n_seq != 4 else add_low)
    grad_kv = jnp.concatenate(grad_kv, axis=0) if isinstance(grad_kv, list) else grad_kv
    grad_projected, head_gain_sums = rope_back(grad_query, grad_kv, projected, head_gains, tables)
    joined_term = dot(normed_low, grad_projected, TN).astype(bf16)
    grad_normed = dot(grad_projected, joined_all, NT)
    gain_one_grad = jnp.sum(grad_normed * flat * scale_one, axis=0)
    token_gradient = grad_residual + norm_back(grad_normed, flat, scale_one, gain_one)
    gain_query_grad = head_gain_sums[0, :HEAD_DIM] + head_gain_sums[0, HEAD_DIM:]
    gain_key_grad = head_gain_sums[1, :HEAD_DIM]
    gain_grads = jnp.concatenate([gain_one_grad, gain_query_grad, gain_key_grad, gain_two_grad])
    gain_block = jnp.pad(gain_grads.reshape(devices, own_gains), ((0, 0), (0, rows * PAIR - own_gains)))
    gain_block = gain_block.reshape(devices * rows, PAIR).astype(bf16)

    def scatter_all(full):
        width = full.shape[1]
        full = full.reshape(n_z, CORES, n_seq, rows, width)
        other = links.core(lax.dynamic_index_in_dim(full, 1 - core, 1, keepdims=False))
        full = add_low([lax.dynamic_index_in_dim(full, core, 1, keepdims=False), other])
        full = full.transpose(1, 0, 2, 3).reshape(n_seq, n_z * rows, width)
        parts = [lax.dynamic_index_in_dim(full, seq ^ k, 0, keepdims=False) for k in range(n_seq)]
        out = links.seq_scatter(parts, add_low)
        out = jnp.concatenate(out, axis=0) if isinstance(out, list) else out
        return add_wide(links.line_scatter(out, add_low))

    output_gradient = scatter_all(output_term).T
    joined_sum = scatter_all(jnp.concatenate([joined_term, gain_block], axis=1))
    kv_sum = joined_sum[:, Q_WIDTH:QKV].reshape(rows, KV_HEADS, 2, HEAD_DIM).transpose(0, 2, 1, 3)
    joined_gradient = jnp.concatenate([joined_sum[:, :Q_WIDTH], kv_sum.reshape(rows, 2 * KV_WIDTH)], axis=1)
    gains_gradient = joined_sum[:, QKV:].reshape(rows * PAIR)[:own_gains]
    return (
        layer_output.reshape(1, local_len, D),
        token_gradient.astype(bf16).reshape(1, local_len, D),
        joined_gradient,
        output_gradient,
        expand_gradient,
        shrink_gradient,
        gains_gradient,
    )


def solution(mesh):
    token_spec, row_spec, column_spec = P("dp", "seq", None), P(AXES, None), P(None, AXES)
    return jax.shard_map(
        functools.partial(body, mesh.shape["dp"], mesh.shape["seq"]),
        mesh=mesh,
        in_specs=(
            token_spec,
            row_spec,
            column_spec,
            row_spec,
            column_spec,
            P(AXES),
            P("dp", None),
            token_spec,
        ),
        out_specs=(token_spec, token_spec, row_spec, column_spec, row_spec, column_spec, P(AXES)),
        check_vma=False,
    )
```

```python
import functools

import jax
import jax.numpy as jnp
from jax import lax
from jax.experimental import pallas as pl
from jax.experimental.pallas import tpu as pltpu
from jax.sharding import PartitionSpec as P

D = 2048
HEADS = 20
KV_HEADS = 5
HEAD_DIM = 64
FF = 6144
ROW_LEN = 2048
GAINS = 4224
PAIR = 2 * HEAD_DIM
Q_WIDTH = HEADS * HEAD_DIM
KV_WIDTH = KV_HEADS * HEAD_DIM
QKV = Q_WIDTH + 2 * KV_WIDTH
CORES = 2

epsilon = 1e-05
f32 = jnp.float32
bf16 = jnp.bfloat16
AXES = ("dp", "seq")
MESH = pl.DeviceIdType.MESH
ANY = pl.BlockSpec(memory_space=pl.ANY)
VMEM = pl.BlockSpec(memory_space=pltpu.VMEM)
NN = (((1,), (0,)), ((), ()))
NT = (((1,), (1,)), ((), ()))
TN = (((0,), (0,)), ((), ()))


def dot(left, right, dims):
    return lax.dot_general(left, right, dims, preferred_element_type=f32)


def rms_scale(values):
    return lax.rsqrt(jnp.mean(values * values, axis=-1, keepdims=True) + epsilon)


def norm_back(upstream, values, scaling, gain_vector):
    weighted = upstream * gain_vector
    average = jnp.mean(weighted * values, axis=-1, keepdims=True)
    return scaling * weighted - values * (scaling * scaling * scaling) * average


def lanes(shape):
    return lax.broadcasted_iota(jnp.int32, shape, len(shape) - 1)


def swap_halves(values):
    half = HEAD_DIM // 2
    first = lanes(values.shape) % HEAD_DIM < half
    return jnp.where(first, pltpu.roll(values, PAIR - half, axis=1), pltpu.roll(values, half, axis=1))


def head_means(values):
    low = lanes(values.shape) < HEAD_DIM
    left = jnp.sum(jnp.where(low, values, 0.0), axis=-1, keepdims=True)
    right = jnp.sum(jnp.where(low, 0.0, values), axis=-1, keepdims=True)
    return jnp.where(low, left, right) * (1.0 / HEAD_DIM)


BAND = 2 * KV_WIDTH
QUERY_BANDS = Q_WIDTH // BAND


def rope_kernel(projected, gains, tables, out):
    is_query = pl.program_id(0) < QUERY_BANDS
    gain = jnp.where(is_query, gains[0:1] * HEAD_DIM**-0.5, gains[1:2])
    direct, crossed = tables[0] * gain, tables[1]
    for start in range(0, BAND, PAIR):
        columns = slice(start, start + PAIR)
        values = projected[:, columns]
        scaling = lax.rsqrt(head_means(values * values) + epsilon)
        turned = values * direct + swap_halves(values * gain) * crossed
        plain = (lanes(values.shape) >= HEAD_DIM) & jnp.logical_not(is_query)
        out[:, columns] = jnp.where(plain, values, turned * scaling).astype(bf16)


def rope(projected, gains, tables):
    tokens, width = projected.shape
    return pl.pallas_call(
        rope_kernel,
        grid=(width // BAND,),
        in_specs=[
            pl.BlockSpec((tokens, BAND), lambda i: (0, i)),
            pl.BlockSpec((2, PAIR), lambda i: (0, 0)),
            pl.BlockSpec((2, tokens, PAIR), lambda i: (0, 0, 0)),
        ],
        out_specs=pl.BlockSpec((tokens, BAND), lambda i: (0, i)),
        out_shape=jax.ShapeDtypeStruct((tokens, width), bf16),
        compiler_params=pltpu.CompilerParams(vmem_limit_bytes=40 << 20),
        cost_estimate=pl.CostEstimate(flops=40 * tokens * width, bytes_accessed=6 * tokens * width, transcendentals=0),
        name="rope",
    )(projected, gains, tables)


def rope_back_kernel(dq, dkv, projected, gains, tables, out, gain_sums):
    step = pl.program_id(0)
    is_query = step < QUERY_BANDS
    gain = jnp.where(is_query, gains[0:1], gains[1:2])
    sums = jnp.zeros((1, PAIR), f32)
    for start in range(0, BAND, PAIR):
        columns = slice(start, start + PAIR)
        values = projected[:, columns]
        upstream = jnp.where(is_query, dq[:, columns] * HEAD_DIM**-0.5, dkv[:, columns].astype(f32))
        plain = (lanes(values.shape) >= HEAD_DIM) & jnp.logical_not(is_query)
        turned = upstream * tables[0] + swap_halves(upstream * tables[1])
        scaling = lax.rsqrt(head_means(values * values) + epsilon)
        unit = values * scaling
        weighted = turned * gain
        back = scaling * (weighted - unit * head_means(weighted * unit))
        out[:, columns] = jnp.where(plain, upstream, back).astype(bf16)
        sums = sums + jnp.sum(jnp.where(plain, 0.0, turned * unit), axis=0, keepdims=True)

    @pl.when(step == 0)
    def _():
        gain_sums[...] = jnp.zeros_like(gain_sums)

    row = lax.broadcasted_iota(jnp.int32, gain_sums.shape, 0)
    gain_sums[...] += jnp.where(row == jnp.where(is_query, 0, 1), sums, 0.0)


def rope_back(dq, dkv, projected, gains, tables):
    tokens, width = projected.shape
    return pl.pallas_call(
        rope_back_kernel,
        grid=(width // BAND,),
        in_specs=[
            pl.BlockSpec((tokens, BAND), lambda i: (0, jnp.minimum(i, QUERY_BANDS - 1))),
            pl.BlockSpec((tokens, BAND), lambda i: (0, 0)),
            pl.BlockSpec((tokens, BAND), lambda i: (0, i)),
            pl.BlockSpec((2, PAIR), lambda i: (0, 0)),
            pl.BlockSpec((2, tokens, PAIR), lambda i: (0, 0, 0)),
        ],
        out_specs=[
            pl.BlockSpec((tokens, BAND), lambda i: (0, i)),
            pl.BlockSpec((8, PAIR), lambda i: (0, 0)),
        ],
        out_shape=[
            jax.ShapeDtypeStruct((tokens, width), bf16),
            jax.ShapeDtypeStruct((8, PAIR), f32),
        ],
        compiler_params=pltpu.CompilerParams(vmem_limit_bytes=40 << 20),
        cost_estimate=pl.CostEstimate(flops=60 * tokens * width, bytes_accessed=10 * tokens * width, transcendentals=0),
        name="rope_back",
    )(dq, dkv, projected, gains, tables)


def three_parts(values):
    first = values.astype(bf16).astype(f32)
    second = (values - first).astype(bf16).astype(f32)
    return first, second, values - first - second


def spread_kv(kv, key_marks, keys, vals):
    both = kv[...]
    lane = lanes(both.shape)
    keys[...] = jnp.where(lane < HEAD_DIM, both, key_marks[...])
    vals[...] = jnp.where(lane < HEAD_DIM, jnp.where(lane < 3, 1.0, 0.0).astype(bf16), both)


MARK = 8


def attend_kernel(tq, tk, offset, q, kv, key_marks, query_marks, out, q_marked, keys, vals, rows):
    local_len = q.shape[0]
    group = q.shape[1] // HEAD_DIM
    spread_kv(kv, key_marks, keys, vals)
    lane1 = lanes((tq, PAIR))
    for tile in range(local_len // tq):
        part = slice(tile * tq, (tile + 1) * tq)
        for head in range(group):
            wide = q[part, (head // 2) * PAIR : (head // 2 + 1) * PAIR].astype(f32)
            if head % 2:
                wide = pltpu.roll(wide, HEAD_DIM, axis=1)
            marked = jnp.where(lane1 < HEAD_DIM, wide, query_marks[part].astype(f32))
            rows[head * tq : (head + 1) * tq] = marked.astype(bf16)
        first = offset[tile]

        def block(index, total, masked):
            span = pl.ds(pl.multiple_of(index * tk, tk), tk)
            expo = jnp.exp(dot(rows[...], keys[span], NT))
            if masked:
                query_pos = first + lax.broadcasted_iota(jnp.int32, (tq, tk), 0)
                key_pos = index * tk + lax.broadcasted_iota(jnp.int32, (tq, tk), 1)
                expo = jnp.where((key_pos <= query_pos)[None], expo.reshape(group, tq, tk), 0.0)
                expo = expo.reshape(group * tq, tk)
            return total + dot(expo.astype(bf16), vals[span], NN)

        full = first // tk
        end = (first + tq + tk - 1) // tk
        total = jnp.zeros((group * tq, PAIR), f32)
        total = lax.fori_loop(0, full, lambda i, t: block(i, t, False), total)
        total = lax.fori_loop(full, end, lambda i, t: block(i, t, True), total)
        denominator = total[:, 0:1]
        mixed = total / denominator
        one, two, three = three_parts(-jnp.log(denominator))
        lane = lanes(total.shape) - HEAD_DIM - MARK
        kept = rows[...].astype(f32)
        kept = jnp.where(lane == 0, one, jnp.where(lane == 1, two, jnp.where(lane == 2, three, kept)))
        kept = kept.astype(bf16)
        for head in range(group):
            q_marked[head, part] = kept[head * tq : (head + 1) * tq]
        for head in range(0, group, 2):
            even = pltpu.roll(mixed[head * tq : (head + 1) * tq], HEAD_DIM, axis=1)
            odd = mixed[(head + 1) * tq : (head + 2) * tq]
            out[part, (head // 2) * PAIR : (head // 2 + 1) * PAIR] = jnp.where(lane1 < HEAD_DIM, even, odd)


def attention_cost(tokens, products):
    pairs = HEADS * tokens * ROW_LEN
    return pl.CostEstimate(flops=products * 2 * 4 * HEAD_DIM * pairs, bytes_accessed=1 << 24, transcendentals=pairs)


def attend(offset, q, kv, key_marks, query_marks):
    tokens = q.shape[0]
    keys = kv.shape[0]
    group = HEADS // KV_HEADS
    width = group * HEAD_DIM
    tq, tk = tokens, min(512, keys)
    spec = pltpu.PrefetchScalarGridSpec(
        num_scalar_prefetch=1,
        grid=(KV_HEADS,),
        in_specs=[
            pl.BlockSpec((tokens, width), lambda g, _: (0, g)),
            pl.BlockSpec((keys, PAIR), lambda g, _: (0, g)),
            pl.BlockSpec((keys, PAIR), lambda g, _: (0, 0)),
            pl.BlockSpec((tokens, PAIR), lambda g, _: (0, 0)),
        ],
        out_specs=[
            pl.BlockSpec((tokens, width), lambda g, _: (0, g)),
            pl.BlockSpec((group, tokens, PAIR), lambda g, _: (g, 0, 0)),
        ],
        scratch_shapes=[
            pltpu.VMEM((keys, PAIR), bf16),
            pltpu.VMEM((keys, PAIR), bf16),
            pltpu.VMEM((group * tq, PAIR), bf16),
        ],
    )
    return pl.pallas_call(
        functools.partial(attend_kernel, tq, tk),
        grid_spec=spec,
        out_shape=[
            jax.ShapeDtypeStruct((tokens, Q_WIDTH), f32),
            jax.ShapeDtypeStruct((HEADS, tokens, PAIR), bf16),
        ],
        compiler_params=pltpu.CompilerParams(vmem_limit_bytes=56 << 20),
        cost_estimate=attention_cost(tokens, 2),
        name="attend",
    )(offset, q, kv, key_marks, query_marks)


def carry_sums(n_seq, parts, sides, folds, held, local, send, receive):
    z, c, s = coordinates()
    step = pl.program_id(0)
    half = parts.shape[1] // 2
    peer = lambda k: (z, c, s ^ k)
    part = lambda k, i: parts.at[k, pl.ds(i * half, half)]
    sems = (send, receive)
    to_side = lambda source, k, i: remote(source, sides.at[k - 1, i], sems, 2 * (k - 1) + i, peer(k))
    folded = n_seq == 4
    direct = [(1, 0), (2, 1)] if folded else [(k, i) for k in range(1, n_seq) for i in range(2)]
    fold = lambda i: remote(part(3, i), folds.at[i], sems, 4 + i, peer(1 + i))
    load = lambda i: pltpu.make_async_copy(part(2 - i, i), held.at[i], local.at[i])
    later = lambda i: to_side(folds.at[i], 2 - i, i)

    @pl.when(step == 0)
    def _():
        greet([peer(k) for k in ((1, 2) if folded else range(1, n_seq))], [])
        if folded:
            for i in range(2):
                fold(i).start()
                load(i).start()

    @pl.when(step == 1)
    def _():
        for k, i in direct:
            to_side(part(k, i), k, i).start()

    if folded:

        @pl.when(step == 2)
        def _():
            for i in range(2):
                load(i).wait()
                fold(i).wait_recv()
                folds[i] = (folds[i].astype(f32) + held[i].astype(f32)).astype(bf16)
                later(i).start()

    @pl.when(step == KV_HEADS - 1)
    def _():
        for k, i in direct:
            to_side(part(k, i), k, i).wait()
        if folded:
            for i in range(2):
                fold(i).wait_send()
                later(i).wait()


def attend_back_kernel(
    n_seq, tq, tk, q_marked, d_out, out, kv, key_marks, parts, dq, dkv, sides,
    keys, vals, d_rows, rows, dk_sum, dv_sum, folds, held, local, send, receive,
):
    carry_sums(n_seq, parts, sides, folds, held, local, send, receive)
    offset = lax.axis_index("seq") * d_out.shape[0]
    local_len = d_out.shape[0]
    group = d_out.shape[1] // HEAD_DIM
    spread_kv(kv, key_marks, keys, vals)
    dk_sum[...] = jnp.zeros_like(dk_sum)
    dv_sum[...] = jnp.zeros_like(dv_sum)
    lane1 = lanes((tq, PAIR))
    for tile in range(local_len // tq):
        part = slice(tile * tq, (tile + 1) * tq)
        for head in range(group):
            pair = slice((head // 2) * PAIR, (head // 2 + 1) * PAIR)
            wide = d_out[part, pair].astype(f32)
            mine = (lane1 < HEAD_DIM) if head % 2 == 0 else (lane1 >= HEAD_DIM)
            delta = jnp.sum(jnp.where(mine, wide * out[part, pair], 0.0), axis=1, keepdims=True)
            one, two, three = three_parts(-delta)
            if head % 2 == 0:
                wide = pltpu.roll(wide, HEAD_DIM, axis=1)
            marks = jnp.where(lane1 == 0, one, jnp.where(lane1 == 1, two, jnp.where(lane1 == 2, three, 0.0)))
            d_rows[head * tq : (head + 1) * tq] = jnp.where(lane1 < HEAD_DIM, marks, wide).astype(bf16)
            rows[head * tq : (head + 1) * tq] = q_marked[head, part]
        first = offset + tile * tq

        def block(index, total, masked):
            span = pl.ds(pl.multiple_of(index * tk, tk), tk)
            prob = jnp.exp(dot(keys[span], rows[...], NT))
            if masked:
                key_pos = index * tk + lax.broadcasted_iota(jnp.int32, (tk, tq), 0)
                query_pos = first + lax.broadcasted_iota(jnp.int32, (tk, tq), 1)
                prob = jnp.where(jnp.concatenate([key_pos <= query_pos] * group, axis=1), prob, 0.0)
            d_scores = (prob * dot(vals[span], d_rows[...], NT)).astype(bf16)
            dv_sum[span] += dot(prob.astype(bf16), d_rows[...], NN)
            dk_sum[span] += dot(d_scores, rows[...], NN)
            return total + dot(d_scores, keys[span], TN)

        full = first // tk
        end = (first + tq + tk - 1) // tk
        total = jnp.zeros((group * tq, PAIR), f32)
        total = lax.fori_loop(0, full, lambda i, t: block(i, t, False), total)
        total = lax.fori_loop(full, end, lambda i, t: block(i, t, True), total)
        for head in range(0, group, 2):
            even = total[head * tq : (head + 1) * tq]
            odd = pltpu.roll(total[(head + 1) * tq : (head + 2) * tq], HEAD_DIM, axis=1)
            dq[part, (head // 2) * PAIR : (head // 2 + 1) * PAIR] = jnp.where(lane1 < HEAD_DIM, even, odd)
    dkv[...] = jnp.where(lanes(dk_sum.shape) < HEAD_DIM, dk_sum[...], dv_sum[...]).astype(bf16)


def attend_back(n_seq, q_marked, d_out, out, kv, key_marks, parts):
    tokens = d_out.shape[0]
    side_count = 2 if n_seq == 4 else n_seq - 1
    slots = 2 * side_count + 2
    keys = kv.shape[0]
    group = HEADS // KV_HEADS
    width = group * HEAD_DIM
    tq, tk = tokens, min(512, keys)
    return pl.pallas_call(
        functools.partial(attend_back_kernel, n_seq, tq, tk),
        grid=(KV_HEADS,),
        in_specs=[
            pl.BlockSpec((group, tokens, PAIR), lambda g: (g, 0, 0)),
            pl.BlockSpec((tokens, width), lambda g: (0, g)),
            pl.BlockSpec((tokens, width), lambda g: (0, g)),
            pl.BlockSpec((keys, PAIR), lambda g: (0, g)),
            pl.BlockSpec((keys, PAIR), lambda g: (0, 0)),
            ANY,
        ],
        out_specs=[
            pl.BlockSpec((tokens, width), lambda g: (0, g)),
            pl.BlockSpec((keys, PAIR), lambda g: (0, g)),
            ANY,
        ],
        scratch_shapes=[
            pltpu.VMEM((keys, PAIR), bf16),
            pltpu.VMEM((keys, PAIR), bf16),
            pltpu.VMEM((group * tq, PAIR), bf16),
            pltpu.VMEM((group * tq, PAIR), bf16),
            pltpu.VMEM((keys, PAIR), f32),
            pltpu.VMEM((keys, PAIR), f32),
            pltpu.VMEM((2, tokens // 2, D), bf16),
            pltpu.VMEM((2, tokens // 2, D), bf16),
            pltpu.SemaphoreType.DMA((2,)),
            pltpu.SemaphoreType.DMA((slots,)),
            pltpu.SemaphoreType.DMA((slots,)),
        ],
        out_shape=[
            jax.ShapeDtypeStruct((tokens, Q_WIDTH), f32),
            jax.ShapeDtypeStruct(kv.shape, bf16),
            jax.ShapeDtypeStruct((side_count, 2, tokens // 2, D), bf16),
        ],
        compiler_params=pltpu.CompilerParams(
            collective_id=6, has_side_effects=True, vmem_limit_bytes=56 << 20
        ),
        cost_estimate=attention_cost(tokens, 4),
        name="attend_back",
    )(q_marked, d_out, out, kv, key_marks, parts)


def coordinates():
    dp = lax.axis_index("dp")
    return dp // CORES, dp % CORES, lax.axis_index("seq")


def device_at(place):
    z, c, s = place
    return z * CORES + c, s


def greet(peers, neighbours):
    barrier = pltpu.get_barrier_semaphore()
    count = len(peers)
    for device in peers:
        pl.semaphore_signal(barrier, inc=1, device_id=device_at(device), device_id_type=MESH)
    for condition, device in neighbours:

        @pl.when(condition)
        def _():
            pl.semaphore_signal(barrier, inc=1, device_id=device_at(device), device_id_type=MESH)

        count = count + condition.astype(jnp.int32)
    pl.semaphore_wait(barrier, count)


def remote(source, target, sems, slot, device):
    send, receive = sems
    return pltpu.make_async_remote_copy(
        src_ref=source,
        dst_ref=target,
        send_sem=send.at[slot],
        recv_sem=receive.at[slot],
        device_id=device_at(device),
        device_id_type=MESH,
    )


def first_gather_kernel(n_z, n_seq, expand, shrink, joined, out_rows, block, joined_z, out_z, local, send, receive):
    z, c, s = coordinates()
    plane = CORES * n_seq
    rows = joined.shape[0]
    me = c * n_seq + s
    others = [(z, c ^ (k // n_seq), s ^ (k % n_seq)) for k in range(1, plane)]
    above, below = (z + 1, c, s), (z - 1, c, s)
    greet(others, [(z > 0, below), (z < n_z - 1, above)])
    sems = (send, receive)
    mine = [
        pltpu.make_async_copy(joined, joined_z.at[z], local.at[0]),
        pltpu.make_async_copy(out_rows, out_z.at[z], local.at[1]),
    ]
    units = block.shape[2] // 3
    half = expand.shape[1] // 2

    def share(p):
        start = pl.multiple_of(p * units, units)
        other = pl.multiple_of(half + p * units, units)
        sources = (expand.at[:, pl.ds(start, units)], expand.at[:, pl.ds(other, units)], shrink.at[:, pl.ds(start, units)])
        return [(a, block.at[me, :, pl.ds(i * units, units)]) for i, a in enumerate(sources)]

    mine += [pltpu.make_async_copy(a, b, local.at[2 + i]) for i, (a, b) in enumerate(share(me))]
    for copy in mine:
        copy.start()
    slot = 0
    chains = []
    for source, target in ((joined, joined_z), (out_rows, out_z)):
        ups, downs = [], []
        for k in range(1, n_z):
            held = source if k == 1 else target.at[(z + n_z - k + 1) % n_z]
            ups.append(remote(held, target.at[(z + n_z - k + 1) % n_z], sems, slot, above))
            held = source if k == 1 else target.at[(z + k - 1) % n_z]
            downs.append(remote(held, target.at[(z + k - 1) % n_z], sems, slot + 1, below))
            slot += 2
        chains.append((ups, downs))
    for ups, downs in chains:
        pl.when(z < n_z - 1)(ups[0].start)
        pl.when(z > 0)(downs[0].start)
    sent = []
    for k, (tz, tc, ts) in enumerate(others):
        for i, (a, b) in enumerate(share(tc * n_seq + ts)):
            copy = remote(a, b, sems, slot + 3 * k + i, (tz, tc, ts))
            copy.start()
            sent.append(copy)
    for k in range(1, n_z):
        for ups, downs in chains:
            pl.when(z >= k)(ups[k - 1].wait_recv)
            pl.when(z + k < n_z)(downs[k - 1].wait_recv)
            if k < n_z - 1:
                pl.when((z >= k) & (z < n_z - 1))(ups[k].start)
                pl.when((z + k < n_z) & (z > 0))(downs[k].start)
    for k in range(1, n_z):
        for ups, downs in chains:
            pl.when((z >= k - 1) & (z < n_z - 1))(ups[k - 1].wait_send)
            pl.when((z + k - 1 < n_z) & (z > 0))(downs[k - 1].wait_send)
    for copy in sent:
        copy.wait()
    for copy in mine:
        copy.wait()


def first_gather(n_z, n_seq, expand, shrink, joined, out_rows):
    plane = CORES * n_seq
    rows = joined.shape[0]
    copies = 4 * (n_z - 1) + 3 * (plane - 1)
    units = shrink.shape[1] // plane
    shape = lambda *dims: jax.ShapeDtypeStruct(dims, bf16)
    return pl.pallas_call(
        functools.partial(first_gather_kernel, n_z, n_seq),
        in_specs=[VMEM] * 4,
        out_specs=[ANY] * 3,
        out_shape=[
            shape(plane, rows, 3 * units),
            shape(n_z, rows, joined.shape[1]),
            shape(n_z, rows, out_rows.shape[1]),
        ],
        scratch_shapes=[
            pltpu.SemaphoreType.DMA((5,)),
            pltpu.SemaphoreType.DMA((copies,)),
            pltpu.SemaphoreType.DMA((copies,)),
        ],
        compiler_params=pltpu.CompilerParams(collective_id=0, has_side_effects=True),
        name="first_gather",
    )(expand, shrink, joined, out_rows)


def plane_routes(n_seq):
    if n_seq == 4:
        return [(1, 0, 0, 1), (2, 0, 0, 2)], [(3, 1, 1, 2), (4, 2, 2, 1)]
    return [(k, 0, 0, k) for k in range(1, n_seq)], []


def spread_plane_kernel(n_z, n_seq, joined_z, out_z, joined, out_rows, local, send, receive):
    z, c, s = coordinates()
    direct, handed = plane_routes(n_seq)
    count = len(direct) + len(handed) + 1
    core_peer = (z, 1 - c, s)
    greet([(z, c, s ^ k) for k in sorted({r[3] for r in direct + handed})] + [core_peer], [])
    half = n_z // 2
    parts = {0: slice(0, n_z), 1: slice(0, half), 2: slice(half, n_z)}
    plans = []
    own = []
    for index, (source, target) in enumerate(((joined_z, joined), (out_z, out_rows))):
        sems = (send.at[index], receive.at[index])
        at = lambda k, part, target=target: target.at[parts[part], c * n_seq + (s ^ k)]
        own.append(pltpu.make_async_copy(source, at(0, 0), local.at[index]))
        own[-1].start()
        first = [remote(source, at(0, 0), sems, slot, (z, c, s ^ peer)) for slot, _, _, peer in direct]
        second = [remote(at(k, p), at(k, p), sems, slot, (z, c, s ^ peer)) for slot, k, p, peer in handed]
        to_core = [remote(source, at(0, 0), sems, count, core_peer)]
        held = [(k, 0) for k in range(1, n_seq)] if not handed else [(1, 0), (2, 0), (3, 1), (3, 2)]
        to_core += [remote(at(k, p), at(k, p), sems, count + 1 + i, core_peer) for i, (k, p) in enumerate(held)]
        plans.append((first, second, to_core))
    for first, second, to_core in plans:
        for copy in first + to_core[:1]:
            copy.start()
    for first, second, to_core in plans:
        for i, copy in enumerate(first):
            copy.wait_recv()
            if second:
                second[i].start()
            to_core[1 + i].start()
    for first, second, to_core in plans:
        for i, copy in enumerate(second):
            copy.wait_recv()
            to_core[1 + len(first) + i].start()
    for first, second, to_core in plans:
        for copy in first + second:
            copy.wait_send()
        for copy in to_core:
            copy.wait()
    for copy in own:
        copy.wait()


def spread_plane(n_z, n_seq, joined_z, out_z):
    rows = joined_z.shape[1]
    direct, handed = plane_routes(n_seq)
    slots = 2 * (len(direct) + len(handed)) + 3
    shape = lambda a: jax.ShapeDtypeStruct((n_z, CORES * n_seq, rows, a.shape[2]), bf16)
    return pl.pallas_call(
        functools.partial(spread_plane_kernel, n_z, n_seq),
        in_specs=[VMEM] * 2,
        out_specs=[ANY] * 2,
        out_shape=[shape(joined_z), shape(out_z)],
        scratch_shapes=[
            pltpu.SemaphoreType.DMA((2,)),
            pltpu.SemaphoreType.DMA((2, slots)),
            pltpu.SemaphoreType.DMA((2, slots)),
        ],
        compiler_params=pltpu.CompilerParams(collective_id=1, has_side_effects=True),
        name="spread_plane",
    )(joined_z, out_z)


TILE = 256


def chunk_of(q):
    k = q // 2
    return k, jnp.where(k == 0, q % 2, 1 - q % 2)


def feed_plane_kernel(n_seq, near_count, *refs):
    near = refs[:near_count]
    normed, weights, n_all, d_all, y_own, y_core, back, gradient, arrived = refs[near_count : near_count + 9]
    scratch = refs[near_count + 9 :]
    (w, hidden, both, core_sum, own_back, t_in, n_tile, d_tile, core_out, y_out, g_out) = scratch[:11]
    (local, tile_sem, y_sem, g_sem, n_send, n_recv, d_send, d_recv, c_send, c_recv, yc_send, yc_recv, r_send, r_recv) = scratch[11:]
    z, c, s = coordinates()
    length = normed.shape[0]
    units = hidden.shape[1]
    steps = length // TILE
    chunks = CORES * n_seq
    folded = (n_seq, steps) == (4, 2)
    core_peer = (z, 1 - c, s)
    peer = lambda k: (z, c, s ^ k)
    neighbours = [1, 2] if folded else list(range(1, n_seq))
    greet([peer(k) for k in neighbours] + [core_peer], [])
    mine = lambda k: 0 if k == 0 else 2 * k + 1
    cross = lambda k: 1 if k == 0 else 2 * k

    w_copy = pltpu.make_async_copy(weights, w.at[:, : 3 * units], local.at[0])
    w_copy.start()
    tile_rows = [pl.ds(h * TILE, TILE) for h in range(steps)]
    piece = lambda k, h: near[0].at[tile_rows[h]] if k == 0 else near[1 + (k - 1) * steps + h]
    n_here = [(0, h, normed.at[tile_rows[h]]) for h in range(steps)]
    d_here = [(mine(k), h, piece(k, h)) for k in range(n_seq) for h in range(steps)]

    def lies(here, gathered, index, h):
        for place, part, ref in here:
            if (place, part) == (index, h):
                return ref
        return gathered.at[index, tile_rows[h]]

    n_sems, d_sems = (n_send, n_recv), (d_send, d_recv)
    parts = [pl.ds(h * TILE, TILE) for h in range(2)] if folded else [pl.ds(0, length)]
    count = len(neighbours) * len(parts)
    n_own = remote(normed, n_all.at[1], n_sems, 0, core_peer)
    d_core = [
        [remote(piece(k, h), d_all.at[cross(k), tile_rows[h]], d_sems, k * steps + h, core_peer) for h in range(steps)]
        for k in range(n_seq)
    ]
    n_direct, n_core = [], []
    for h, part in enumerate(parts):
        slots = [1 + h * len(neighbours) + i for i in range(len(neighbours))]
        n_direct.append(
            [remote(normed.at[part], n_all.at[mine(k), part], n_sems, i, peer(k)) for i, k in zip(slots, neighbours)]
        )
        n_core.append(
            [
                remote(n_all.at[mine(k), part], n_all.at[cross(k), part], n_sems, count + i, core_peer)
                for i, k in zip(slots, neighbours)
            ]
        )
    n_own.start()
    for copies in n_direct + d_core:
        for copy in copies:
            copy.start()
    n_fold, n_last = [], []
    if folded:
        for h, part in enumerate(parts):
            source, slot = n_all.at[mine(1 + h), part], 2 * count + 1 + h
            n_fold.append(remote(source, n_all.at[mine(3), part], n_sems, slot, peer(2 - h)))
            n_last.append(remote(n_all.at[mine(3), part], n_all.at[cross(3), part], n_sems, slot + 2, core_peer))

    def tile_place(t):
        if not folded:
            return t // steps, t % steps
        turn, j = t // 4, t % 4
        middle = ((turn + 1) // 2) % 2
        ends = 1 - middle
        q = middle * (2 + j) + ends * ((turn // 3) * 6 + j % 2)
        return q, middle * (turn // 2) + ends * (j // 2)

    def d_came(k):
        for copy in d_core[k]:
            copy.wait_recv()

    def part_came(h):
        for copy in n_direct[h]:
            copy.wait_recv()
        for copy in n_core[h]:
            copy.start()
        if folded:
            n_fold[h].start()

    def tile_ready(t):
        @pl.when(t == 1 if folded else t == steps)
        def _():
            n_own.wait_recv()
            d_came(0)

        for h in range(len(parts)):
            first = 4 + 4 * h if folded else 2 * steps
            pl.when(t == first)(lambda: part_came(h))
            for i, k in enumerate(neighbours):
                when = t == (first + 2 * i if folded else cross(k) * steps)
                pl.when(when)(n_core[h][i].wait_recv)
                if h == 0:
                    pl.when(when)(lambda: d_came(k))
        if folded:

            @pl.when(t == 12)
            def _():
                for h in range(2):
                    n_fold[h].wait_recv()
                    n_last[h].start()
                for h in range(2):
                    n_last[h].wait_recv()
                d_came(3)

    def tile_copies(t, step_of):
        q, h = tile_place(t)
        rows = pl.ds(pl.multiple_of(h * TILE, TILE), TILE)
        for a, (here, gathered, tile) in enumerate(((n_here, n_all, n_tile), (d_here, d_all, d_tile))):
            copy = lambda source: pltpu.make_async_copy(source, tile.at[t % 2], tile_sem.at[a, t % 2])
            elsewhere = True
            for index, part, ref in here:
                pl.when((q == index) & (h == part))(lambda: step_of(copy(ref)))
                if part == 0:
                    elsewhere = elsewhere & (q != index)
            pl.when(elsewhere)(lambda: step_of(copy(gathered.at[q, rows])))

    def begin(copy):
        copy.start()

    def finish(copy):
        copy.wait()

    def core_copy(k, h):
        return remote(core_out.at[h], core_sum.at[k, h], (c_send.at[k], c_recv.at[k]), h, core_peer)

    def y_local(k, h):
        rows = pl.ds(pl.multiple_of(h * TILE, TILE), TILE)
        return pltpu.make_async_copy(y_out.at[h], y_own.at[k, rows], y_sem.at[h])

    def y_remote(k, h):
        rows = pl.ds(pl.multiple_of(h * TILE, TILE), TILE)
        return remote(y_out.at[h], y_core.at[k, rows], (yc_send.at[k], yc_recv.at[k]), h, core_peer)

    ends = (r_send, r_recv)

    def to_peer(k, h):
        if (folded, k) == (True, 3):
            return remote(core_sum.at[3, h], t_in.at[h], ends, h, peer(1 + h))
        slot = (2 if folded else 0) + (k - 1) * steps + h
        return remote(core_sum.at[k, h], arrived.at[k - 1, h], ends, slot, peer(k))

    late = [(2, 0), (1, 1)] if folded else []
    prompt = [(k, h) for k in range(1, n_seq) for h in range(steps)]
    for pair in late:
        prompt.remove(pair)

    tile_copies(jnp.int32(0), begin)
    w_copy.wait()

    def tile_step(t, _):
        q, h = tile_place(t)
        k, other = chunk_of(q)
        slot = t % 2
        tile_copies(t, finish)
        values = n_tile[slot]
        gate = dot(values, w[:, :units], NN)
        up = dot(values, w[:, units : 2 * units], NN)
        d_hidden = dot(d_tile[slot], w[:, 2 * units : 3 * units], NN)
        sigmoid = 1.0 / (1.0 + jnp.exp(-gate))
        silu = gate * sigmoid
        low = (silu * up).astype(bf16)
        d_gate = (d_hidden * up * sigmoid * (1.0 + gate * (1.0 - sigmoid))).astype(bf16)
        d_up = (d_hidden * silu).astype(bf16)
        rows = pl.ds(pl.multiple_of((q * steps + h) * TILE, TILE), TILE)
        hidden[rows] = low
        both[rows, :units] = d_gate
        both[rows, units:] = d_up

        @pl.when(t + 1 < chunks * steps)
        def _():
            tile_ready(t + 1)
            tile_copies(t + 1, begin)

        result = dot(low, w[:, 2 * units : 3 * units], NT).astype(bf16)
        before = q - 1
        k_before, other_before = chunk_of(jnp.maximum(before, 0))
        pl.when((before >= 0) & (other_before == 0))(lambda: y_local(k_before, h).wait())
        pl.when((before >= 0) & (other_before == 1))(lambda: y_remote(k_before, h).wait_send())
        y_out[h] = result
        pl.when(other == 0)(lambda: y_local(k, h).start())
        pl.when(other == 1)(lambda: y_remote(k, h).start())

        part = dot(d_gate, w[:, :units], NT) + dot(d_up, w[:, units : 2 * units], NT)

        @pl.when(q == 0)
        def _():
            own_back[h] = part.astype(bf16)

        @pl.when(other == 1)
        def _():
            pl.when(k > 0)(lambda: core_copy(k - 1, h).wait_send())
            core_out[h] = part.astype(bf16)
            core_copy(k, h).start()

        @pl.when((other == 0) & (k > 0))
        def _():
            core_copy(k, h).wait_recv()
            core_sum[k, h] = (part + core_sum[k, h].astype(f32)).astype(bf16)
            for key, half in prompt:
                pl.when((k == key) & (h == half))(to_peer(key, half).start)

        return 0

    lax.fori_loop(0, chunks * steps, tile_step, 0)

    blocks = chunks * length // D
    width = blocks * TILE

    def column_copies(j):
        slot = j % 2
        columns = pl.ds(pl.multiple_of(j * TILE, TILE), TILE)
        copies = []
        for a, (here, gathered) in enumerate(((n_here, n_all), (d_here, d_all))):
            for b in range(blocks):
                for q in range(D // length):
                    first = pl.multiple_of((slot * 2 + a) * width + b * TILE, TILE)
                    for h in range(steps):
                        target = w.at[pl.ds(q * length + h * TILE, TILE), pl.ds(first, TILE)]
                        source = lies(here, gathered, b * (D // length) + q, h)
                        copies.append((source.at[:, columns], target, (slot, a * blocks + b, q * steps + h)))
        return [pltpu.make_async_copy(x, y, g_sem.at[i]) for x, y, i in copies]

    def g_store(j):
        rows = pl.ds(pl.multiple_of(j * TILE, TILE), TILE)
        return pltpu.make_async_copy(g_out.at[j % 2], gradient.at[rows], local.at[j % 2])

    for copy in column_copies(0):
        copy.start()

    def column_step(j, _):
        slot = j % 2

        @pl.when(j + 1 < D // TILE)
        def _():
            for copy in column_copies(j + 1):
                copy.start()

        for copy in column_copies(j):
            copy.wait()
        pl.when(j >= 2)(lambda: g_store(j - 2).wait())
        expand = shrink = None
        for b in range(blocks):
            rows = slice(b * D, (b + 1) * D)
            at = lambda a: pl.ds(pl.multiple_of((slot * 2 + a) * width + b * TILE, TILE), TILE)
            one = dot(w[:, at(0)], both[rows], TN)
            two = dot(w[:, at(1)], hidden[rows], TN)
            expand = one if expand is None else expand + one
            shrink = two if shrink is None else shrink + two
        g_out[slot, :, : 2 * units] = expand.astype(bf16)
        g_out[slot, :, 2 * units :] = shrink.astype(bf16)
        g_store(j).start()
        if folded:

            @pl.when(j == 3)
            def _():
                for i, (key, half) in enumerate(late):
                    to_peer(3, i).wait_recv()
                    total = core_sum[key, half].astype(f32) + t_in[i].astype(f32)
                    core_sum[key, half] = total.astype(bf16)
                    to_peer(key, half).start()

        return 0

    lax.fori_loop(0, D // TILE, column_step, 0)
    for j in (D // TILE - 2, D // TILE - 1):
        g_store(j).wait()

    for h in range(steps):
        core_copy(0, h).wait_recv()
        held = own_back[h].astype(f32) + core_sum[0, h].astype(f32)
        for i, key in enumerate(neighbours):
            to_peer(key, h).wait_recv()
            incoming = pltpu.make_async_copy(arrived.at[i, h], n_tile.at[i % 2], tile_sem.at[0, i % 2])
            incoming.start()
            incoming.wait()
            held = held + n_tile[i % 2].astype(f32)
        d_tile[h % 2] = held.astype(bf16)
        out = pltpu.make_async_copy(d_tile.at[h % 2], back.at[pl.ds(h * TILE, TILE)], tile_sem.at[1, h % 2])
        out.start()
        out.wait()

    n_own.wait_send()
    for copies in n_direct + n_core + d_core + [n_fold, n_last]:
        for copy in copies:
            copy.wait_send()
    for key, half in prompt + late:
        to_peer(key, half).wait_send()
    for h in range(steps):
        core_copy(n_seq - 1, h).wait_send()
        y_local(n_seq - 1, h).wait()
        for k in range(n_seq):
            y_remote(k, h).wait_recv()


def feed_plane(n_seq, normed, upstream, weights):
    length = normed.shape[0]
    units = weights.shape[1] // 3
    steps = length // TILE
    chunks = CORES * n_seq
    tokens = chunks * length
    near = len(upstream)
    folded = (n_seq, steps) == (4, 2)
    count = 2 if folded else n_seq - 1
    copies = 13 if folded else 2 * count + 1
    w_columns = 3 * units if 3 * units > 4 * TILE * tokens // D else 4 * TILE * tokens // D
    sums = 2 + count * steps
    shape = lambda *dims: jax.ShapeDtypeStruct(dims, bf16)

    outs = pl.pallas_call(
        functools.partial(feed_plane_kernel, n_seq, near),
        in_specs=[ANY] * (near + 2),
        out_specs=[ANY] * 7,
        out_shape=[
            shape(chunks, length, D),
            shape(chunks, length, D),
            shape(n_seq, length, D),
            shape(n_seq, length, D),
            shape(length, D),
            shape(D, 3 * units),
            shape(count, steps, TILE, D),
        ],
        scratch_shapes=[
            pltpu.VMEM((D, w_columns), bf16),
            pltpu.VMEM((tokens, units), bf16),
            pltpu.VMEM((tokens, 2 * units), bf16),
            pltpu.VMEM((n_seq, steps, TILE, D), bf16),
            pltpu.VMEM((steps, TILE, D), bf16),
            pltpu.VMEM((2, TILE, D), bf16),
            pltpu.VMEM((2, TILE, D), bf16),
            pltpu.VMEM((2, TILE, D), bf16),
            pltpu.VMEM((steps, TILE, D), bf16),
            pltpu.VMEM((steps, TILE, D), bf16),
            pltpu.VMEM((2, TILE, 3 * units), bf16),
            pltpu.SemaphoreType.DMA((near + 3,)),
            pltpu.SemaphoreType.DMA((2, 2)),
            pltpu.SemaphoreType.DMA((steps,)),
            pltpu.SemaphoreType.DMA((2, 2 * tokens // D, D // TILE)),
            pltpu.SemaphoreType.DMA((copies,)),
            pltpu.SemaphoreType.DMA((copies,)),
            pltpu.SemaphoreType.DMA((copies,)),
            pltpu.SemaphoreType.DMA((copies,)),
            pltpu.SemaphoreType.DMA((n_seq, steps)),
            pltpu.SemaphoreType.DMA((n_seq, steps)),
            pltpu.SemaphoreType.DMA((n_seq, steps)),
            pltpu.SemaphoreType.DMA((n_seq, steps)),
            pltpu.SemaphoreType.DMA((sums,)),
            pltpu.SemaphoreType.DMA((sums,)),
        ],
        compiler_params=pltpu.CompilerParams(
            collective_id=2, has_side_effects=True, vmem_limit_bytes=60 << 20
        ),
        cost_estimate=pl.CostEstimate(
            flops=20 * tokens * D * units, bytes_accessed=12 * tokens * D, transcendentals=tokens * units
        ),
        name="feed_plane",
    )(*upstream, normed, weights)
    return outs[2:6]


def last_sums_kernel(n_z, n_seq, out_term, joined_term, gain_term, shares, out_sum, joined_sum, exchanged, *scratch):
    terms, core_sums, folds, sides, ups, downs = (scratch[2 * i : 2 * i + 2] for i in range(6))
    out_parts, local, a_send, a_recv, c_send, c_recv, p_send, p_recv, u_send, u_recv, v_send, v_recv = scratch[12:]
    z, c, s = coordinates()
    plane = CORES * n_seq
    me = c * n_seq + s
    others = [(z, c ^ (k // n_seq), s ^ (k % n_seq)) for k in range(1, plane)]
    core_peer, above, below = (z, 1 - c, s), (z + 1, c, s), (z - 1, c, s)
    peer = lambda k: (z, c, s ^ k)
    folded = n_seq == 4
    half = n_z // 2
    first, second = pl.ds(0, half), pl.ds(half, n_z - half)
    width = joined_term.shape[4]
    fetch = [
        pltpu.make_async_copy(joined_term, terms[0].at[:, :, :, :, pl.ds(0, width)], local.at[0]),
        pltpu.make_async_copy(gain_term, terms[0].at[:, :, :, :, pl.ds(width, PAIR)], local.at[1]),
        pltpu.make_async_copy(out_term, terms[1], local.at[2]),
    ]
    for copy in fetch:
        copy.start()
    greet(others, [(z > 0, below), (z < n_z - 1, above)])
    units = shares.shape[2] // 3
    hidden_units = exchanged.shape[1] // 3

    def piece(p, i):
        start = pl.multiple_of(i * hidden_units + me * units, units)
        return shares.at[p, :, pl.ds(i * units, units)], exchanged.at[:, pl.ds(start, units)]

    kept = [pltpu.make_async_copy(*piece(me, i), local.at[3 + i]) for i in range(3)]
    for copy in kept:
        copy.start()
    exchange = []
    for k, (tz, tc, ts) in enumerate(others):
        for i in range(3):
            a, b = piece(tc * n_seq + ts, i)
            exchange.append(remote(a, b, (a_send, a_recv), 3 * k + i, (tz, tc, ts)))

    order = list(range(n_seq - 1, -1, -1))
    to_core = lambda g, k: remote(
        terms[g].at[:, 1 - c, s ^ k], core_sums[g].at[k], (c_send.at[g], c_recv.at[g]), k, core_peer
    )

    rows = out_parts.shape[1]
    wholes = (pl.ds(0, n_z), pl.ds(0, rows))
    halves = ((first, second), (pl.ds(0, rows // 2), pl.ds(rows // 2, rows // 2)))
    held = (core_sums[0], out_parts)

    def to_side(g, k, part, slot):
        sems = (p_send.at[g], p_recv.at[g])
        return remote(held[g].at[k, part], sides[g].at[k - 1, part], sems, slot, peer(k))

    def to_fold(g, i):
        sems = (p_send.at[g], p_recv.at[g])
        return remote(held[g].at[3, halves[g][i]], folds[g].at[i], sems, 4 + i, peer(1 + i))

    def prompt_copies(g):
        if folded:
            return [to_side(g, 1, halves[g][0], 0), to_side(g, 2, halves[g][1], 1)]
        return [to_side(g, k, wholes[g], k - 1) for k in range(1, n_seq)]

    def later_copies(g):
        return [to_side(g, 2, halves[g][0], 2), to_side(g, 1, halves[g][1], 3)] if folded else []

    def add_folds(g):
        if folded:
            later = later_copies(g)
            for i in range(2):
                k, part = 2 - i, halves[g][i]
                to_fold(g, i).wait_recv()
                held[g][k, part] = plus(held[g][k, part], folds[g][i])
                later[i].start()

    def side_total(g):
        for copy in prompt_copies(g) + later_copies(g):
            copy.wait_recv()
        total = held[g][0].astype(f32)
        for k in range(sides[g].shape[0]):
            total = total + sides[g][k].astype(f32)
        return total

    def plus(one, two):
        return (one.astype(f32) + two.astype(f32)).astype(bf16)

    block = lambda g, d: core_sums[0].at[0, d] if g == 0 else core_sums[1].at[:, d]
    up_copy = lambda g, k: remote(
        block(g, (z + n_z - k) % n_z), ups[g].at[k - 1], (u_send.at[g], u_recv.at[g]), k - 1, above
    )
    down_copy = lambda g, k: remote(
        block(g, (z + k) % n_z), downs[g].at[k - 1], (v_send.at[g], v_recv.at[g]), k - 1, below
    )

    def line_step(g, k):
        if k > 1:

            @pl.when((z >= 1) & (z <= k - 1))
            def _():
                up_copy(g, k - 1).wait_recv()

            @pl.when((z >= 1) & (z <= k - 1) & (z < n_z - 1))
            def _():
                target = block(g, (z + n_z - k) % n_z)
                target[...] = plus(target[...], ups[g][k - 2])

            @pl.when((z < n_z - 1) & (z >= n_z - k))
            def _():
                down_copy(g, k - 1).wait_recv()

            @pl.when((z < n_z - 1) & (z >= n_z - k) & (z > 0))
            def _():
                target = block(g, (z + k) % n_z)
                target[...] = plus(target[...], downs[g][k - 2])

        pl.when((z <= k - 1) & (z < n_z - 1))(lambda: up_copy(g, k).start())
        pl.when((z >= n_z - k) & (z > 0))(lambda: down_copy(g, k).start())

    def line_total(g, target):
        own = block(g, z)
        target[...] = own[...].astype(target.dtype)
        if n_z > 1:

            @pl.when(z >= 1)
            def _():
                up_copy(g, n_z - 1).wait_recv()
                target[...] = (target[...].astype(f32) + ups[g][n_z - 2].astype(f32)).astype(target.dtype)

            @pl.when(z < n_z - 1)
            def _():
                down_copy(g, n_z - 1).wait_recv()
                target[...] = (target[...].astype(f32) + downs[g][n_z - 2].astype(f32)).astype(target.dtype)

    for g in (1, 0):
        for copy in fetch[2 * g : 2 + g]:
            copy.wait()
        for k in order:
            to_core(g, k).start()
    for copy in exchange[: len(exchange) // 2]:
        copy.start()
    for k in order:
        to_core(1, k).wait_recv()
        core_sums[1][k] = plus(terms[1][:, c, s ^ k], core_sums[1][k])
    if n_z > 1:
        line_step(1, 1)
    prompt = prompt_copies(0)
    for k in order:
        to_core(0, k).wait_recv()
        core_sums[0][k] = plus(terms[0][:, c, s ^ k], core_sums[0][k])
        if (folded, k) == (True, 3):
            to_fold(0, 0).start()
            to_fold(0, 1).start()
        elif k:
            prompt[k - 1].start()
    if n_z > 2:
        line_step(1, 2)
    add_folds(0)
    for copy in exchange[len(exchange) // 2 :]:
        copy.start()
    for k in range(3, n_z):
        line_step(1, k)
    core_sums[0][0] = side_total(0).astype(bf16)
    if n_z > 1:
        line_step(0, 1)
    line_total(1, out_parts)
    if folded:
        to_fold(1, 0).start()
        to_fold(1, 1).start()
    for copy in prompt_copies(1):
        copy.start()
    if n_z > 2:
        line_step(0, 2)
    add_folds(1)
    for k in range(3, n_z):
        line_step(0, k)
    out_sum[...] = side_total(1)
    line_total(0, joined_sum)

    for g in range(2):
        for k in order:
            to_core(g, k).wait_send()
        for copy in prompt_copies(g) + later_copies(g):
            copy.wait_send()
        if folded:
            to_fold(g, 0).wait_send()
            to_fold(g, 1).wait_send()
        for k in range(1, n_z):
            pl.when((z <= k - 1) & (z < n_z - 1))(lambda: up_copy(g, k).wait_send())
            pl.when((z >= n_z - k) & (z > 0))(lambda: down_copy(g, k).wait_send())
    for copy in exchange:
        copy.wait()
    for copy in kept:
        copy.wait()


def last_sums(n_z, n_seq, out_term, joined_term, gain_term, shares):
    rows = out_term.shape[3]
    widths = (joined_term.shape[4] + PAIR, out_term.shape[4])
    half = n_z - n_z // 2
    sides = 2 if n_seq == 4 else n_seq - 1
    line = n_z - 1 if n_z > 1 else 1
    buffers = lambda *lead: [pltpu.VMEM((*lead, rows, w), bf16) for w in widths]
    line_buffers = [pltpu.VMEM((line, rows, widths[0]), bf16), pltpu.VMEM((line, n_seq, rows, widths[1]), bf16)]
    sems = lambda *dims: [pltpu.SemaphoreType.DMA(dims), pltpu.SemaphoreType.DMA(dims)]
    return pl.pallas_call(
        functools.partial(last_sums_kernel, n_z, n_seq),
        in_specs=[ANY, ANY, ANY, VMEM],
        out_specs=[VMEM, VMEM, ANY],
        out_shape=[
            jax.ShapeDtypeStruct((rows, widths[1]), f32),
            jax.ShapeDtypeStruct((rows, widths[0]), f32),
            jax.ShapeDtypeStruct((rows, shares.shape[0] * shares.shape[2]), bf16),
        ],
        scratch_shapes=[
            *buffers(n_z, CORES, n_seq),
            *buffers(n_seq, n_z),
            pltpu.VMEM((2, half, rows, widths[0]), bf16),
            pltpu.VMEM((2, rows // 2, widths[1]), bf16),
            pltpu.VMEM((sides, n_z, rows, widths[0]), bf16),
            pltpu.VMEM((sides, rows, widths[1]), bf16),
            *line_buffers,
            *line_buffers,
            pltpu.VMEM((n_seq, rows, widths[1]), bf16),
            pltpu.SemaphoreType.DMA((6,)),
            *sems(3 * (CORES * n_seq - 1)),
            *sems(2, n_seq),
            *sems(2, n_seq + 2),
            *sems(2, line),
            *sems(2, line),
        ],
        compiler_params=pltpu.CompilerParams(collective_id=3, has_side_effects=True, vmem_limit_bytes=56 << 20),
        cost_estimate=pl.CostEstimate(flops=1 << 24, bytes_accessed=1 << 26, transcendentals=0),
        name="last_sums",
    )(out_term, joined_term, gain_term, shares)


def kv_routes(n_seq):
    if n_seq == 4:
        return [(1, 0), (1, 1), (2, 0), (2, 1)], [(2, 1, 0), (1, 2, 1)]
    return [(k, i) for k in range(1, n_seq) for i in range(2)], []


def half_rows(half, s, i):
    return pl.ds(pl.multiple_of((2 * s + i) * half, half), half)


def kv_gather_kernel(n_seq, own, kv, local, send, receive):
    z, c, s = coordinates()
    half = own.shape[0] // 2
    prompt, handed = kv_routes(n_seq)
    peer = lambda k: (z, c, s ^ k)
    greet([peer(k) for k in sorted({r[0] for r in prompt})], [])
    rows = lambda k, i: kv.at[half_rows(half, s ^ k, i)]
    mine = lambda i: own.at[pl.ds(i * half, half)]
    sems = (send, receive)
    copies = [remote(mine(i), rows(0, i), sems, slot, peer(k)) for slot, (k, i) in enumerate(prompt)]
    later = [
        remote(rows(k, i), rows(k, i), sems, len(prompt) + slot, peer(to)) for slot, (to, k, i) in enumerate(handed)
    ]
    for copy in copies:
        copy.start()
    kept = [pltpu.make_async_copy(mine(i), rows(0, i), local.at[i]) for i in range(2)]
    for copy in kept:
        copy.start()
    for copy in copies:
        copy.wait_recv()
    for copy in later:
        copy.start()
    for copy in copies:
        copy.wait_send()
    for copy in later + kept:
        copy.wait()


def kv_gather(n_seq, own):
    prompt, handed = kv_routes(n_seq)
    count = len(prompt) + len(handed)
    return pl.pallas_call(
        functools.partial(kv_gather_kernel, n_seq),
        in_specs=[VMEM],
        out_specs=ANY,
        out_shape=jax.ShapeDtypeStruct((n_seq * own.shape[0], own.shape[1]), bf16),
        scratch_shapes=[
            pltpu.SemaphoreType.DMA((2,)),
            pltpu.SemaphoreType.DMA((count,)),
            pltpu.SemaphoreType.DMA((count,)),
        ],
        compiler_params=pltpu.CompilerParams(collective_id=4, has_side_effects=True),
        name="kv_gather",
    )(own)


def sum_kv_kernel(n_seq, parts, out, folds, sides, send, receive):
    z, c, s = coordinates()
    half = out.shape[0] // 2
    peer = lambda k: (z, c, s ^ k)
    part = lambda k, i: parts.at[half_rows(half, s ^ k, i)]
    sems = (send, receive)
    to_side = lambda source, k, i: remote(source, sides.at[k - 1, i], sems, 2 * (k - 1) + i, peer(k))
    greet([peer(k) for k in ((1, 2) if n_seq == 4 else range(1, n_seq))], [])
    if n_seq == 4:
        fold = [remote(part(3, i), folds.at[i], sems, 4 + i, peer(1 + i)) for i in range(2)]
        prompt = [to_side(part(1, 0), 1, 0), to_side(part(2, 1), 2, 1)]
        later = [to_side(folds.at[0], 2, 0), to_side(folds.at[1], 1, 1)]
        for copy in fold + prompt:
            copy.start()
        for i in range(2):
            fold[i].wait_recv()
            total = folds[i].astype(f32) + part(2 - i, i)[...].astype(f32)
            folds[i] = total.astype(bf16)
            later[i].start()
        copies = prompt + later
        for copy in fold:
            copy.wait_send()
    else:
        copies = [to_side(part(k, i), k, i) for k in range(1, n_seq) for i in range(2)]
        for copy in copies:
            copy.start()
    for copy in copies:
        copy.wait()
    for i in range(2):
        total = part(0, i)[...].astype(f32)
        for k in range(sides.shape[0]):
            total = total + sides[k, i].astype(f32)
        out[pl.ds(i * half, half)] = total


def sum_kv(n_seq, parts):
    length, width = parts.shape[0] // n_seq, parts.shape[1]
    sides = 2 if n_seq == 4 else n_seq - 1
    return pl.pallas_call(
        functools.partial(sum_kv_kernel, n_seq),
        in_specs=[VMEM],
        out_specs=VMEM,
        out_shape=jax.ShapeDtypeStruct((length, width), f32),
        scratch_shapes=[
            pltpu.VMEM((2, length // 2, width), bf16),
            pltpu.VMEM((sides, 2, length // 2, width), bf16),
            pltpu.SemaphoreType.DMA((2 * sides + 2,)),
            pltpu.SemaphoreType.DMA((2 * sides + 2,)),
        ],
        compiler_params=pltpu.CompilerParams(collective_id=5, has_side_effects=True, vmem_limit_bytes=32 << 20),
        name="sum_kv",
    )(parts)


class Links:
    def __init__(self, n_dp, n_seq):
        self.n_z = n_dp // CORES
        self.n_seq = n_seq
        self.plane = CORES * n_seq

    def place(self):
        return coordinates()

    def send(self, values, pairs_of):
        pairs = []
        for z in range(self.n_z):
            for c in range(CORES):
                for s in range(self.n_seq):
                    to = pairs_of(z, c, s)
                    if to is not None:
                        tz, tc, ts = to
                        pairs.append((((z * CORES + c) * self.n_seq + s), (tz * CORES + tc) * self.n_seq + ts))
        return lax.ppermute(values, AXES, pairs)

    def core(self, values):
        return self.send(values, lambda z, c, s: (z, 1 - c, s))

    def peer(self, values, k):
        return self.send(values, lambda z, c, s: (z, c, s ^ k))

    def up(self, values, first, last):
        return self.send(values, lambda z, c, s: (z + 1, c, s) if first <= z <= last else None)

    def down(self, values, first, last):
        return self.send(values, lambda z, c, s: (z - 1, c, s) if first <= z <= last else None)


def body(
    n_dp,
    n_seq,
    tokens,
    joined_weight,
    output_weight,
    expand_weight,
    shrink_weight,
    norm_gains,
    doc_lengths,
    cotangent,
):
    links = Links(n_dp, n_seq)
    n_z, plane = links.n_z, links.plane
    z, core, seq = links.place()
    me = core * n_seq + seq
    devices = n_dp * n_seq
    local_len = tokens.shape[1]
    rows = D // devices
    units = FF // plane
    own_gains = GAINS // devices

    kv_columns = joined_weight[:, Q_WIDTH:].reshape(rows, 2, KV_HEADS, HEAD_DIM).transpose(0, 2, 1, 3)
    gain_block = jnp.pad(norm_gains, (0, rows * PAIR - own_gains)).reshape(rows, PAIR)
    joined_block = jnp.concatenate(
        [joined_weight[:, :Q_WIDTH], kv_columns.reshape(rows, 2 * KV_WIDTH), gain_block], axis=1
    )
    block, joined_z, output_z = first_gather(
        n_z, n_seq, expand_weight, shrink_weight.T, joined_block, output_weight.T
    )
    lines = [[a * CORES + c for a in range(n_z)] for c in range(CORES)]
    weights = lax.all_gather(
        block.reshape(plane * rows, 3 * units), "dp", axis=0, tiled=True, axis_index_groups=lines
    )
    joined_all, output_all = spread_plane(n_z, n_seq, joined_z, output_z)
    cot = cotangent.reshape(local_len, D)
    top, bottom = cot[:TILE], cot[TILE:]
    early_top, early_bottom, joined_all = lax.optimization_barrier((top, bottom, joined_all))
    joined_all = joined_all.reshape(D, QKV + PAIR)
    output_all = output_all.reshape(D, Q_WIDTH)
    gains = joined_all[:, QKV:].reshape(devices, rows * PAIR)[:, :own_gains].reshape(GAINS).astype(f32)
    joined_all = joined_all[:, :QKV]
    gain_one = gains[:D]
    gain_query = gains[D : D + HEAD_DIM]
    gain_key = gains[D + HEAD_DIM : D + PAIR]
    gain_two = gains[D + PAIR :]
    head_gains = jnp.stack([jnp.tile(gain_query, 2), jnp.tile(gain_key, 2)])

    half = HEAD_DIM // 2
    frequency = 10000.0 ** (-jnp.arange(half, dtype=f32) / half)
    offset = seq * local_len
    positions = offset + jnp.arange(local_len, dtype=jnp.int32)
    angles = positions.astype(f32)[:, None] * frequency[None, :]
    cosine, sine = jnp.cos(angles), jnp.sin(angles)
    tables = jnp.stack(
        [jnp.concatenate([cosine] * 4, axis=1), jnp.concatenate([-sine, sine, -sine, sine], axis=1)]
    )
    places = jnp.arange(ROW_LEN, dtype=jnp.int32)
    docs = jnp.zeros((ROW_LEN,), jnp.int32)
    bound = 0
    for index in range(doc_lengths.shape[1] - 1):
        bound = bound + doc_lengths[0, index]
        docs = docs + (places >= bound).astype(jnp.int32)
    mark = jnp.arange(PAIR, dtype=jnp.int32)[None] - HEAD_DIM
    same = (mark >= 0) & (mark < MARK) & (mark == docs[:, None])
    other = (mark >= 0) & (mark < MARK) & (mark != docs[:, None])
    carries = (mark >= MARK) & (mark < MARK + 3)
    key_marks = jnp.where(other, -1024.0, jnp.where(carries, 1.0, 0.0)).astype(bf16)
    query_marks = lax.dynamic_slice_in_dim(same.astype(bf16), offset, local_len, 0)
    starts = jnp.reshape(offset, (1,)).astype(jnp.int32)

    flat = tokens.reshape(local_len, D).astype(f32)
    scale_one = rms_scale(flat)
    normed_low = (flat * scale_one * gain_one).astype(bf16)
    projected = dot(normed_low, joined_all, NN)
    turned = rope(projected, head_gains, tables)
    kv = kv_gather(n_seq, turned[:, Q_WIDTH:])
    upstream_low = cotangent.reshape(local_len, D)
    upstream_near = [upstream_low]
    if (n_seq, local_len) == (4, 2 * TILE):
        late_top, late_bottom, kv = lax.optimization_barrier((top, bottom, kv))
        one, two = links.peer(early_top, 1), links.peer(early_bottom, 2)
        one_late, two_late = links.peer(late_bottom, 1), links.peer(late_top, 2)
        kv, one, two = lax.optimization_barrier((kv, one, two))
        upstream_near += [one, one_late, two_late, two, links.peer(one, 2), links.peer(two, 1)]
    else:
        upstream_near += [links.peer(upstream_low, k) for k in range(1, n_seq)]
    attended, q_marked = attend(starts, turned, kv, key_marks, query_marks)
    attended_low = attended.astype(bf16)
    residual = flat + dot(attended_low, output_all, NT)
    scale_two = rms_scale(residual)
    normed_two = (residual * scale_two * gain_two).astype(bf16)

    y_own, y_core, back, share_gradient = feed_plane(n_seq, normed_two, upstream_near, weights)
    grad_normed_two = back.astype(f32)
    mine = lax.psum_scatter(
        share_gradient, "dp", scatter_dimension=0, tiled=True, axis_index_groups=lines
    )
    upstream = upstream_low.astype(f32)
    gain_two_grad = jnp.sum(grad_normed_two * residual * scale_two, axis=0)
    grad_residual = upstream + norm_back(grad_normed_two, residual, scale_two, gain_two)
    grad_attn_low = grad_residual.astype(bf16)
    output_term = dot(grad_attn_low, attended_low, TN).astype(bf16)
    grad_out_low = dot(grad_attn_low, output_all, NN).astype(bf16)
    feed_parts = (y_own.astype(f32) + y_core.astype(f32)).astype(bf16)
    grad_query, grad_kv_all, feed_sides = attend_back(
        n_seq, q_marked, grad_out_low, attended, kv, key_marks, feed_parts
    )
    feed_result = feed_parts[0].astype(f32) + jnp.sum(feed_sides.astype(f32), axis=0).reshape(local_len, D)
    layer_output = (residual + feed_result).astype(bf16)
    grad_kv = sum_kv(n_seq, grad_kv_all)
    grad_projected, head_gain_sums = rope_back(grad_query, grad_kv, projected, head_gains, tables)
    joined_term = dot(normed_low, grad_projected, TN).astype(bf16)
    grad_normed = dot(grad_projected, joined_all, NT)
    gain_one_grad = jnp.sum(grad_normed * flat * scale_one, axis=0)
    token_gradient = grad_residual + norm_back(grad_normed, flat, scale_one, gain_one)
    gain_query_grad = head_gain_sums[0, :HEAD_DIM] + head_gain_sums[0, HEAD_DIM:]
    gain_key_grad = head_gain_sums[1, :HEAD_DIM]
    gain_grads = jnp.concatenate([gain_one_grad, gain_query_grad, gain_key_grad, gain_two_grad])
    gain_block = jnp.pad(gain_grads.reshape(devices, own_gains), ((0, 0), (0, rows * PAIR - own_gains)))
    by_owner = lambda a: a.astype(bf16).reshape(n_z, CORES, n_seq, rows, -1)
    output_sum, joined_sum, exchanged = last_sums(
        n_z,
        n_seq,
        by_owner(output_term),
        by_owner(joined_term),
        by_owner(gain_block.reshape(D, PAIR)),
        mine.reshape(plane, rows, 3 * units),
    )
    output_gradient = output_sum.T
    expand_gradient = exchanged[:, : 2 * FF].astype(f32)
    shrink_gradient = exchanged[:, 2 * FF :].T.astype(f32)
    kv_sum = joined_sum[:, Q_WIDTH:QKV].reshape(rows, KV_HEADS, 2, HEAD_DIM).transpose(0, 2, 1, 3)
    joined_gradient = jnp.concatenate([joined_sum[:, :Q_WIDTH], kv_sum.reshape(rows, 2 * KV_WIDTH)], axis=1)
    gains_gradient = joined_sum[:, QKV:].reshape(rows * PAIR)[:own_gains]
    return (
        layer_output.reshape(1, local_len, D),
        token_gradient.astype(bf16).reshape(1, local_len, D),
        joined_gradient,
        output_gradient,
        expand_gradient,
        shrink_gradient,
        gains_gradient,
    )


def solution(mesh):
    token_spec, row_spec, column_spec = P("dp", "seq", None), P(AXES, None), P(None, AXES)
    return jax.shard_map(
        functools.partial(body, mesh.shape["dp"], mesh.shape["seq"]),
        mesh=mesh,
        in_specs=(
            token_spec,
            row_spec,
            column_spec,
            row_spec,
            column_spec,
            P(AXES),
            P("dp", None),
            token_spec,
        ),
        out_specs=(token_spec, token_spec, row_spec, column_spec, row_spec, column_spec, P(AXES)),
        check_vma=False,
    )
```
